32 devices in a mesh: groups: 2 (over y), row: 8 (over z, x), col: 2 (over core).
Axes of the slice: x: 2, y: 2, z: 4, core: 2. Of those that a mesh axis runs over, the one named last changes fastest.
Arguments:
- wavenumber: float32 [2], P('groups'), parts along dimension 0, may hold values from 30 to 90
- tgt_geom: float32 [6, 4096], P(None, ('groups', 'row')), parts along dimension 1, may hold values from -2 to 8, as said below
- src_geom: float32 [4, 512], P(None, ('groups', 'row', 'col')), parts along dimension 1, may hold values from -2 to 8, as said below
- excite: bfloat16 [128, 512], P(None, ('groups', 'row', 'col')), parts along dimension 1, may hold values from -6 to 6
- tgt_nodes: float32 [3, 6144], P(None, ('groups', 'row')), parts along dimension 1, may hold values from -2 to 8, as said below
- src_nodes: float32 [3, 3072], P(None, ('groups', 'row')), parts along dimension 1, may hold values from -2 to 8, as said below
- tgt_weights: bfloat16 [2, 192, 4096], P(None, None, ('groups', 'row')), parts along dimension 2, may hold values from -0.109375 to 0.109375
- src_weights: bfloat16 [2, 192, 512], P(None, None, ('groups', 'row', 'col')), parts along dimension 2, may hold values from -1 to 1
- near_order: int32 [32, 9], P(('groups', 'row')), parts along dimension 0, may hold values from 0 to 3
Outputs:
- responses: float32 [4096, 128], P(('groups', 'row', 'col')), parts along dimension 0
The draws below stay inside these ranges and needn't reach their ends.
There are 2 independent parts, one for each index of `groups`. The reference program is written for one: setup_inputs(seed, part) draws one part's arguments, and reference() takes and returns one part's arrays. A program takes and returns all parts, laid end to end along the dimension named above; each array names one. Nothing has to cross between parts.
Inputs may be any that keep to these rules, and one draw needn't show every extreme that they name: `tgt_geom`: rows 0 to 2 are points, rows 3 to 5 unit normals. `src_geom`: rows 0 to 2 are points, row 3 positive areas. `tgt_nodes`: Points. `src_nodes`: Points. `near_order`: 0 marks a pair that is not near.
All inputs are finite; a program needn't handle non-finite values.
Results may differ from the reference program's by a relative error of at most 0.0011.
Values may be sent and summed in bfloat16 or wider, within the bound.
No kernel may reach another device: no remote copies, remote signals or barrier semaphores. Data moves between devices by JAX's collectives and lax.ppermute only.
A program may use at most 64 MiB of HBM per device.

```python
import jax
import jax.numpy as jnp
from jax import lax

BLK = 128
RBD = 2
CPD = 16
NEXC = 64
QSTEP = 64
ORDERS = 3
NEARW = 4
QN = 192
NBAND = 9
NROWS = 2048
NCOL = 256
N_ROW = 8


ACROSS = 2.0


def line_positions(key, count, per_unit):
    first, second = jax.random.split(key)
    along = (jnp.arange(count, dtype=jnp.float32) + jax.random.uniform(first, (count,), jnp.float32)) / per_unit
    across = jax.random.uniform(second, (2, count), jnp.float32, -ACROSS, ACROSS)
    return jnp.concatenate([along[None, :], across], 0)


def draw_tgt_geom(key, part):
    place_key, normal_key = jax.random.split(jax.random.fold_in(key, 11))
    points = line_positions(place_key, NROWS, BLK * RBD)
    raw = jax.random.normal(normal_key, (3, NROWS), jnp.float32)
    length = jnp.sqrt(jnp.sum(raw * raw, 0, keepdims=True))
    return jnp.concatenate([points, raw / jnp.maximum(length, 0.001)], 0)


def draw_src_geom(key, part):
    place_key, area_key = jax.random.split(jax.random.fold_in(key, 23))
    points = line_positions(place_key, NCOL, NCOL * BLK * RBD // NROWS)
    areas = jnp.exp(jax.random.uniform(area_key, (1, NCOL), jnp.float32, jnp.log(0.1), jnp.log(0.4)))
    return jnp.concatenate([points, areas], 0)


def draw_tgt_nodes(key, part):
    return line_positions(jax.random.fold_in(key, 37), QN * NROWS // BLK, QN * RBD)


def draw_src_nodes(key, part):
    return line_positions(jax.random.fold_in(key, 41), QN * NROWS // (BLK * RBD), QN)


def plant(values, key, smallest, largest):
    extent = values.shape
    index_at = [jax.random.randint(jax.random.fold_in(key, axis), (), 0, extent[axis]) for axis in range(len(extent))]
    values = values.at[tuple(index_at)].set(smallest)
    longest = extent.index(max(extent))
    index_at[longest] = (index_at[longest] + 1) % extent[longest]
    return values.at[tuple(index_at)].set(largest)


def levels(rng, shape, shards, low, largest):
    loudness, own = 1.0, jax.random.fold_in(rng, 6)
    for position, shards_of in shards:
        steps = jnp.exp(jax.random.uniform(jax.random.fold_in(own, position), (shards_of,), jnp.float32, low / len(shards), largest / len(shards)))
        loudness = loudness * jnp.repeat(steps, shape[position] // shards_of).reshape([-1 if axis == position else 1 for axis in range(len(shape))])
    return loudness


def noise(rng, extent, deviation, most, pieces=(), kind=jnp.bfloat16):
    array = deviation * jax.random.normal(rng, extent, jnp.float32)
    if pieces:
        array = array * levels(rng, extent, pieces, -0.22, 0.18)
    return jnp.clip(array, -most, most).astype(kind)


def setup_inputs(seed: int = 0, part: int = 0) -> dict:
    seeds = jax.random.split(jax.random.key(seed), 10)
    part_splits = jax.random.split(jax.random.fold_in(seeds[9], part), 10)
    return {
        "wavenumber": jnp.clip(jax.random.uniform(part_splits[0], (1,), jnp.float32, 30.0, 90.0), 30.0, 90.0),
        "tgt_geom": draw_tgt_geom(jax.random.fold_in(jax.random.fold_in(seeds[9], part), 71), part),
        "src_geom": draw_src_geom(jax.random.fold_in(jax.random.fold_in(seeds[9], part), 71), part),
        "excite": noise(part_splits[3], (2 * NEXC, NCOL), 1.0, 6.0, ((1, 16),)),
        "tgt_nodes": draw_tgt_nodes(jax.random.fold_in(jax.random.fold_in(seeds[9], part), 71), part),
        "src_nodes": draw_src_nodes(jax.random.fold_in(jax.random.fold_in(seeds[9], part), 71), part),
        "tgt_weights": noise(part_splits[6], (2, QN, NROWS), (16 * QN) ** -0.5, 0.109375, ((2, 8),)),
        "src_weights": noise(part_splits[7], (2, QN, NCOL), (2 * CPD) ** -0.5, 1.0, ((2, 16),)),
        "near_order": plant(jax.random.randint(part_splits[8], (N_ROW * RBD, NBAND), 0, ORDERS + 1), jax.random.fold_in(part_splits[8], 1), 0, ORDERS).astype(jnp.int32),
    }


SOFT = 0.05
FOUR_PI = 4.0 * 3.141592653589793
HIGH = lax.Precision.HIGHEST

def far_block(targets, sources, excite_cols, wave_number):
    delta_x = targets[0][:, None] - sources[0][None, :]
    delta_y = targets[1][:, None] - sources[1][None, :]
    delta_z = targets[2][:, None] - sources[2][None, :]
    radius = jnp.sqrt(delta_x * delta_x + delta_y * delta_y + delta_z * delta_z + SOFT * SOFT)
    cosine = (targets[3][:, None] * delta_x + targets[4][:, None] * delta_y + targets[5][:, None] * delta_z) / radius
    scale = sources[3][None, :] / (FOUR_PI * radius)
    phase = wave_number * radius
    green_re = scale * jnp.cos(phase)
    green_im = scale * jnp.sin(phase)
    factor_re = 1.0 - cosine
    factor_im = -cosine / phase
    kern_re = (green_re * factor_re - green_im * factor_im).astype(jnp.bfloat16)
    kern_im = (green_re * factor_im + green_im * factor_re).astype(jnp.bfloat16)
    dims = (((1,), (1,)), ((), ()))
    first = lax.dot_general(kern_re, excite_cols, dims, preferred_element_type=jnp.float32)
    second = lax.dot_general(kern_im, excite_cols, dims, preferred_element_type=jnp.float32)
    half = excite_cols.shape[0] // 2
    return jnp.concatenate([first[:, :half] - second[:, half:], first[:, half:] + second[:, :half]], 1)

def near_term(tnodes, snodes, moments, unodes, order_val, wave_number):
    delta_x = tnodes[0][:, None] - snodes[0][None, :]
    delta_y = tnodes[1][:, None] - snodes[1][None, :]
    delta_z = tnodes[2][:, None] - snodes[2][None, :]
    radius = jnp.sqrt(delta_x * delta_x + delta_y * delta_y + delta_z * delta_z + SOFT * SOFT)
    scale = 1.0 / (FOUR_PI * radius)
    node_live = (jnp.arange(QN, dtype=jnp.int32) < order_val * QSTEP).astype(jnp.float32)
    node_mask = node_live[:, None] * node_live[None, :]
    green_re = scale * jnp.cos(wave_number * radius) * node_mask
    green_im = scale * jnp.sin(wave_number * radius) * node_mask
    half = moments.shape[1] // 2
    mom_re = moments[:, :half]
    mom_im = moments[:, half:]
    inner_re = jnp.dot(green_re, mom_re, precision=HIGH) - jnp.dot(green_im, mom_im, precision=HIGH)
    inner_im = jnp.dot(green_re, mom_im, precision=HIGH) + jnp.dot(green_im, mom_re, precision=HIGH)
    test_re = unodes[0].astype(jnp.float32)
    test_im = unodes[1].astype(jnp.float32)
    dims = (((0,), (0,)), ((), ()))
    out_re = lax.dot_general(test_re, inner_re, dims, precision=HIGH) - lax.dot_general(test_im, inner_im, dims, precision=HIGH)
    out_im = lax.dot_general(test_re, inner_im, dims, precision=HIGH) + lax.dot_general(test_im, inner_re, dims, precision=HIGH)
    return jnp.concatenate([out_re, out_im], 1)

def reference(wavenumber, tgt_geom, src_geom, excite, tgt_nodes, src_nodes, tgt_weights, src_weights, near_order):
    wave_number = wavenumber[0]
    row_blocks = NROWS // BLK
    col_blocks = row_blocks // RBD
    cols_block = NCOL // col_blocks
    half = excite.shape[0] // 2

    def moment(index):
        start = (index * cols_block).astype(jnp.int32)
        weights = lax.dynamic_slice_in_dim(src_weights, start, cols_block, 2)
        cols = lax.dynamic_slice_in_dim(excite, start, cols_block, 1)
        dims = (((1,), (1,)), ((), ()))
        first = lax.dot_general(weights[0], cols, dims, preferred_element_type=jnp.float32)
        second = lax.dot_general(weights[1], cols, dims, preferred_element_type=jnp.float32)
        return jnp.concatenate([first[:, :half] - second[:, half:], first[:, half:] + second[:, :half]], 1)
    moments = lax.map(moment, jnp.arange(col_blocks, dtype=jnp.int32))

    def row_block(index):
        targets = lax.dynamic_slice_in_dim(tgt_geom, (index * BLK).astype(jnp.int32), BLK, 1)
        total = far_block(targets, src_geom, excite, wave_number)
        tnodes = lax.dynamic_slice_in_dim(tgt_nodes, (index * QN).astype(jnp.int32), QN, 1)
        unodes = lax.dynamic_slice_in_dim(tgt_weights, (index * BLK).astype(jnp.int32), BLK, 2)
        home = index // RBD
        for offset in range(NBAND):
            other = home + offset - NEARW
            valid = jnp.logical_and(other >= 0, other < col_blocks).astype(jnp.float32)
            clipped = jnp.clip(other, 0, col_blocks - 1).astype(jnp.int32)
            snodes = lax.dynamic_slice_in_dim(src_nodes, clipped * QN, QN, 1) * valid
            there = moments[clipped] * valid
            total = total + near_term(tnodes, snodes, there, unodes, near_order[index, offset], wave_number)
        return total
    result = lax.map(row_block, jnp.arange(row_blocks, dtype=jnp.int32))
    return result.reshape(NROWS, 2 * NEXC)
```

```python
import functools
import math

import jax
import jax.numpy as jnp
from jax import lax
from jax.experimental import pallas as pl
from jax.experimental.pallas import tpu as pltpu
from jax.sharding import PartitionSpec as P

QSTEP = 64
ORDERS = 3
QN = 192
LANES = 128
PARTS = 3
SOFT = 0.05
FOUR_PI = 4.0 * math.pi
INV_TURN = 1.0 / (2.0 * math.pi)
TURN_HIGH = 6.28125
TURN_LOW = 2.0 * math.pi - TURN_HIGH
ROUNDER = 1.5 * 2.0**23
SIN_HALF = (3.14159264, -5.16771009, 2.55007766, -0.59829216, 0.07765941)
COS_HALF = (1.0, -4.93480214, 4.05870916, -1.33521206, 0.23493756, -0.02439672)
BF16 = jnp.bfloat16
F32 = jnp.float32
NN = (((1,), (0,)), ((), ()))
NT = (((1,), (1,)), ((), ()))


def dot(left, right, dims=NN):
    return lax.dot_general(left, right, dims, preferred_element_type=F32)


def polynomial(z, coefficients):
    total = coefficients[-1]
    for c in coefficients[-2::-1]:
        total = total * z + c
    return total


def sincos_turns(f):
    z = f * f
    s = f * polynomial(z, SIN_HALF)
    c = polynomial(z, COS_HALF)
    twice = s + s
    return twice * c, 1.0 - twice * s


def three_parts(x):
    first = x.astype(BF16)
    rest = x - first.astype(F32)
    second = rest.astype(BF16)
    third = (rest - second.astype(F32)).astype(BF16)
    return first, second, third


def two_parts(x):
    first = x.astype(BF16)
    return first, (x - first.astype(F32)).astype(BF16)


def exchange_steps(count):
    bits = [1 << b for b in range(count.bit_length() - 2, 0, -1)]
    swapped = bits[:-2] + bits[-2:][::-1] if len(bits) >= 2 else bits
    return [b | 1 for b in bits], [b | 1 for b in swapped]


def relative_places(steps):
    places = [0]
    for step in steps:
        places = places + [p ^ step for p in places]
    return places


def pack_kernel(geom_ref, excite_ref, nodes_ref, weights_ref, out_ref):
    cpd = geom_ref.shape[1]
    exc = excite_ref.shape[0]
    half = QN // 2
    col = lax.axis_index("col")
    eye = (
        lax.broadcasted_iota(jnp.int32, (cpd, cpd), 0)
        == lax.broadcasted_iota(jnp.int32, (cpd, cpd), 1)
    )
    eye16 = eye.astype(BF16)
    for part in range(2):
        out_ref[:, part * QN : (part + 1) * QN] = dot(eye16, weights_ref[part], NT).astype(BF16)
    out_ref[:, 2 * QN : 2 * QN + exc] = dot(eye16, excite_ref[...], NT).astype(BF16)
    nodes = jnp.where(col == 0, nodes_ref[:, :half], nodes_ref[:, half:])
    parts = [p.astype(F32) for p in three_parts(nodes)]
    filler = jnp.zeros((cpd - 3 * PARTS, half), F32)
    left = jnp.concatenate(parts + [filler], 0)
    geom = jnp.concatenate([p.astype(F32) for p in three_parts(geom_ref[...])], 0)
    right = dot(eye16, geom.astype(BF16), NT)
    rest = jnp.zeros((cpd, LANES - half - right.shape[1]), F32)
    out_ref[:, 2 * QN + exc :] = jnp.concatenate([left, right, rest], 1).astype(BF16)


def field_kernel(
    rows, places, wave_ref, order_ref, data_ref, tgeom_ref, tnodes_ref, ut_ref, out_ref,
    gre_hi, gre_lo, gim_hi, gim_lo, hre, him,
):
    cpd = 16
    exc = out_ref.shape[1]
    nrow = rows
    reach = (order_ref.shape[1] - 1) // 2
    half = QN // 2
    tail = 2 * QN + exc
    row = lax.axis_index("row")
    col = lax.axis_index("col")
    wave = wave_ref[0]
    me = row * 2 + col
    parity = lax.rem(
        sum(lax.rem(lax.div(me, 1 << b), 2) for b in range((2 * nrow).bit_length() - 1)), 2
    )
    even, odd = places

    def start(relative):
        a, b = even.index(relative), odd.index(relative)
        return pl.multiple_of(jnp.where(parity == 0, a * cpd, b * cpd), cpd)

    turns = wave * INV_TURN
    tx = jnp.broadcast_to(tnodes_ref[:, 0:1], (QN, 2 * LANES))
    ty = jnp.broadcast_to(tnodes_ref[:, 1:2], (QN, 2 * LANES))
    tz = jnp.broadcast_to(tnodes_ref[:, 2:3], (QN, 2 * LANES))
    p_at = lax.broadcasted_iota(jnp.int32, (QN, 2 * LANES), 0)
    q_at = lax.broadcasted_iota(jnp.int32, (QN, 2 * LANES), 1)
    for u in range(nrow):
        offset = (row ^ u) - row + reach
        inside = jnp.logical_and(offset >= 0, offset <= 2 * reach)
        order = jnp.where(inside, order_ref[col, jnp.clip(offset, 0, 2 * reach)], 0)
        live = order * QSTEP
        first, second = start(2 * u), start(2 * u + 1)
        pieces = []
        for core in range(2):
            where = jnp.where(col == core, first, second)
            block = data_ref[pl.ds(pl.multiple_of(where, cpd), cpd), tail:].astype(F32)
            pieces.append(block[0:3, :half] + block[3:6, :half] + block[6:9, :half])
        snodes = jnp.concatenate(pieces + [jnp.zeros((3, 2 * LANES - QN), F32)], 1)
        dx = tx - snodes[0:1]
        dy = ty - snodes[1:2]
        dz = tz - snodes[2:3]
        d2 = dx * dx + dy * dy + dz * dz + SOFT * SOFT
        inv = lax.rsqrt(d2)
        radius = d2 * inv
        radius = radius + (0.5 * inv) * (d2 - radius * radius)
        t = radius * turns
        f = t - ((t + ROUNDER) - ROUNDER)
        sin, cos = sincos_turns(f)
        mask = jnp.logical_and(p_at < live, q_at < live)
        scale = jnp.where(mask, (1.0 / FOUR_PI) * inv, 0.0)
        gre_hi[...], gre_lo[...] = two_parts(scale * cos)
        gim_hi[...], gim_lo[...] = two_parts(scale * sin)
        weights = jnp.concatenate(
            [
                data_ref[pl.ds(first, cpd), 0:QN],
                data_ref[pl.ds(second, cpd), 0:QN],
                data_ref[pl.ds(first, cpd), QN : 2 * QN],
                data_ref[pl.ds(second, cpd), QN : 2 * QN],
            ],
            0,
        )
        by_re = dot(gre_hi[:, :QN], weights, NT) + dot(gre_lo[:, :QN], weights, NT)
        by_im = dot(gim_hi[:, :QN], weights, NT) + dot(gim_lo[:, :QN], weights, NT)
        w = 2 * cpd
        hre[:, u * w : (u + 1) * w] = by_re[:, :w] - by_im[:, w:]
        him[:, u * w : (u + 1) * w] = by_re[:, w:] + by_im[:, :w]

    ut_re, ut_im = ut_ref[0], ut_ref[1]
    hre_hi, hre_lo = two_parts(hre[...])
    him_hi, him_lo = two_parts(him[...])
    near_re = (dot(ut_re, hre_hi) + dot(ut_re, hre_lo)) - (dot(ut_im, him_hi) + dot(ut_im, him_lo))
    near_im = (dot(ut_re, him_hi) + dot(ut_re, him_lo)) + (dot(ut_im, hre_hi) + dot(ut_im, hre_lo))

    order_rows = [start(s) for s in range(2 * nrow)]
    excite = jnp.concatenate([data_ref[pl.ds(s, cpd), 2 * QN : tail] for s in order_rows], 0)
    geom_rows = jnp.concatenate([data_ref[pl.ds(s, cpd), tail:] for s in order_rows], 0)
    picked = lax.broadcasted_iota(jnp.int32, (8, LANES), 1) - half
    which = lax.broadcasted_iota(jnp.int32, (8, LANES), 0)
    pick = jnp.logical_and(
        jnp.logical_and(picked >= 0, picked < 4 * PARTS),
        jnp.logical_and(lax.rem(picked + 4 * half, 4) == which, which < 4),
    )
    src = dot(pick.astype(BF16), geom_rows, NT)
    dx = tgeom_ref[:, 0:1] - src[0:1]
    dy = tgeom_ref[:, 1:2] - src[1:2]
    dz = tgeom_ref[:, 2:3] - src[2:3]
    d2 = dx * dx + dy * dy + dz * dz + SOFT * SOFT
    inv = lax.rsqrt(d2)
    radius = d2 * inv
    radius = radius + (0.5 * inv) * (d2 - radius * radius)
    inv = inv * (1.5 - 0.5 * d2 * inv * inv)
    cosine = (tgeom_ref[:, 3:4] * dx + tgeom_ref[:, 4:5] * dy + tgeom_ref[:, 5:6] * dz) * inv
    scale = src[3:4] * ((1.0 / FOUR_PI) * inv)
    phase = wave * radius
    t = phase * INV_TURN
    n = (t + ROUNDER) - ROUNDER
    f = ((phase - n * TURN_HIGH) - n * TURN_LOW) * INV_TURN
    sin, cos = sincos_turns(f)
    green_re = scale * cos
    green_im = scale * sin
    factor_re = 1.0 - cosine
    factor_im = -cosine / phase
    kern_re = (green_re * factor_re - green_im * factor_im).astype(BF16)
    kern_im = (green_re * factor_im + green_im * factor_re).astype(BF16)
    zre_hi, zre_lo = two_parts(near_re)
    zim_hi, zim_lo = two_parts(near_im)
    by_re = dot(kern_re, excite) + (dot(zre_hi, excite) + dot(zre_lo, excite))
    by_im = dot(kern_im, excite) + (dot(zim_hi, excite) + dot(zim_lo, excite))
    h = exc // 2
    out_ref[...] = jnp.concatenate([by_re[:, :h] - by_im[:, h:], by_re[:, h:] + by_im[:, :h]], 1)


def on_device(
    wavenumber, tgt_geom, src_geom, excite, tgt_nodes, src_nodes, tgt_weights, src_weights, near_order
):
    cpd = src_geom.shape[1]
    exc = excite.shape[0]
    cores = lax.axis_size("col")
    nrow = lax.axis_size("row")
    count = cores * nrow
    col = lax.axis_index("col")
    rows_here = tgt_geom.shape[1] // cores
    width = 2 * QN + exc + LANES
    data = pl.pallas_call(
        pack_kernel,
        out_shape=jax.ShapeDtypeStruct((cpd, width), BF16),
    )(src_geom, excite, src_nodes, src_weights)
    even, odd = exchange_steps(count)
    for a, b in zip(even, odd):
        pairs = [(i, i ^ (b if bin(i).count("1") % 2 else a)) for i in range(count)]
        data = jnp.concatenate([data, lax.ppermute(data, ("row", "col"), pairs)], 0)
    data = jnp.concatenate(
        [data, lax.ppermute(data, ("row", "col"), [(i, i ^ 1) for i in range(count)])], 0
    )
    places = (relative_places(even), relative_places(odd))
    places = (
        places[0] + [p ^ 1 for p in places[1]],
        places[1] + [p ^ 1 for p in places[0]],
    )
    tgeom = lax.dynamic_slice_in_dim(tgt_geom, col * rows_here, rows_here, 1).T
    tnodes = lax.dynamic_slice_in_dim(tgt_nodes, col * QN, QN, 1).T
    ut = lax.dynamic_slice_in_dim(tgt_weights, col * rows_here, rows_here, 2).transpose(0, 2, 1)
    return pl.pallas_call(
        functools.partial(field_kernel, nrow, places),
        out_shape=jax.ShapeDtypeStruct((rows_here, exc), F32),
        in_specs=[pl.BlockSpec(memory_space=pltpu.SMEM)] * 2 + [pl.BlockSpec(memory_space=pltpu.VMEM)] * 4,
        scratch_shapes=[pltpu.VMEM((QN, 2 * LANES), BF16)] * 4
        + [pltpu.VMEM((QN, nrow * cores * cpd), F32)] * 2,
    )(wavenumber, near_order, data, tgeom, tnodes, ut)


def solution(mesh):
    return jax.shard_map(
        on_device,
        mesh=mesh,
        in_specs=(
            P("groups"),
            P(None, ("groups", "row")),
            P(None, ("groups", "row", "col")),
            P(None, ("groups", "row", "col")),
            P(None, ("groups", "row")),
            P(None, ("groups", "row")),
            P(None, None, ("groups", "row")),
            P(None, None, ("groups", "row", "col")),
            P(("groups", "row"), None),
        ),
        out_specs=P(("groups", "row", "col"), None),
        check_vma=False,
    )
```

```python
import functools
import math

import jax
import jax.numpy as jnp
from jax import lax
from jax.experimental import pallas as pl
from jax.experimental.pallas import tpu as pltpu
from jax.sharding import PartitionSpec as P

QSTEP = 64
QN = 192
LANES = 128
PARTS = 3
SOFT = 0.05
INV_FOUR_PI = 1.0 / (4.0 * math.pi)
INV_TURN = 1.0 / (2.0 * math.pi)
TURN_HIGH = 6.28125
TURN_LOW = 2.0 * math.pi - TURN_HIGH
SIN_HALF = (3.14159264, -5.16771009, 2.55007766, -0.59829216, 0.07765941)
COS_HALF = (1.0, -4.93480214, 4.05870916, -1.33521206, 0.23493756, -0.02439672)
COS_FULL = (
    0.99999999, -19.73920453, 64.93911898, -85.45016555, 60.16783171, -25.96831321, 6.52961029
)
BF16 = jnp.bfloat16
F32 = jnp.float32
NN = (((1,), (0,)), ((), ()))
NT = (((1,), (1,)), ((), ()))
EXC_AT = 2 * QN
GEOM_AT = QN
NODE_WIDTH = 2 * LANES
SMALL = pltpu.CompilerParams(vmem_limit_bytes=24 * 2**20)


def dot(left, right, dims=NN):
    return lax.dot_general(left, right, dims, preferred_element_type=F32)


def polynomial(z, coefficients):
    total = coefficients[-1]
    for c in coefficients[-2::-1]:
        total = total * z + c
    return total


def sincos_turns(f):
    z = f * f
    s = f * polynomial(z, SIN_HALF)
    c = polynomial(z, COS_HALF)
    twice = s + s
    return twice * c, 1.0 - twice * s


def three_parts(x):
    first = x.astype(BF16)
    rest = x - first.astype(F32)
    second = rest.astype(BF16)
    third = (rest - second.astype(F32)).astype(BF16)
    return first, second, third


def two_parts(x):
    first = x.astype(BF16)
    return first, (x - first.astype(F32)).astype(BF16)


def exchange_steps(count):
    bits = [1 << b for b in range(count.bit_length() - 2, 0, -1)]
    swapped = bits[:-2] + bits[-2:][::-1] if len(bits) >= 2 else bits
    return [b | 1 for b in bits], [b | 1 for b in swapped]


def relative_places(steps):
    places = [0]
    for step in steps:
        places = places + [p ^ step for p in places]
    return places


def pack_kernel(
    units, order_ref, geom_ref, excite_ref, nodes_ref, weights_ref, tnodes_ref, tweights_ref,
    out_ref, target_ref, ut_ref, found_ref,
):
    for slot, order in enumerate(slot_orders(order_ref, units)):
        found_ref[slot] = order
    cpd, exc = excite_ref.shape
    main = LANES
    rest = QN - main
    re, im = weights_ref[0], weights_ref[1]
    out_ref[:, 0:main] = re[:, :main]
    out_ref[:, main : 2 * main] = im[:, :main]
    out_ref[:, 2 * main : 2 * main + 2 * rest] = jnp.concatenate([re[:, main:], im[:, main:]], 1)
    out_ref[:, EXC_AT : EXC_AT + exc] = excite_ref[...]
    parts = [p.astype(F32) for p in three_parts(nodes_ref[...])]
    filler = jnp.zeros((cpd - 3 * PARTS, QN), F32)
    left = jnp.concatenate(parts + [filler], 0)
    geom = jnp.concatenate([p.astype(F32) for p in three_parts(geom_ref[...])], 0).astype(BF16)
    eye = (
        lax.broadcasted_iota(jnp.int32, (cpd, cpd), 0)
        == lax.broadcasted_iota(jnp.int32, (cpd, cpd), 1)
    )
    right = dot(eye.astype(BF16), geom, NT)
    empty = jnp.zeros((cpd, NODE_WIDTH - QN - right.shape[1]), F32)
    out_ref[:, EXC_AT + exc :] = jnp.concatenate([left, right, empty], 1).astype(BF16)
    col = lax.axis_index("col")
    block = tnodes_ref.shape[1] // QN
    nodes = tnodes_ref[:, :QN]
    rows = tweights_ref.shape[2] // block
    for b in range(1, block):
        nodes = jnp.where(col == b, tnodes_ref[:, b * QN : (b + 1) * QN], nodes)
    rest = nodes[:, LANES:]
    start = nodes[:, :QSTEP]
    target_ref[0, 0:3] = nodes[:, :LANES]
    target_ref[1, 0:3] = jnp.concatenate([rest, rest], 1)
    target_ref[2, 0:3] = jnp.concatenate([start, start], 1)
    at = pl.ds(pl.multiple_of(col * rows, LANES), rows)
    re, im = tweights_ref[0, :, at], tweights_ref[1, :, at]
    main = LANES
    ut_ref[0:main, :] = jnp.concatenate([re[:main], im[:main]], 1)
    ut_ref[main : 2 * main, :] = jnp.concatenate([-im[:main], re[:main]], 1)
    ut_ref[2 * main : 2 * main + QSTEP, :] = jnp.concatenate([re[main:], im[main:]], 1)
    ut_ref[2 * main + QSTEP :, :] = jnp.concatenate([-im[main:], re[main:]], 1)


def node_columns(data_ref, slots, exc):
    rows = []
    for slot in range(slots):
        block = data_ref[slot * 16 : slot * 16 + 16, EXC_AT + exc :].astype(F32)
        total = (block[0:3] + block[3:6]) + block[6:9]
        rows.append(jnp.concatenate([total, jnp.zeros((5, NODE_WIDTH), F32)], 0))
    stacked = rows[0] if slots == 1 else jnp.concatenate(rows, 0)
    return stacked.T


def near_slot(order, columns, slot, target_ref, ut_ref, turns, out_ref):
    lane = lax.broadcasted_iota(jnp.int32, (1, LANES), 1)
    quarter = jnp.where(lane < QSTEP, 0.0, 0.25)
    main = LANES

    def distance2(count, tile):
        total = SOFT * SOFT
        for axis in range(3):
            at = columns[:count, 8 * slot + axis : 8 * slot + axis + 1]
            d = at - target_ref[tile, axis : axis + 1, :]
            total = total + d * d
        return total

    def both(count):
        d2 = distance2(count, 0)
        inv = lax.rsqrt(d2)
        t = (d2 * inv) * turns
        sin, cos = sincos_turns(t - jnp.round(t))
        return two_parts(inv * cos), two_parts(inv * sin)

    def split_lanes(count, tile):
        d2 = distance2(count, tile)
        inv = lax.rsqrt(d2)
        t = (d2 * inv) * turns
        f = (t - jnp.round(t - quarter)) - quarter
        return two_parts(inv * polynomial(f * f, COS_FULL))

    def put(at, value):
        high, low = two_parts(value)
        count = value.shape[0]
        out_ref[at : at + count, :LANES] = high
        out_ref[at : at + count, LANES:] = low

    def clear(begin, end):
        out_ref[begin:end, :] = jnp.zeros((end - begin, 2 * LANES), BF16)

    @pl.when(order == 3)
    def _():
        (re_high, re_low), (im_high, im_low) = both(QN)
        rest_high, rest_low = split_lanes(QN, 1)
        high = jnp.concatenate([re_high, im_high, rest_high], 1)
        low = jnp.concatenate([re_low, im_low, rest_low], 1)
        v = dot(high, ut_ref[...]) + dot(low, ut_ref[...])
        put(0, v[:main, :LANES])
        put(main, v[:main, LANES:])
        put(2 * main, v[main:, :LANES])
        put(2 * main + QSTEP, v[main:, LANES:])

    @pl.when(order == 2)
    def _():
        (re_high, re_low), (im_high, im_low) = both(main)
        high = jnp.concatenate([re_high, im_high], 1)
        low = jnp.concatenate([re_low, im_low], 1)
        v = dot(high, ut_ref[: 2 * main]) + dot(low, ut_ref[: 2 * main])
        put(0, v[:, :LANES])
        put(main, v[:, LANES:])
        clear(2 * main, 3 * main)

    @pl.when(order == 1)
    def _():
        high, low = split_lanes(QSTEP, 2)
        weights = jnp.concatenate([ut_ref[0:QSTEP], ut_ref[main : main + QSTEP]], 0)
        v = dot(high, weights) + dot(low, weights)
        put(0, v[:, :LANES])
        clear(QSTEP, main)
        put(main, v[:, LANES:])
        clear(main + QSTEP, 3 * main)

    @pl.when(order == 0)
    def _():
        clear(0, 3 * main)


def slot_orders(order_ref, units):
    row, col = lax.axis_index("row"), lax.axis_index("col")
    nrow = lax.axis_size("row")
    band = order_ref.shape[1]
    reach = (band - 1) // 2
    if units is None:
        offsets = [jnp.where(jnp.logical_and(row + o >= reach, row + o - reach < nrow), o, -1) for o in range(band)]
    else:
        place, parity = row * lax.axis_size("col") + col, 0
        for _ in range((nrow * lax.axis_size("col")).bit_length() - 1):
            parity = parity + lax.rem(place, 2)
            place = lax.div(place, 2)
        parity = lax.rem(parity, 2)
        offsets = [
            (row ^ (a if a == b else jnp.where(parity == 0, a, b))) - row + reach for a, b in zip(*units)
        ]
    return [
        jnp.where(
            jnp.logical_and(o >= 0, o < band), order_ref[col, jnp.clip(o, 0, band - 1)], 0
        )
        for o in offsets
    ]


def near_kernel(
    exc, first, wave_ref, found_ref, data_ref, own_ref, target_ref, ut_ref, v_ref, *copy_ref
):
    if copy_ref:
        copy_ref[0][...] = own_ref[...]
    turns = wave_ref[0] * INV_TURN
    slots = v_ref.shape[0]
    columns = node_columns(data_ref, slots, exc)
    for slot in range(slots):
        near_slot(found_ref[first + slot], columns, slot, target_ref, ut_ref, turns, v_ref.at[slot])


def far_kernel_values(wave, source, tgeom):
    dx = tgeom[0:1] - source[0]
    dy = tgeom[1:2] - source[1]
    dz = tgeom[2:3] - source[2]
    d2 = dx * dx + dy * dy + dz * dz + SOFT * SOFT
    inv = lax.rsqrt(d2)
    radius = d2 * inv
    cosine = (tgeom[3:4] * dx + tgeom[4:5] * dy + tgeom[5:6] * dz) * inv
    scale = source[3] * (INV_FOUR_PI * inv)
    phase = wave * radius
    t = phase * INV_TURN
    n = jnp.round(t)
    sin, cos = sincos_turns(((phase - n * TURN_HIGH) - n * TURN_LOW) * INV_TURN)
    green_re = scale * cos
    green_im = scale * sin
    factor_re = 1.0 - cosine
    factor_im = -cosine / phase
    kern_re = (green_re * factor_re - green_im * factor_im).astype(BF16)
    kern_im = (green_re * factor_im + green_im * factor_re).astype(BF16)
    return kern_re.astype(F32), kern_im.astype(F32)


def last_kernel(exc, partner, wave_ref, own_ref, other_ref, tgeom_ref, *refs):
    out_ref, zre, zim = refs[-3:]
    col = lax.axis_index("col")
    rows = out_ref.shape[0]
    cpd = 16
    main = LANES
    slots = len(partner)
    sign = jnp.where(lax.broadcasted_iota(jnp.int32, (1, LANES), 1) < QSTEP, 1.0, -1.0).astype(BF16)

    def weight_rows(ref):
        w = [ref[:, i * main : (i + 1) * main] for i in range(3)]
        swapped = jnp.concatenate([w[2][:, QSTEP:], w[2][:, :QSTEP]], 1)
        return jnp.concatenate([w[0], -w[1], w[2] * sign], 1), jnp.concatenate([w[1], w[0], swapped], 1)

    own_re, own_im = weight_rows(own_ref)
    other_re, other_im = weight_rows(other_ref)
    slot = 0
    for v_ref in refs[:-3]:
        for i in range(v_ref.shape[0]):
            here = slice(slot * cpd, (slot + 1) * cpd)
            there = slice(partner[slot] * cpd, (partner[slot] + 1) * cpd)
            left = jnp.concatenate([own_re[here], other_re[there], own_im[here], other_im[there]], 0)
            product = dot(left, v_ref[i])
            a = (product[:, :LANES] + product[:, LANES:]) * INV_FOUR_PI
            there = slice((slots + partner[slot]) * cpd, (slots + partner[slot] + 1) * cpd)
            zre[here] = a[0:cpd]
            zre[there] = a[cpd : 2 * cpd]
            zim[here] = a[2 * cpd : 3 * cpd]
            zim[there] = a[3 * cpd :]
            slot += 1

    geom_at = EXC_AT + exc + GEOM_AT - QSTEP
    geom = jnp.concatenate([own_ref[:, geom_at:], other_ref[:, geom_at:]], 0)
    at = lax.broadcasted_iota(jnp.int32, (LANES, 4 * LANES), 0) - QSTEP
    wanted = lax.div(lax.broadcasted_iota(jnp.int32, (LANES, 4 * LANES), 1), LANES)
    pick = jnp.logical_and(
        jnp.logical_and(at >= 0, at < 4 * PARTS), lax.rem(at + QSTEP, 4) == wanted
    )
    spread = dot(geom, jnp.where(pick, 1.0, 0.0).astype(BF16))
    source = [spread[:, i * LANES : (i + 1) * LANES] for i in range(4)]
    tgeom = tgeom_ref[:, pl.ds(pl.multiple_of(col * rows, LANES), rows)]
    kern_re, kern_im = far_kernel_values(wave_ref[0], source, tgeom)
    excite = jnp.concatenate(
        [own_ref[:, EXC_AT : EXC_AT + exc], other_ref[:, EXC_AT : EXC_AT + exc]], 0
    ).T
    re = two_parts(kern_re + zre[...])
    im = two_parts(kern_im + zim[...])
    by_re = dot(excite, re[0]) + dot(excite, re[1])
    by_im = dot(excite, im[0]) + dot(excite, im[1])
    h = exc // 2
    result = jnp.concatenate([by_re[:h] - by_im[h:], by_re[h:] + by_im[:h]], 0)
    out_ref[...] = result.T


def in_vmem(x):
    return pltpu.with_memory_space_constraint(x, pltpu.VMEM)


def in_smem(x):
    return pltpu.with_memory_space_constraint(x, pltpu.SMEM)


def in_hbm(x):
    return pltpu.with_memory_space_constraint(x, pltpu.HBM)


SMEM_SPEC = pl.BlockSpec(memory_space=pltpu.SMEM)
VMEM_SPEC = pl.BlockSpec(memory_space=pltpu.VMEM)


def packed(units, slots, src_geom, excite, src_nodes, src_weights, tgt_nodes, tgt_weights, near_order):
    cpd = src_geom.shape[1]
    width = EXC_AT + excite.shape[0] + NODE_WIDTH
    return pl.pallas_call(
        functools.partial(pack_kernel, units),
        out_shape=[
            pltpu.VMEM((cpd, width), BF16),
            pltpu.VMEM((3, 8, LANES), F32),
            pltpu.VMEM((2 * QN, 2 * LANES), BF16),
            pltpu.SMEM((slots,), jnp.int32),
        ],
        in_specs=[SMEM_SPEC] + [VMEM_SPEC] * 6,
        out_specs=[VMEM_SPEC] * 3 + [SMEM_SPEC],
        compiler_params=SMALL,
    )(
        in_hbm(near_order),
        *[in_hbm(x) for x in (src_geom, excite.T, src_nodes, src_weights.transpose(0, 2, 1))],
        in_hbm(tgt_nodes),
        in_hbm(tgt_weights),
    )


def near_blocks(exc, first, slots, wavenumber, found, fresh, own, target, ut, hand_on):
    cost = pl.CostEstimate(flops=slots * 10**8, bytes_accessed=10**6, transcendentals=slots * 36864)
    return pl.pallas_call(
        functools.partial(near_kernel, exc, first),
        out_shape=[pltpu.VMEM((slots, 2 * QN, 2 * LANES), BF16), pltpu.VMEM(own.shape, BF16)][: 1 + hand_on],
        in_specs=[SMEM_SPEC] * 2 + [VMEM_SPEC] * 4,
        out_specs=[VMEM_SPEC] * (1 + hand_on),
        compiler_params=SMALL,
        cost_estimate=cost,
    )(wavenumber, in_smem(found), in_vmem(fresh), in_vmem(own), in_vmem(target), in_vmem(ut))


def exchanged(
    wavenumber, tgt_geom, src_geom, excite, tgt_nodes, src_nodes, tgt_weights, src_weights, near_order
):
    cpd = src_geom.shape[1]
    exc = excite.shape[0]
    cores = lax.axis_size("col")
    count = cores * lax.axis_size("row")
    rows_here = tgt_geom.shape[1] // cores
    even, odd = exchange_steps(count)
    units = [[p >> 1 for p in relative_places(s)] for s in (even, odd)]
    own, target, ut, found = packed(
        units, len(units[0]), src_geom, excite, src_nodes, src_weights, tgt_nodes, tgt_weights, near_order
    )

    def moved(value, a, b):
        pairs = [(i, i ^ (b if bin(i).count("1") % 2 else a)) for i in range(count)]
        return lax.ppermute(value, ("row", "col"), pairs)

    fresh = own
    near = []
    done = 0
    for a, b in list(zip(even, odd)) + [(1, 1)]:
        arriving = moved(own, a, b)
        slots = fresh.shape[0] // cpd
        v, *copy = near_blocks(exc, done, slots, wavenumber, found, fresh, own, target, ut, a != 1)
        near.append(v)
        done += slots
        fresh = arriving
        if a != 1:
            own = jnp.concatenate([copy[0], arriving], 0)
    partner = [units[1].index(u) for u in units[0]]
    return pl.pallas_call(
        functools.partial(last_kernel, exc, partner),
        out_shape=jax.ShapeDtypeStruct((rows_here, exc), F32),
        in_specs=[SMEM_SPEC] + [VMEM_SPEC] * (3 + len(near)),
        out_specs=VMEM_SPEC,
        scratch_shapes=[pltpu.VMEM((count * cpd, rows_here), F32)] * 2,
        compiler_params=SMALL,
    )(wavenumber, in_vmem(own), in_vmem(fresh), in_vmem(tgt_geom), *[in_vmem(v) for v in near])


def gathered(
    wavenumber, tgt_geom, src_geom, excite, tgt_nodes, src_nodes, tgt_weights, src_weights, near_order
):
    cpd = src_geom.shape[1]
    exc = excite.shape[0]
    half = exc // 2
    cores = lax.axis_size("col")
    nrow = lax.axis_size("row")
    row = lax.axis_index("row")
    rows_here = tgt_geom.shape[1] // cores
    band = near_order.shape[1]
    own, target, ut, found = packed(
        None, band, src_geom, excite, src_nodes, src_weights, tgt_nodes, tgt_weights, near_order
    )
    everything = lax.all_gather(own, ("row", "col"), axis=0, tiled=True)
    sources = lax.all_gather(src_geom, ("row", "col"), axis=1, tiled=True)
    blocks = [
        lax.dynamic_slice_in_dim(
            everything, jnp.clip(row + o - (band - 1) // 2, 0, nrow - 1) * cores * cpd, cores * cpd, 0
        )
        for o in range(band)
    ]
    fresh = jnp.concatenate([block[:cpd] for block in blocks], 0)
    (near,) = near_blocks(exc, 0, band, wavenumber, found, fresh, own, target, ut, False)
    high = lax.Precision.HIGHEST
    total = jnp.zeros((rows_here, exc), F32)
    dims = (((0,), (0,)), ((), ()))
    m, r = LANES, QN - LANES
    for o, block in enumerate(blocks):
        w, x = block[:, :EXC_AT].astype(F32), block[:, EXC_AT : EXC_AT + exc].astype(F32)
        v = near[o, :, :LANES].astype(F32) + near[o, :, LANES:].astype(F32)
        w_re = jnp.concatenate([w[:, :m], w[:, 2 * m : 2 * m + r]], 1)
        w_im = jnp.concatenate([w[:, m : 2 * m], w[:, 2 * m + r :]], 1)
        v_re = jnp.concatenate([v[:m], v[2 * m : 2 * m + r]], 0)
        v_im = jnp.concatenate([v[m : 2 * m], v[2 * m + r :]], 0)
        a_re = jnp.dot(w_re, v_re, precision=high) - jnp.dot(w_im, v_im, precision=high)
        a_im = jnp.dot(w_re, v_im, precision=high) + jnp.dot(w_im, v_re, precision=high)
        re = lax.dot_general(a_re, x, dims, precision=high)
        im = lax.dot_general(a_im, x, dims, precision=high)
        total = total + INV_FOUR_PI * jnp.concatenate(
            [re[:, :half] - im[:, half:], re[:, half:] + im[:, :half]], 1
        )
    targets = lax.dynamic_slice_in_dim(tgt_geom, lax.axis_index("col") * rows_here, rows_here, 1)
    width = math.gcd(everything.shape[0], 512)

    def far(index, accum):
        places = lax.dynamic_slice_in_dim(sources, index * width, width, 1)
        x = lax.dynamic_slice_in_dim(everything, index * width, width, 0)[:, EXC_AT : EXC_AT + exc]
        kern_re, kern_im = far_kernel_values(
            wavenumber[0], [places[i][:, None] for i in range(4)], targets
        )
        re = lax.dot_general(kern_re.astype(BF16), x, dims, preferred_element_type=F32)
        im = lax.dot_general(kern_im.astype(BF16), x, dims, preferred_element_type=F32)
        return accum + jnp.concatenate([re[:, :half] - im[:, half:], re[:, half:] + im[:, :half]], 1)

    return lax.fori_loop(0, everything.shape[0] // width, far, total)


def on_device(*arguments):
    count = lax.axis_size("row") * lax.axis_size("col")
    short = lax.axis_size("col") == 2 and lax.axis_size("row") <= 16 and count & (count - 1) == 0
    return (exchanged if short and count >= 8 else gathered)(*arguments)


def solution(mesh):
    return jax.shard_map(
        on_device,
        mesh=mesh,
        in_specs=(
            P("groups"),
            P(None, ("groups", "row")),
            P(None, ("groups", "row", "col")),
            P(None, ("groups", "row", "col")),
            P(None, ("groups", "row")),
            P(None, ("groups", "row")),
            P(None, None, ("groups", "row")),
            P(None, None, ("groups", "row", "col")),
            P(("groups", "row"), None),
        ),
        out_specs=P(("groups", "row", "col"), None),
        check_vma=False,
    )
```

```python
import functools
import math

import jax
import jax.numpy as jnp
from jax import lax
from jax.experimental import pallas as pl
from jax.experimental.pallas import tpu as pltpu
from jax.sharding import PartitionSpec as P

QSTEP = 64
QN = 192
LANES = 128
PARTS = 3
SOFT = 0.05
INV_FOUR_PI = 1.0 / (4.0 * math.pi)
INV_TURN = 1.0 / (2.0 * math.pi)
TURN_HIGH = 6.28125
TURN_LOW = 2.0 * math.pi - TURN_HIGH
SIN_HALF = (3.14159264, -5.16771009, 2.55007766, -0.59829216, 0.07765941)
COS_HALF = (1.0, -4.93480214, 4.05870916, -1.33521206, 0.23493756, -0.02439672)
COS_FULL = (
    0.99999999, -19.73920453, 64.93911898, -85.45016555, 60.16783171, -25.96831321, 6.52961029
)
BF16 = jnp.bfloat16
F32 = jnp.float32
NN = (((1,), (0,)), ((), ()))
NT = (((1,), (1,)), ((), ()))
EXC_AT = 2 * QN
NODE_WIDTH = LANES
SMALL = pltpu.CompilerParams(vmem_limit_bytes=24 * 2**20)


def dot(left, right, dims=NN):
    return lax.dot_general(left, right, dims, preferred_element_type=F32)


def polynomial(z, coefficients):
    total = coefficients[-1]
    for c in coefficients[-2::-1]:
        total = total * z + c
    return total


def sincos_turns(f):
    z = f * f
    s = f * polynomial(z, SIN_HALF)
    c = polynomial(z, COS_HALF)
    twice = s + s
    return twice * c, 1.0 - twice * s


def three_parts(x):
    first = x.astype(BF16)
    rest = x - first.astype(F32)
    second = rest.astype(BF16)
    third = (rest - second.astype(F32)).astype(BF16)
    return first, second, third


def two_parts(x):
    first = x.astype(BF16)
    return first, (x - first.astype(F32)).astype(BF16)


def exchange_steps(count):
    bits = [1 << b for b in range(count.bit_length() - 2, 0, -1)]
    swapped = bits[:-2] + bits[-2:][::-1] if len(bits) >= 2 else bits
    return [b | 1 for b in bits], [b | 1 for b in swapped]


def relative_places(steps):
    places = [0]
    for step in steps:
        places = places + [p ^ step for p in places]
    return places


def iota(shape, axis):
    return lax.broadcasted_iota(jnp.int32, shape, axis)


def geom_lane(cpd):
    return 3 * PARTS * (QN // cpd)


def place_matrices(cpd):
    groups = QN // cpd
    shape = (LANES, 2 * 16)
    begin, row = iota(shape, 0), iota(shape, 1)
    node = jnp.logical_and(begin >= row * groups, begin < (row + 1) * groups)
    node = jnp.logical_and(node, row < 3 * PARTS)
    source = jnp.logical_and(begin - geom_lane(cpd) == row - 16, row >= 16)
    row_of = jnp.where(jnp.logical_or(node, source), 1.0, 0.0).astype(BF16)
    shape = (LANES, QN)
    lane, group = iota(shape, 0), lax.div(iota(shape, 1), cpd)
    wanted = jnp.where(lane < geom_lane(cpd), lax.rem(lane, groups), 0)
    kept = jnp.where(group == wanted, 1.0, 0.0)
    shape = (cpd, QN)
    column_of = jnp.where(lax.rem(iota(shape, 1), cpd) == iota(shape, 0), 1.0, 0.0).astype(BF16)
    return row_of, kept, column_of


def pack_kernel(
    units, order_hbm, geom_hbm, excite_hbm, nodes_hbm, weights_hbm, tnodes_hbm, tweights_hbm,
    out_ref, target_ref, tests_ref, found_ref,
    order_ref, geom_ref, excite_ref, nodes_ref, weights_ref, tnodes_ref, arrived,
):
    col = lax.axis_index("col")
    rows = tests_ref.shape[2]
    at = pl.ds(pl.multiple_of(col * rows, LANES), rows)
    moves = [
        (weights_hbm, weights_ref),
        (nodes_hbm, nodes_ref),
        (geom_hbm, geom_ref),
        (excite_hbm, excite_ref),
        (tnodes_hbm, tnodes_ref),
        (order_hbm, order_ref),
        (tweights_hbm.at[:, :, at], tests_ref),
    ]
    copies = [pltpu.make_async_copy(*move, arrived.at[i]) for i, move in enumerate(moves)]
    for copy in copies:
        copy.start()
    cpd, exc = excite_ref.shape
    row_of, kept, column_of = place_matrices(cpd)
    for copy in copies[:-1]:
        copy.wait()
    main = LANES
    rest = QN - main
    re, im = weights_ref[0], weights_ref[1]
    out_ref[:, 0:main] = re[:, :main]
    out_ref[:, main : 2 * main] = im[:, :main]
    out_ref[:, 2 * main : 2 * main + 2 * rest] = jnp.concatenate([re[:, main:], im[:, main:]], 1)
    out_ref[:, EXC_AT : EXC_AT + exc] = excite_ref[...]
    nodes = [p.astype(F32) for p in three_parts(nodes_ref[...])]
    geom = jnp.concatenate([p.astype(F32) for p in three_parts(geom_ref[...])], 0)
    values = jnp.concatenate(
        nodes
        + [
            jnp.zeros((16 - 3 * PARTS, QN), F32),
            jnp.concatenate([geom, jnp.zeros((geom.shape[0], QN - cpd), F32)], 1),
            jnp.zeros((16 - geom.shape[0], QN), F32),
        ],
        0,
    ).astype(BF16)
    spread = (dot(row_of, values) * kept).astype(BF16)
    out_ref[:, EXC_AT + exc :] = dot(column_of, spread, NT).astype(BF16)
    nodes = tnodes_ref[:, :QN]
    for b in range(1, tnodes_ref.shape[1] // QN):
        nodes = jnp.where(col == b, tnodes_ref[:, b * QN : (b + 1) * QN], nodes)
    end = nodes[:, LANES:]
    start = nodes[:, :QSTEP]
    target_ref[0, 0:3] = nodes[:, :LANES]
    target_ref[1, 0:3] = jnp.concatenate([end, end], 1)
    target_ref[2, 0:3] = jnp.concatenate([start, start], 1)
    for slot, order in enumerate(slot_orders(order_ref, units)):
        found_ref[slot] = order
    copies[-1].wait()


def store_tests(tests_ref, ut_ref):
    re, im = tests_ref[0], tests_ref[1]
    main = LANES
    ut_ref[0:main, :] = jnp.concatenate([re[:main], im[:main]], 1)
    ut_ref[main : 2 * main, :] = jnp.concatenate([-im[:main], re[:main]], 1)
    ut_ref[2 * main : 2 * main + QSTEP, :] = jnp.concatenate([re[main:], im[main:]], 1)
    ut_ref[2 * main + QSTEP :, :] = jnp.concatenate([-im[main:], re[main:]], 1)


def node_columns(data_ref, exc):
    block = data_ref[:, EXC_AT + exc :].astype(F32)
    step = geom_lane(16) // PARTS
    return (block[:, :step] + block[:, step : 2 * step]) + block[:, 2 * step : 3 * step]


def two_part_dot(high, low, right):
    count = high.shape[0]
    both = dot(jnp.concatenate([high, low], 0), right)
    return both[:count] + both[count:]


def near_slot(order, columns, slot, target_ref, ut_ref, turns, out_ref):
    lane = lax.broadcasted_iota(jnp.int32, (1, LANES), 1)
    quarter = jnp.where(lane < QSTEP, 0.0, 0.25)
    main = LANES

    def distance2(count, tile):
        total = SOFT * SOFT
        for axis in range(3):
            at = [
                jnp.broadcast_to(columns[16 * slot : 16 * slot + 16, lane : lane + 1], (16, LANES))
                for lane in range(axis * (QN // 16), axis * (QN // 16) + count // 16)
            ]
            d = jnp.concatenate(at, 0) - target_ref[tile, axis : axis + 1, :]
            total = total + d * d
        return total

    def both(count):
        d2 = distance2(count, 0)
        inv = lax.rsqrt(d2)
        t = (d2 * inv) * turns
        sin, cos = sincos_turns(t - jnp.round(t))
        return two_parts(inv * cos), two_parts(inv * sin)

    def split_lanes(count, tile):
        d2 = distance2(count, tile)
        inv = lax.rsqrt(d2)
        t = (d2 * inv) * turns
        f = (t - jnp.round(t - quarter)) - quarter
        return two_parts(inv * polynomial(f * f, COS_FULL))

    def put(at, value):
        high, low = two_parts(value)
        count = value.shape[0]
        out_ref[at : at + count, :LANES] = high
        out_ref[at : at + count, LANES:] = low

    def clear(begin, end):
        out_ref[begin:end, :] = jnp.zeros((end - begin, 2 * LANES), BF16)

    @pl.when(order == 3)
    def _():
        (re_high, re_low), (im_high, im_low) = both(QN)
        rest_high, rest_low = split_lanes(QN, 1)
        high = jnp.concatenate([re_high, im_high, rest_high], 1)
        low = jnp.concatenate([re_low, im_low, rest_low], 1)
        v = two_part_dot(high, low, ut_ref[...])
        put(0, v[:main, :LANES])
        put(main, v[:main, LANES:])
        put(2 * main, v[main:, :LANES])
        put(2 * main + QSTEP, v[main:, LANES:])

    @pl.when(order == 2)
    def _():
        (re_high, re_low), (im_high, im_low) = both(main)
        high = jnp.concatenate([re_high, im_high], 1)
        low = jnp.concatenate([re_low, im_low], 1)
        v = two_part_dot(high, low, ut_ref[: 2 * main])
        put(0, v[:, :LANES])
        put(main, v[:, LANES:])
        clear(2 * main, 3 * main)

    @pl.when(order == 1)
    def _():
        high, low = split_lanes(QSTEP, 2)
        weights = jnp.concatenate([ut_ref[0:QSTEP], ut_ref[main : main + QSTEP]], 0)
        v = two_part_dot(high, low, weights)
        put(0, v[:, :LANES])
        clear(QSTEP, main)
        put(main, v[:, LANES:])
        clear(main + QSTEP, 3 * main)

    @pl.when(order == 0)
    def _():
        clear(0, 3 * main)


def slot_orders(order_ref, units):
    row, col = lax.axis_index("row"), lax.axis_index("col")
    nrow = lax.axis_size("row")
    band = order_ref.shape[1]
    reach = (band - 1) // 2
    if units is None:
        offsets = [jnp.where(jnp.logical_and(row + o >= reach, row + o - reach < nrow), o, -1) for o in range(band)]
    else:
        place, parity = row * lax.axis_size("col") + col, 0
        for _ in range((nrow * lax.axis_size("col")).bit_length() - 1):
            parity = parity + lax.rem(place, 2)
            place = lax.div(place, 2)
        parity = lax.rem(parity, 2)
        offsets = [
            (row ^ (a if a == b else jnp.where(parity == 0, a, b))) - row + reach for a, b in zip(*units)
        ]
    return [
        jnp.where(
            jnp.logical_and(o >= 0, o < band), order_ref[col, jnp.clip(o, 0, band - 1)], 0
        )
        for o in offsets
    ]


def far_kernel_values(wave, source, tgeom):
    dx = tgeom[0:1] - source[0]
    dy = tgeom[1:2] - source[1]
    dz = tgeom[2:3] - source[2]
    d2 = dx * dx + dy * dy + dz * dz + SOFT * SOFT
    inv = lax.rsqrt(d2)
    radius = d2 * inv
    cosine = (tgeom[3:4] * dx + tgeom[4:5] * dy + tgeom[5:6] * dz) * inv
    scale = source[3] * (INV_FOUR_PI * inv)
    phase = wave * radius
    t = phase * INV_TURN
    n = jnp.round(t)
    sin, cos = sincos_turns(((phase - n * TURN_HIGH) - n * TURN_LOW) * INV_TURN)
    green_re = scale * cos
    green_im = scale * sin
    factor_re = 1.0 - cosine
    factor_im = cosine * (inv * (-1.0 / wave))
    kern_re = (green_re * factor_re - green_im * factor_im).astype(BF16)
    kern_im = (green_re * factor_im + green_im * factor_re).astype(BF16)
    return kern_re, kern_im


def far_rows(data, exc, wave, tgeom):
    shape = (LANES, 4 * LANES)
    at, wanted = iota(shape, 0) - geom_lane(16), lax.div(iota(shape, 1), LANES)
    pick = jnp.logical_and(
        jnp.logical_and(at >= 0, at < 4 * PARTS), lax.rem(at + 4 * LANES, 4) == wanted
    )
    geom = data[:, EXC_AT + exc :]
    spread = dot(geom, jnp.where(pick, 1.0, 0.0).astype(BF16))
    return far_kernel_values(wave, [spread[:, i * LANES : (i + 1) * LANES] for i in range(4)], tgeom)


def own_targets(tgeom_ref, rows):
    at = pl.multiple_of(lax.axis_index("col") * rows, LANES)
    return tgeom_ref[:, pl.ds(at, rows)]


def near_kernel(
    exc, first, wave_ref, found_ref, data_ref, own_ref, target_ref, ut_ref, tgeom_ref,
    v_ref, kern_re_ref, kern_im_ref, *copy_ref,
):
    if copy_ref:
        copy_ref[0][...] = own_ref[...]
    wave = wave_ref[0]
    tgeom = own_targets(tgeom_ref, kern_re_ref.shape[1])
    kern_re_ref[...], kern_im_ref[...] = far_rows(data_ref, exc, wave, tgeom)
    slots = v_ref.shape[0]
    columns = node_columns(data_ref, exc)
    for slot in range(slots):
        near_slot(found_ref[first + slot], columns, slot, target_ref, ut_ref, wave * INV_TURN, v_ref.at[slot])


def first_near_kernel(
    exc, first, wave_ref, found_ref, data_ref, own_ref, target_ref, tests_ref, tgeom_ref, *refs
):
    *refs, ut_ref = refs
    store_tests(tests_ref, ut_ref)
    near_kernel(exc, first, wave_ref, found_ref, data_ref, own_ref, target_ref, ut_ref, tgeom_ref, *refs)


def last_kernel(exc, partner, wave_ref, own_ref, other_ref, tgeom_ref, *refs):
    out_ref, zre, zim = refs[-3:]
    v_refs, kern_re_refs, kern_im_refs = refs[:-3:3], refs[1:-3:3], refs[2:-3:3]
    rows = out_ref.shape[0]
    cpd = 16
    main = LANES
    slots = len(partner)
    sign = jnp.where(lax.broadcasted_iota(jnp.int32, (1, LANES), 1) < QSTEP, 1.0, -1.0).astype(BF16)

    def weight_rows(ref):
        w = [ref[:, i * main : (i + 1) * main] for i in range(3)]
        swapped = jnp.concatenate([w[2][:, QSTEP:], w[2][:, :QSTEP]], 1)
        return jnp.concatenate([w[0], -w[1], w[2] * sign], 1), jnp.concatenate([w[1], w[0], swapped], 1)

    own_re, own_im = weight_rows(own_ref)
    other_re, other_im = weight_rows(other_ref)
    slot = 0
    for v_ref in v_refs:
        for i in range(v_ref.shape[0]):
            here = slice(slot * cpd, (slot + 1) * cpd)
            there = slice(partner[slot] * cpd, (partner[slot] + 1) * cpd)
            left = jnp.concatenate([own_re[here], other_re[there], own_im[here], other_im[there]], 0)
            product = dot(left, v_ref[i])
            a = (product[:, :LANES] + product[:, LANES:]) * INV_FOUR_PI
            there = slice((slots + partner[slot]) * cpd, (slots + partner[slot] + 1) * cpd)
            zre[here] = a[0:cpd]
            zre[there] = a[cpd : 2 * cpd]
            zim[here] = a[2 * cpd : 3 * cpd]
            zim[there] = a[3 * cpd :]
            slot += 1

    other_kern = far_rows(other_ref, exc, wave_ref[0], own_targets(tgeom_ref, rows))
    kern_re, kern_im = [
        jnp.concatenate([ref[...] for ref in refs] + [other], 0).astype(F32)
        for refs, other in zip((kern_re_refs, kern_im_refs), other_kern)
    ]
    excite = jnp.concatenate(
        [own_ref[:, EXC_AT : EXC_AT + exc], other_ref[:, EXC_AT : EXC_AT + exc]], 0
    ).T
    re = two_parts(kern_re + zre[...])
    im = two_parts(kern_im + zim[...])
    product = dot(excite, jnp.concatenate([*re, *im], 1))
    by_re = product[:, :rows] + product[:, rows : 2 * rows]
    by_im = product[:, 2 * rows : 3 * rows] + product[:, 3 * rows :]
    h = exc // 2
    result = jnp.concatenate([by_re[:h] - by_im[h:], by_re[h:] + by_im[:h]], 0)
    out_ref[...] = result.T


def in_vmem(x):
    return pltpu.with_memory_space_constraint(x, pltpu.VMEM)


def in_smem(x):
    return pltpu.with_memory_space_constraint(x, pltpu.SMEM)


def in_hbm(x):
    return pltpu.with_memory_space_constraint(x, pltpu.HBM)


SMEM_SPEC = pl.BlockSpec(memory_space=pltpu.SMEM)
VMEM_SPEC = pl.BlockSpec(memory_space=pltpu.VMEM)


def packed(units, slots, src_geom, excite, src_nodes, src_weights, tgt_nodes, tgt_weights, near_order):
    excite = excite.T
    src_weights = src_weights.transpose(0, 2, 1)
    cpd, exc = excite.shape
    rows_here = tgt_weights.shape[2] // lax.axis_size("col")
    inputs = (near_order, src_geom, excite, src_nodes, src_weights, tgt_nodes)
    return pl.pallas_call(
        functools.partial(pack_kernel, units),
        out_shape=[
            pltpu.VMEM((cpd, EXC_AT + exc + NODE_WIDTH), BF16),
            pltpu.VMEM((3, 8, LANES), F32),
            pltpu.VMEM((2, QN, rows_here), BF16),
            pltpu.SMEM((slots,), jnp.int32),
        ],
        in_specs=[pl.BlockSpec(memory_space=pl.ANY)] * 7,
        out_specs=[VMEM_SPEC] * 3 + [SMEM_SPEC],
        scratch_shapes=[pltpu.SMEM(near_order.shape, jnp.int32)]
        + [pltpu.VMEM(x.shape, x.dtype) for x in inputs[1:]]
        + [pltpu.SemaphoreType.DMA((7,))],
        compiler_params=SMALL,
    )(*[in_hbm(x) for x in inputs], in_hbm(tgt_weights))


def near_blocks(exc, first, slots, wavenumber, found, fresh, own, target, ut, tgt_geom, hand_on):
    rows_here = tgt_geom.shape[1] // lax.axis_size("col")
    kern = pltpu.VMEM((fresh.shape[0], rows_here), BF16)
    cost = pl.CostEstimate(flops=slots * 10**8, bytes_accessed=10**6, transcendentals=slots * 36864)
    outs = [pltpu.VMEM((slots, 2 * QN, 2 * LANES), BF16), kern, kern] + [pltpu.VMEM(own.shape, BF16)] * hand_on
    if first == 0:
        outs.append(pltpu.VMEM((2 * QN, 2 * LANES), BF16))
    return pl.pallas_call(
        functools.partial(near_kernel if first else first_near_kernel, exc, first),
        out_shape=outs,
        in_specs=[SMEM_SPEC] * 2 + [VMEM_SPEC] * 5,
        out_specs=[VMEM_SPEC] * len(outs),
        compiler_params=SMALL,
        cost_estimate=cost,
    )(wavenumber, in_smem(found), in_vmem(fresh), in_vmem(own), in_vmem(target), in_vmem(ut), in_vmem(tgt_geom))


def exchanged(
    wavenumber, tgt_geom, src_geom, excite, tgt_nodes, src_nodes, tgt_weights, src_weights, near_order
):
    cpd = src_geom.shape[1]
    exc = excite.shape[0]
    cores = lax.axis_size("col")
    count = cores * lax.axis_size("row")
    rows_here = tgt_geom.shape[1] // cores
    even, odd = exchange_steps(count)
    units = [[p >> 1 for p in relative_places(s)] for s in (even, odd)]
    own, target, ut, found = packed(
        units, len(units[0]), src_geom, excite, src_nodes, src_weights, tgt_nodes, tgt_weights, near_order
    )

    def moved(value, a, b):
        pairs = [(i, i ^ (b if bin(i).count("1") % 2 else a)) for i in range(count)]
        return lax.ppermute(value, ("row", "col"), pairs)

    fresh = own
    near = []
    done = 0
    for a, b in list(zip(even, odd)) + [(1, 1)]:
        arriving = moved(own, a, b)
        slots = fresh.shape[0] // cpd
        made = near_blocks(exc, done, slots, wavenumber, found, fresh, own, target, ut, tgt_geom, a != 1)
        near.extend(made[:3])
        if not done:
            ut = made[4]
        done += slots
        fresh = arriving
        if a != 1:
            own = jnp.concatenate([made[3], arriving], 0)
    partner = [units[1].index(u) for u in units[0]]
    return pl.pallas_call(
        functools.partial(last_kernel, exc, partner),
        out_shape=jax.ShapeDtypeStruct((rows_here, exc), F32),
        in_specs=[SMEM_SPEC] + [VMEM_SPEC] * (3 + len(near)),
        out_specs=VMEM_SPEC,
        scratch_shapes=[pltpu.VMEM((count * cpd, rows_here), F32)] * 2,
        compiler_params=SMALL,
    )(wavenumber, in_vmem(own), in_vmem(fresh), in_vmem(tgt_geom), *[in_vmem(v) for v in near])


def gathered(
    wavenumber, tgt_geom, src_geom, excite, tgt_nodes, src_nodes, tgt_weights, src_weights, near_order
):
    cpd = src_geom.shape[1]
    exc = excite.shape[0]
    half = exc // 2
    cores = lax.axis_size("col")
    nrow = lax.axis_size("row")
    row = lax.axis_index("row")
    rows_here = tgt_geom.shape[1] // cores
    band = near_order.shape[1]
    own, target, ut, found = packed(
        None, band, src_geom, excite, src_nodes, src_weights, tgt_nodes, tgt_weights, near_order
    )
    everything = lax.all_gather(own, ("row", "col"), axis=0, tiled=True)
    sources = lax.all_gather(src_geom, ("row", "col"), axis=1, tiled=True)
    blocks = [
        lax.dynamic_slice_in_dim(
            everything, jnp.clip(row + o - (band - 1) // 2, 0, nrow - 1) * cores * cpd, cores * cpd, 0
        )
        for o in range(band)
    ]
    fresh = jnp.concatenate([block[:cpd] for block in blocks], 0)
    near = near_blocks(exc, 0, band, wavenumber, found, fresh, own, target, ut, tgt_geom, False)[0]
    high = lax.Precision.HIGHEST
    total = jnp.zeros((rows_here, exc), F32)
    dims = (((0,), (0,)), ((), ()))
    m, r = LANES, QN - LANES
    for o, block in enumerate(blocks):
        w, x = block[:, :EXC_AT].astype(F32), block[:, EXC_AT : EXC_AT + exc].astype(F32)
        v = near[o, :, :LANES].astype(F32) + near[o, :, LANES:].astype(F32)
        w_re = jnp.concatenate([w[:, :m], w[:, 2 * m : 2 * m + r]], 1)
        w_im = jnp.concatenate([w[:, m : 2 * m], w[:, 2 * m + r :]], 1)
        v_re = jnp.concatenate([v[:m], v[2 * m : 2 * m + r]], 0)
        v_im = jnp.concatenate([v[m : 2 * m], v[2 * m + r :]], 0)
        a_re = jnp.dot(w_re, v_re, precision=high) - jnp.dot(w_im, v_im, precision=high)
        a_im = jnp.dot(w_re, v_im, precision=high) + jnp.dot(w_im, v_re, precision=high)
        re = lax.dot_general(a_re, x, dims, precision=high)
        im = lax.dot_general(a_im, x, dims, precision=high)
        total = total + INV_FOUR_PI * jnp.concatenate(
            [re[:, :half] - im[:, half:], re[:, half:] + im[:, :half]], 1
        )
    targets = lax.dynamic_slice_in_dim(tgt_geom, lax.axis_index("col") * rows_here, rows_here, 1)
    width = math.gcd(everything.shape[0], 512)

    def far(index, accum):
        places = lax.dynamic_slice_in_dim(sources, index * width, width, 1)
        x = lax.dynamic_slice_in_dim(everything, index * width, width, 0)[:, EXC_AT : EXC_AT + exc]
        kern_re, kern_im = far_kernel_values(
            wavenumber[0], [places[i][:, None] for i in range(4)], targets
        )
        re = lax.dot_general(kern_re.astype(BF16), x, dims, preferred_element_type=F32)
        im = lax.dot_general(kern_im.astype(BF16), x, dims, preferred_element_type=F32)
        return accum + jnp.concatenate([re[:, :half] - im[:, half:], re[:, half:] + im[:, :half]], 1)

    return lax.fori_loop(0, everything.shape[0] // width, far, total)


def on_device(*arguments):
    count = lax.axis_size("row") * lax.axis_size("col")
    short = lax.axis_size("col") == 2 and lax.axis_size("row") <= 16 and count & (count - 1) == 0
    return (exchanged if short and count >= 8 else gathered)(*arguments)


def solution(mesh):
    return jax.shard_map(
        on_device,
        mesh=mesh,
        in_specs=(
            P("groups"),
            P(None, ("groups", "row")),
            P(None, ("groups", "row", "col")),
            P(None, ("groups", "row", "col")),
            P(None, ("groups", "row")),
            P(None, ("groups", "row")),
            P(None, None, ("groups", "row")),
            P(None, None, ("groups", "row", "col")),
            P(("groups", "row"), None),
        ),
        out_specs=P(("groups", "row", "col"), None),
        check_vma=False,
    )
```

```python
import functools
import math

import jax
import jax.numpy as jnp
from jax import lax
from jax.experimental import pallas as pl
from jax.experimental.pallas import tpu as pltpu
from jax.sharding import PartitionSpec as P

QSTEP = 64
QN = 192
LANES = 128
PARTS = 3
SOFT = 0.05
INV_FOUR_PI = 1.0 / (4.0 * math.pi)
INV_TURN = 1.0 / (2.0 * math.pi)
TURN_HIGH = 6.28125
TURN_LOW = 2.0 * math.pi - TURN_HIGH
SIN_HALF = (3.14159264, -5.16771009, 2.55007766, -0.59829216, 0.07765941)
COS_HALF = (1.0, -4.93480214, 4.05870916, -1.33521206, 0.23493756, -0.02439672)
COS_FULL = (
    0.99999999, -19.73920453, 64.93911898, -85.45016555, 60.16783171, -25.96831321, 6.52961029
)
BF16 = jnp.bfloat16
F32 = jnp.float32
NN = (((1,), (0,)), ((), ()))
NT = (((1,), (1,)), ((), ()))
EXC_AT = 2 * QN
NODE_WIDTH = LANES
SMALL = pltpu.CompilerParams(vmem_limit_bytes=24 * 2**20)


def dot(left, right, dims=NN):
    return lax.dot_general(left, right, dims, preferred_element_type=F32)


def polynomial(z, coefficients):
    total = coefficients[-1]
    for c in coefficients[-2::-1]:
        total = total * z + c
    return total


def sincos_turns(f):
    z = f * f
    s = f * polynomial(z, SIN_HALF)
    c = polynomial(z, COS_HALF)
    twice = s + s
    return twice * c, 1.0 - twice * s


def three_parts(x):
    first = x.astype(BF16)
    rest = x - first.astype(F32)
    second = rest.astype(BF16)
    third = (rest - second.astype(F32)).astype(BF16)
    return first, second, third


def two_parts(x):
    first = x.astype(BF16)
    return first, (x - first.astype(F32)).astype(BF16)


def exchange_steps(count):
    bits = [1 << b for b in range(count.bit_length() - 2, 0, -1)]
    swapped = bits[:-2] + bits[-2:][::-1] if len(bits) >= 2 else bits
    return [b | 1 for b in bits], [b | 1 for b in swapped]


def relative_places(steps):
    places = [0]
    for step in steps:
        places = places + [p ^ step for p in places]
    return places


def iota(shape, axis):
    return lax.broadcasted_iota(jnp.int32, shape, axis)


def geom_lane(cpd):
    return 3 * PARTS * (QN // cpd)


def place_matrices(cpd):
    groups = QN // cpd
    shape = (LANES, 2 * 16)
    begin, row = iota(shape, 0), iota(shape, 1)
    node = jnp.logical_and(begin >= row * groups, begin < (row + 1) * groups)
    node = jnp.logical_and(node, row < 3 * PARTS)
    source = jnp.logical_and(begin - geom_lane(cpd) == row - 16, row >= 16)
    row_of = jnp.where(jnp.logical_or(node, source), 1.0, 0.0).astype(BF16)
    shape = (LANES, QN)
    lane, group = iota(shape, 0), lax.div(iota(shape, 1), cpd)
    wanted = jnp.where(lane < geom_lane(cpd), lax.rem(lane, groups), 0)
    kept = jnp.where(group == wanted, 1.0, 0.0)
    shape = (cpd, QN)
    column_of = jnp.where(lax.rem(iota(shape, 1), cpd) == iota(shape, 0), 1.0, 0.0).astype(BF16)
    return row_of, kept, column_of


def pack_kernel(
    units, order_hbm, geom_hbm, excite_hbm, nodes_hbm, weights_hbm, tnodes_hbm, tweights_hbm,
    out_ref, target_ref, tests_ref, found_ref,
    order_ref, geom_ref, excite_ref, nodes_ref, weights_ref, tnodes_ref, arrived,
):
    col = lax.axis_index("col")
    rows = tests_ref.shape[2]
    at = pl.ds(pl.multiple_of(col * rows, LANES), rows)
    moves = [
        (weights_hbm, weights_ref),
        (nodes_hbm, nodes_ref),
        (geom_hbm, geom_ref),
        (excite_hbm, excite_ref),
        (tnodes_hbm, tnodes_ref),
        (order_hbm, order_ref),
        (tweights_hbm.at[:, :, at], tests_ref),
    ]
    copies = [pltpu.make_async_copy(*move, arrived.at[i]) for i, move in enumerate(moves)]
    for copy in copies:
        copy.start()
    cpd, exc = excite_ref.shape
    row_of, kept, column_of = place_matrices(cpd)
    for copy in copies[:-1]:
        copy.wait()
    main = LANES
    rest = QN - main
    re, im = weights_ref[0], weights_ref[1]
    out_ref[:, 0:main] = re[:, :main]
    out_ref[:, main : 2 * main] = im[:, :main]
    out_ref[:, 2 * main : 2 * main + 2 * rest] = jnp.concatenate([re[:, main:], im[:, main:]], 1)
    out_ref[:, EXC_AT : EXC_AT + exc] = excite_ref[...]
    nodes = [p.astype(F32) for p in three_parts(nodes_ref[...])]
    geom = jnp.concatenate([p.astype(F32) for p in three_parts(geom_ref[...])], 0)
    values = jnp.concatenate(
        nodes
        + [
            jnp.zeros((16 - 3 * PARTS, QN), F32),
            jnp.concatenate([geom, jnp.zeros((geom.shape[0], QN - cpd), F32)], 1),
            jnp.zeros((16 - geom.shape[0], QN), F32),
        ],
        0,
    ).astype(BF16)
    spread = (dot(row_of, values) * kept).astype(BF16)
    out_ref[:, EXC_AT + exc :] = dot(column_of, spread, NT).astype(BF16)
    nodes = tnodes_ref[:, :QN]
    for b in range(1, tnodes_ref.shape[1] // QN):
        nodes = jnp.where(col == b, tnodes_ref[:, b * QN : (b + 1) * QN], nodes)
    end = nodes[:, LANES:]
    start = nodes[:, :QSTEP]
    target_ref[0, 0:3] = nodes[:, :LANES]
    target_ref[1, 0:3] = jnp.concatenate([end, end], 1)
    target_ref[2, 0:3] = jnp.concatenate([start, start], 1)
    for slot, order in enumerate(slot_orders(order_ref, units)):
        found_ref[slot] = order
    copies[-1].wait()


def store_tests(tests_ref, ut_ref):
    re, im = tests_ref[0], tests_ref[1]
    main = LANES
    ut_ref[0:main, :] = jnp.concatenate([re[:main], im[:main]], 1)
    ut_ref[main : 2 * main, :] = jnp.concatenate([-im[:main], re[:main]], 1)
    ut_ref[2 * main : 2 * main + QSTEP, :] = jnp.concatenate([re[main:], im[main:]], 1)
    ut_ref[2 * main + QSTEP :, :] = jnp.concatenate([-im[main:], re[main:]], 1)


def node_columns(data_ref, exc):
    block = data_ref[:, EXC_AT + exc :].astype(F32)
    step = geom_lane(16) // PARTS
    return (block[:, :step] + block[:, step : 2 * step]) + block[:, 2 * step : 3 * step]


def two_part_dot(high, low, right):
    count = high.shape[0]
    both = dot(jnp.concatenate([high, low], 0), right)
    return both[:count] + both[count:]


def near_slot(order, columns, slot, target_ref, ut_ref, turns, out_ref):
    lane = lax.broadcasted_iota(jnp.int32, (1, LANES), 1)
    quarter = jnp.where(lane < QSTEP, 0.0, 0.25)
    main = LANES

    def located(count):
        return [
            jnp.concatenate(
                [
                    jnp.broadcast_to(columns[16 * slot : 16 * slot + 16, lane : lane + 1], (16, LANES))
                    for lane in range(axis * (QN // 16), axis * (QN // 16) + count // 16)
                ],
                0,
            )
            for axis in range(3)
        ]

    def distance2(source, tile):
        total = SOFT * SOFT
        for axis in range(3):
            d = source[axis] - target_ref[tile, axis : axis + 1, :]
            total = total + d * d
        return total

    def both(source):
        d2 = distance2(source, 0)
        inv = lax.rsqrt(d2)
        t = (d2 * inv) * turns
        sin, cos = sincos_turns(t - jnp.round(t))
        return two_parts(inv * cos), two_parts(inv * sin)

    def split_lanes(source, tile):
        d2 = distance2(source, tile)
        inv = lax.rsqrt(d2)
        t = (d2 * inv) * turns
        f = (t - jnp.round(t - quarter)) - quarter
        return two_parts(inv * polynomial(f * f, COS_FULL))

    def put(at, value):
        high, low = two_parts(value)
        count = value.shape[0]
        out_ref[at : at + count, :LANES] = high
        out_ref[at : at + count, LANES:] = low

    def clear(begin, end):
        out_ref[begin:end, :] = jnp.zeros((end - begin, 2 * LANES), BF16)

    @pl.when(order == 3)
    def _():
        source = located(QN)
        (re_high, re_low), (im_high, im_low) = both(source)
        rest_high, rest_low = split_lanes(source, 1)
        high = jnp.concatenate([re_high, im_high, rest_high], 1)
        low = jnp.concatenate([re_low, im_low, rest_low], 1)
        v = two_part_dot(high, low, ut_ref[...])
        put(0, v[:main, :LANES])
        put(main, v[:main, LANES:])
        put(2 * main, v[main:, :LANES])
        put(2 * main + QSTEP, v[main:, LANES:])

    @pl.when(order == 2)
    def _():
        (re_high, re_low), (im_high, im_low) = both(located(main))
        high = jnp.concatenate([re_high, im_high], 1)
        low = jnp.concatenate([re_low, im_low], 1)
        v = two_part_dot(high, low, ut_ref[: 2 * main])
        put(0, v[:, :LANES])
        put(main, v[:, LANES:])
        clear(2 * main, 3 * main)

    @pl.when(order == 1)
    def _():
        high, low = split_lanes(located(QSTEP), 2)
        weights = jnp.concatenate([ut_ref[0:QSTEP], ut_ref[main : main + QSTEP]], 0)
        v = two_part_dot(high, low, weights)
        put(0, v[:, :LANES])
        clear(QSTEP, main)
        put(main, v[:, LANES:])
        clear(main + QSTEP, 3 * main)

    @pl.when(order == 0)
    def _():
        clear(0, 3 * main)


def slot_orders(order_ref, units):
    row, col = lax.axis_index("row"), lax.axis_index("col")
    nrow = lax.axis_size("row")
    band = order_ref.shape[1]
    reach = (band - 1) // 2
    if units is None:
        offsets = [jnp.where(jnp.logical_and(row + o >= reach, row + o - reach < nrow), o, -1) for o in range(band)]
    else:
        place, parity = row * lax.axis_size("col") + col, 0
        for _ in range((nrow * lax.axis_size("col")).bit_length() - 1):
            parity = parity + lax.rem(place, 2)
            place = lax.div(place, 2)
        parity = lax.rem(parity, 2)
        offsets = [
            (row ^ (a if a == b else jnp.where(parity == 0, a, b))) - row + reach for a, b in zip(*units)
        ]
    return [
        jnp.where(
            jnp.logical_and(o >= 0, o < band), order_ref[col, jnp.clip(o, 0, band - 1)], 0
        )
        for o in offsets
    ]


def far_kernel_values(wave, source, tgeom):
    dx = tgeom[0:1] - source[0]
    dy = tgeom[1:2] - source[1]
    dz = tgeom[2:3] - source[2]
    d2 = dx * dx + dy * dy + dz * dz + SOFT * SOFT
    inv = lax.rsqrt(d2)
    radius = d2 * inv
    cosine = (tgeom[3:4] * dx + tgeom[4:5] * dy + tgeom[5:6] * dz) * inv
    scale = source[3] * (INV_FOUR_PI * inv)
    phase = wave * radius
    t = phase * INV_TURN
    n = jnp.round(t)
    sin, cos = sincos_turns(((phase - n * TURN_HIGH) - n * TURN_LOW) * INV_TURN)
    green_re = scale * cos
    green_im = scale * sin
    factor_re = 1.0 - cosine
    factor_im = cosine * (inv * (-1.0 / wave))
    kern_re = (green_re * factor_re - green_im * factor_im).astype(BF16)
    kern_im = (green_re * factor_im + green_im * factor_re).astype(BF16)
    return kern_re, kern_im


def far_rows(data, exc, wave, tgeom):
    shape = (LANES, 4 * LANES)
    at, wanted = iota(shape, 0) - geom_lane(16), lax.div(iota(shape, 1), LANES)
    pick = jnp.logical_and(
        jnp.logical_and(at >= 0, at < 4 * PARTS), lax.rem(at + 4 * LANES, 4) == wanted
    )
    geom = data[:, EXC_AT + exc :]
    spread = dot(geom, jnp.where(pick, 1.0, 0.0).astype(BF16))
    return far_kernel_values(wave, [spread[:, i * LANES : (i + 1) * LANES] for i in range(4)], tgeom)


def own_targets(tgeom_ref, rows):
    at = pl.multiple_of(lax.axis_index("col") * rows, LANES)
    return tgeom_ref[:, pl.ds(at, rows)]


def near_kernel(
    exc, first, wave_ref, found_ref, data_ref, own_ref, target_ref, ut_ref, tgeom_ref,
    v_ref, kern_re_ref, kern_im_ref, *copy_ref,
):
    if copy_ref:
        copy_ref[0][...] = own_ref[...]
    wave = wave_ref[0]
    tgeom = own_targets(tgeom_ref, kern_re_ref.shape[1])
    kern_re_ref[...], kern_im_ref[...] = far_rows(data_ref, exc, wave, tgeom)
    slots = v_ref.shape[0]
    columns = node_columns(data_ref, exc)
    for slot in range(slots):
        near_slot(found_ref[first + slot], columns, slot, target_ref, ut_ref, wave * INV_TURN, v_ref.at[slot])


def first_near_kernel(
    exc, first, wave_ref, found_ref, data_ref, own_ref, target_ref, tests_ref, tgeom_ref, *refs
):
    *refs, ut_ref = refs
    store_tests(tests_ref, ut_ref)
    near_kernel(exc, first, wave_ref, found_ref, data_ref, own_ref, target_ref, ut_ref, tgeom_ref, *refs)


def last_kernel(exc, partner, wave_ref, own_early, own_late, other_early, other_late, tgeom_ref, *refs):
    own = jnp.concatenate([own_early[...], own_late[...]], 0)
    other = jnp.concatenate([other_early[...], other_late[...]], 0)
    out_ref, zre, zim = refs[-3:]
    v_refs, kern_re_refs, kern_im_refs = refs[:-3:3], refs[1:-3:3], refs[2:-3:3]
    rows = out_ref.shape[0]
    cpd = 16
    main = LANES
    slots = len(partner)
    sign = jnp.where(lax.broadcasted_iota(jnp.int32, (1, LANES), 1) < QSTEP, 1.0, -1.0).astype(BF16)

    def weight_rows(data):
        w = [data[:, i * main : (i + 1) * main] for i in range(3)]
        swapped = jnp.concatenate([w[2][:, QSTEP:], w[2][:, :QSTEP]], 1)
        return jnp.concatenate([w[0], -w[1], w[2] * sign], 1), jnp.concatenate([w[1], w[0], swapped], 1)

    own_re, own_im = weight_rows(own)
    other_re, other_im = weight_rows(other)
    slot = 0
    for v_ref in v_refs:
        for i in range(v_ref.shape[0]):
            here = slice(slot * cpd, (slot + 1) * cpd)
            there = slice(partner[slot] * cpd, (partner[slot] + 1) * cpd)
            left = jnp.concatenate([own_re[here], other_re[there], own_im[here], other_im[there]], 0)
            product = dot(left, v_ref[i])
            a = (product[:, :LANES] + product[:, LANES:]) * INV_FOUR_PI
            there = slice((slots + partner[slot]) * cpd, (slots + partner[slot] + 1) * cpd)
            zre[here] = a[0:cpd]
            zre[there] = a[cpd : 2 * cpd]
            zim[here] = a[2 * cpd : 3 * cpd]
            zim[there] = a[3 * cpd :]
            slot += 1

    other_kern = far_rows(other, exc, wave_ref[0], own_targets(tgeom_ref, rows))
    kern_re, kern_im = [
        jnp.concatenate([ref[...] for ref in refs] + [last], 0).astype(F32)
        for refs, last in zip((kern_re_refs, kern_im_refs), other_kern)
    ]
    excite = jnp.concatenate(
        [own[:, EXC_AT : EXC_AT + exc], other[:, EXC_AT : EXC_AT + exc]], 0
    ).T
    re = two_parts(kern_re + zre[...])
    im = two_parts(kern_im + zim[...])
    product = dot(excite, jnp.concatenate([*re, *im], 1))
    by_re = product[:, :rows] + product[:, rows : 2 * rows]
    by_im = product[:, 2 * rows : 3 * rows] + product[:, 3 * rows :]
    h = exc // 2
    result = jnp.concatenate([by_re[:h] - by_im[h:], by_re[h:] + by_im[:h]], 0)
    out_ref[...] = result.T


def in_vmem(x):
    return pltpu.with_memory_space_constraint(x, pltpu.VMEM)


def in_smem(x):
    return pltpu.with_memory_space_constraint(x, pltpu.SMEM)


def in_hbm(x):
    return pltpu.with_memory_space_constraint(x, pltpu.HBM)


SMEM_SPEC = pl.BlockSpec(memory_space=pltpu.SMEM)
VMEM_SPEC = pl.BlockSpec(memory_space=pltpu.VMEM)


def packed(units, slots, src_geom, excite, src_nodes, src_weights, tgt_nodes, tgt_weights, near_order):
    excite = excite.T
    src_weights = src_weights.transpose(0, 2, 1)
    cpd, exc = excite.shape
    rows_here = tgt_weights.shape[2] // lax.axis_size("col")
    inputs = (near_order, src_geom, excite, src_nodes, src_weights, tgt_nodes)
    return pl.pallas_call(
        functools.partial(pack_kernel, units),
        out_shape=[
            pltpu.VMEM((cpd, EXC_AT + exc + NODE_WIDTH), BF16),
            pltpu.VMEM((3, 8, LANES), F32),
            pltpu.VMEM((2, QN, rows_here), BF16),
            pltpu.SMEM((slots,), jnp.int32),
        ],
        in_specs=[pl.BlockSpec(memory_space=pl.ANY)] * 7,
        out_specs=[VMEM_SPEC] * 3 + [SMEM_SPEC],
        scratch_shapes=[pltpu.SMEM(near_order.shape, jnp.int32)]
        + [pltpu.VMEM(x.shape, x.dtype) for x in inputs[1:]]
        + [pltpu.SemaphoreType.DMA((7,))],
        compiler_params=SMALL,
    )(*[in_hbm(x) for x in inputs], in_hbm(tgt_weights))


def near_blocks(exc, first, slots, wavenumber, found, fresh, own, target, ut, tgt_geom, hand_on):
    rows_here = tgt_geom.shape[1] // lax.axis_size("col")
    kern = pltpu.VMEM((fresh.shape[0], rows_here), BF16)
    cost = pl.CostEstimate(flops=slots * 10**8, bytes_accessed=10**6, transcendentals=slots * 36864)
    outs = [pltpu.VMEM((slots, 2 * QN, 2 * LANES), BF16), kern, kern] + [pltpu.VMEM(own.shape, BF16)] * hand_on
    if first == 0:
        outs.append(pltpu.VMEM((2 * QN, 2 * LANES), BF16))
    return pl.pallas_call(
        functools.partial(near_kernel if first else first_near_kernel, exc, first),
        out_shape=outs,
        in_specs=[SMEM_SPEC] * 2 + [VMEM_SPEC] * 5,
        out_specs=[VMEM_SPEC] * len(outs),
        compiler_params=SMALL,
        cost_estimate=cost,
    )(wavenumber, in_smem(found), in_vmem(fresh), in_vmem(own), in_vmem(target), in_vmem(ut), in_vmem(tgt_geom))


def exchanged(
    wavenumber, tgt_geom, src_geom, excite, tgt_nodes, src_nodes, tgt_weights, src_weights, near_order
):
    cpd = src_geom.shape[1]
    exc = excite.shape[0]
    cores = lax.axis_size("col")
    count = cores * lax.axis_size("row")
    rows_here = tgt_geom.shape[1] // cores
    even, odd = exchange_steps(count)
    units = [[p >> 1 for p in relative_places(s)] for s in (even, odd)]
    own, target, ut, found = packed(
        units, len(units[0]), src_geom, excite, src_nodes, src_weights, tgt_nodes, tgt_weights, near_order
    )

    def moved(value, a, b):
        pairs = [(i, i ^ (b if bin(i).count("1") % 2 else a)) for i in range(count)]
        return lax.ppermute(value, ("row", "col"), pairs)

    fresh = own
    near = []
    done = 0
    steps = list(zip(even, odd))
    for step, (a, b) in enumerate(steps):
        arriving = moved(own, a, b)
        slots = fresh.shape[0] // cpd
        made = near_blocks(exc, done, slots, wavenumber, found, fresh, own, target, ut, tgt_geom, True)
        near.extend(made[:3])
        if not done:
            ut = made[4]
        done += slots
        fresh = arriving
        if step < len(steps) - 1:
            own = jnp.concatenate([made[3], arriving], 0)
    other_early = moved(made[3], 1, 1)
    other_late = moved(fresh, 1, 1)
    near.extend(near_blocks(exc, done, done, wavenumber, found, fresh, fresh, target, ut, tgt_geom, False))
    partner = [units[1].index(u) for u in units[0]]
    return pl.pallas_call(
        functools.partial(last_kernel, exc, partner),
        out_shape=jax.ShapeDtypeStruct((rows_here, exc), F32),
        in_specs=[SMEM_SPEC] + [VMEM_SPEC] * (5 + len(near)),
        out_specs=VMEM_SPEC,
        scratch_shapes=[pltpu.VMEM((count * cpd, rows_here), F32)] * 2,
        compiler_params=SMALL,
    )(
        wavenumber,
        *[in_vmem(x) for x in (made[3], fresh, other_early, other_late, tgt_geom)],
        *[in_vmem(v) for v in near],
    )


def gathered(
    wavenumber, tgt_geom, src_geom, excite, tgt_nodes, src_nodes, tgt_weights, src_weights, near_order
):
    cpd = src_geom.shape[1]
    exc = excite.shape[0]
    half = exc // 2
    cores = lax.axis_size("col")
    nrow = lax.axis_size("row")
    row = lax.axis_index("row")
    rows_here = tgt_geom.shape[1] // cores
    band = near_order.shape[1]
    own, target, ut, found = packed(
        None, band, src_geom, excite, src_nodes, src_weights, tgt_nodes, tgt_weights, near_order
    )
    everything = lax.all_gather(own, ("row", "col"), axis=0, tiled=True)
    sources = lax.all_gather(src_geom, ("row", "col"), axis=1, tiled=True)
    blocks = [
        lax.dynamic_slice_in_dim(
            everything, jnp.clip(row + o - (band - 1) // 2, 0, nrow - 1) * cores * cpd, cores * cpd, 0
        )
        for o in range(band)
    ]
    fresh = jnp.concatenate([block[:cpd] for block in blocks], 0)
    near = near_blocks(exc, 0, band, wavenumber, found, fresh, own, target, ut, tgt_geom, False)[0]
    high = lax.Precision.HIGHEST
    total = jnp.zeros((rows_here, exc), F32)
    dims = (((0,), (0,)), ((), ()))
    m, r = LANES, QN - LANES
    for o, block in enumerate(blocks):
        w, x = block[:, :EXC_AT].astype(F32), block[:, EXC_AT : EXC_AT + exc].astype(F32)
        v = near[o, :, :LANES].astype(F32) + near[o, :, LANES:].astype(F32)
        w_re = jnp.concatenate([w[:, :m], w[:, 2 * m : 2 * m + r]], 1)
        w_im = jnp.concatenate([w[:, m : 2 * m], w[:, 2 * m + r :]], 1)
        v_re = jnp.concatenate([v[:m], v[2 * m : 2 * m + r]], 0)
        v_im = jnp.concatenate([v[m : 2 * m], v[2 * m + r :]], 0)
        a_re = jnp.dot(w_re, v_re, precision=high) - jnp.dot(w_im, v_im, precision=high)
        a_im = jnp.dot(w_re, v_im, precision=high) + jnp.dot(w_im, v_re, precision=high)
        re = lax.dot_general(a_re, x, dims, precision=high)
        im = lax.dot_general(a_im, x, dims, precision=high)
        total = total + INV_FOUR_PI * jnp.concatenate(
            [re[:, :half] - im[:, half:], re[:, half:] + im[:, :half]], 1
        )
    targets = lax.dynamic_slice_in_dim(tgt_geom, lax.axis_index("col") * rows_here, rows_here, 1)
    width = math.gcd(everything.shape[0], 512)

    def far(index, accum):
        places = lax.dynamic_slice_in_dim(sources, index * width, width, 1)
        x = lax.dynamic_slice_in_dim(everything, index * width, width, 0)[:, EXC_AT : EXC_AT + exc]
        kern_re, kern_im = far_kernel_values(
            wavenumber[0], [places[i][:, None] for i in range(4)], targets
        )
        re = lax.dot_general(kern_re.astype(BF16), x, dims, preferred_element_type=F32)
        im = lax.dot_general(kern_im.astype(BF16), x, dims, preferred_element_type=F32)
        return accum + jnp.concatenate([re[:, :half] - im[:, half:], re[:, half:] + im[:, :half]], 1)

    return lax.fori_loop(0, everything.shape[0] // width, far, total)


def on_device(*arguments):
    count = lax.axis_size("row") * lax.axis_size("col")
    short = lax.axis_size("col") == 2 and lax.axis_size("row") <= 16 and count & (count - 1) == 0
    return (exchanged if short and count >= 8 else gathered)(*arguments)


def solution(mesh):
    return jax.shard_map(
        on_device,
        mesh=mesh,
        in_specs=(
            P("groups"),
            P(None, ("groups", "row")),
            P(None, ("groups", "row", "col")),
            P(None, ("groups", "row", "col")),
            P(None, ("groups", "row")),
            P(None, ("groups", "row")),
            P(None, None, ("groups", "row")),
            P(None, None, ("groups", "row", "col")),
            P(("groups", "row"), None),
        ),
        out_specs=P(("groups", "row", "col"), None),
        check_vma=False,
    )
```

```python
import functools
import math

import jax
import jax.numpy as jnp
from jax import lax
from jax.experimental import pallas as pl
from jax.experimental.pallas import tpu as pltpu
from jax.sharding import PartitionSpec as P

QSTEP = 64
QN = 192
LANES = 128
PARTS = 3
SOFT = 0.05
INV_FOUR_PI = 1.0 / (4.0 * math.pi)
INV_TURN = 1.0 / (2.0 * math.pi)
TURN_HIGH = 6.28125
TURN_LOW = 2.0 * math.pi - TURN_HIGH
SIN_HALF = (3.14159264, -5.16771009, 2.55007766, -0.59829216, 0.07765941)
COS_HALF = (1.0, -4.93480214, 4.05870916, -1.33521206, 0.23493756, -0.02439672)
COS_FULL = (
    0.99999999, -19.73920453, 64.93911898, -85.45016555, 60.16783171, -25.96831321, 6.52961029
)
BF16 = jnp.bfloat16
F32 = jnp.float32
NN = (((1,), (0,)), ((), ()))
NT = (((1,), (1,)), ((), ()))
EXC_AT = 2 * QN
NODE_WIDTH = LANES
SMALL = pltpu.CompilerParams(vmem_limit_bytes=24 * 2**20)


def dot(left, right, dims=NN):
    return lax.dot_general(left, right, dims, preferred_element_type=F32)


def polynomial(z, coefficients):
    total = coefficients[-1]
    for c in coefficients[-2::-1]:
        total = total * z + c
    return total


def sincos_turns(f):
    z = f * f
    s = f * polynomial(z, SIN_HALF)
    c = polynomial(z, COS_HALF)
    twice = s + s
    return twice * c, 1.0 - twice * s


def three_parts(x):
    first = x.astype(BF16)
    rest = x - first.astype(F32)
    second = rest.astype(BF16)
    third = (rest - second.astype(F32)).astype(BF16)
    return first, second, third


def two_parts(x):
    first = x.astype(BF16)
    return first, (x - first.astype(F32)).astype(BF16)


def exchange_steps(count):
    bits = [1 << b for b in range(count.bit_length() - 2, 0, -1)]
    swapped = bits[:-2] + bits[-2:][::-1] if len(bits) >= 2 else bits
    return [b | 1 for b in bits], [b | 1 for b in swapped]


def relative_places(steps):
    places = [0]
    for step in steps:
        places = places + [p ^ step for p in places]
    return places


def iota(shape, axis):
    return lax.broadcasted_iota(jnp.int32, shape, axis)


def geom_lane(cpd):
    return 3 * PARTS * (QN // cpd)


def place_matrices(cpd):
    groups = QN // cpd
    shape = (LANES, 2 * 16)
    begin, row = iota(shape, 0), iota(shape, 1)
    node = jnp.logical_and(begin >= row * groups, begin < (row + 1) * groups)
    node = jnp.logical_and(node, row < 3 * PARTS)
    source = jnp.logical_and(begin - geom_lane(cpd) == row - 16, row >= 16)
    row_of = jnp.where(jnp.logical_or(node, source), 1.0, 0.0).astype(BF16)
    shape = (LANES, QN)
    lane, group = iota(shape, 0), lax.div(iota(shape, 1), cpd)
    wanted = jnp.where(lane < geom_lane(cpd), lax.rem(lane, groups), 0)
    kept = jnp.where(group == wanted, 1.0, 0.0)
    shape = (cpd, QN)
    column_of = jnp.where(lax.rem(iota(shape, 1), cpd) == iota(shape, 0), 1.0, 0.0).astype(BF16)
    return row_of, kept, column_of


def pack_kernel(
    units, order_hbm, geom_hbm, excite_hbm, nodes_hbm, weights_hbm, tnodes_hbm, tweights_hbm,
    out_ref, target_ref, tests_ref, found_ref,
    order_ref, geom_ref, excite_ref, nodes_ref, weights_ref, tnodes_ref, arrived,
):
    col = lax.axis_index("col")
    rows = tests_ref.shape[2]
    at = pl.ds(pl.multiple_of(col * rows, LANES), rows)
    moves = [
        (weights_hbm, weights_ref),
        (nodes_hbm, nodes_ref),
        (geom_hbm, geom_ref),
        (excite_hbm, excite_ref),
        (tnodes_hbm, tnodes_ref),
        (order_hbm, order_ref),
        (tweights_hbm.at[:, :, at], tests_ref),
    ]
    copies = [pltpu.make_async_copy(*move, arrived.at[i]) for i, move in enumerate(moves)]
    for copy in copies:
        copy.start()
    cpd, exc = excite_ref.shape
    row_of, kept, column_of = place_matrices(cpd)
    for copy in copies[:-1]:
        copy.wait()
    main = LANES
    rest = QN - main
    re, im = weights_ref[0], weights_ref[1]
    out_ref[:, 0:main] = re[:, :main]
    out_ref[:, main : 2 * main] = im[:, :main]
    out_ref[:, 2 * main : 2 * main + 2 * rest] = jnp.concatenate([re[:, main:], im[:, main:]], 1)
    out_ref[:, EXC_AT : EXC_AT + exc] = excite_ref[...]
    nodes = [p.astype(F32) for p in three_parts(nodes_ref[...])]
    geom = jnp.concatenate([p.astype(F32) for p in three_parts(geom_ref[...])], 0)
    values = jnp.concatenate(
        nodes
        + [
            jnp.zeros((16 - 3 * PARTS, QN), F32),
            jnp.concatenate([geom, jnp.zeros((geom.shape[0], QN - cpd), F32)], 1),
            jnp.zeros((16 - geom.shape[0], QN), F32),
        ],
        0,
    ).astype(BF16)
    spread = (dot(row_of, values) * kept).astype(BF16)
    out_ref[:, EXC_AT + exc :] = dot(column_of, spread, NT).astype(BF16)
    nodes = tnodes_ref[:, :QN]
    for b in range(1, tnodes_ref.shape[1] // QN):
        nodes = jnp.where(col == b, tnodes_ref[:, b * QN : (b + 1) * QN], nodes)
    end = nodes[:, LANES:]
    start = nodes[:, :QSTEP]
    target_ref[0, 0:3] = nodes[:, :LANES]
    target_ref[1, 0:3] = jnp.concatenate([end, end], 1)
    target_ref[2, 0:3] = jnp.concatenate([start, start], 1)
    for slot, order in enumerate(slot_orders(order_ref, units)):
        found_ref[slot] = order
    copies[-1].wait()


def store_tests(tests_ref, ut_ref):
    re, im = tests_ref[0], tests_ref[1]
    main = LANES
    ut_ref[0:main, :] = jnp.concatenate([re[:main], im[:main]], 1)
    ut_ref[main : 2 * main, :] = jnp.concatenate([-im[:main], re[:main]], 1)
    ut_ref[2 * main : 2 * main + QSTEP, :] = jnp.concatenate([re[main:], im[main:]], 1)
    ut_ref[2 * main + QSTEP :, :] = jnp.concatenate([-im[main:], re[main:]], 1)


def node_columns(data_ref, exc):
    block = data_ref[:, EXC_AT + exc :].astype(F32)
    step = geom_lane(16) // PARTS
    return (block[:, :step] + block[:, step : 2 * step]) + block[:, 2 * step : 3 * step]


def two_part_dot(high, low, right):
    count = high.shape[0]
    both = dot(jnp.concatenate([high, low], 0), right)
    return both[:count] + both[count:]


def near_slot(order, columns, slot, target_ref, ut_ref, turns, out_ref):
    lane = lax.broadcasted_iota(jnp.int32, (1, LANES), 1)
    quarter = jnp.where(lane < QSTEP, 0.0, 0.25)
    main = LANES

    def located(count):
        return [
            jnp.concatenate(
                [
                    jnp.broadcast_to(columns[16 * slot : 16 * slot + 16, lane : lane + 1], (16, LANES))
                    for lane in range(axis * (QN // 16), axis * (QN // 16) + count // 16)
                ],
                0,
            )
            for axis in range(3)
        ]

    def distance2(source, tile):
        total = SOFT * SOFT
        for axis in range(3):
            d = source[axis] - target_ref[tile, axis : axis + 1, :]
            total = total + d * d
        return total

    def both(source):
        d2 = distance2(source, 0)
        inv = lax.rsqrt(d2)
        t = (d2 * inv) * turns
        sin, cos = sincos_turns(t - jnp.round(t))
        return two_parts(inv * cos), two_parts(inv * sin)

    def split_lanes(source, tile):
        d2 = distance2(source, tile)
        inv = lax.rsqrt(d2)
        t = (d2 * inv) * turns
        f = (t - jnp.round(t - quarter)) - quarter
        return two_parts(inv * polynomial(f * f, COS_FULL))

    def put(at, value):
        high, low = two_parts(value)
        count = value.shape[0]
        out_ref[at : at + count, :LANES] = high
        out_ref[at : at + count, LANES:] = low

    def clear(begin, end):
        out_ref[begin:end, :] = jnp.zeros((end - begin, 2 * LANES), BF16)

    @pl.when(order == 3)
    def _():
        source = located(QN)
        (re_high, re_low), (im_high, im_low) = both(source)
        rest_high, rest_low = split_lanes(source, 1)
        high = jnp.concatenate([re_high, im_high, rest_high], 1)
        low = jnp.concatenate([re_low, im_low, rest_low], 1)
        v = two_part_dot(high, low, ut_ref[...])
        put(0, v[:main, :LANES])
        put(main, v[:main, LANES:])
        put(2 * main, v[main:, :LANES])
        put(2 * main + QSTEP, v[main:, LANES:])

    @pl.when(order == 2)
    def _():
        (re_high, re_low), (im_high, im_low) = both(located(main))
        high = jnp.concatenate([re_high, im_high], 1)
        low = jnp.concatenate([re_low, im_low], 1)
        v = two_part_dot(high, low, ut_ref[: 2 * main])
        put(0, v[:, :LANES])
        put(main, v[:, LANES:])
        clear(2 * main, 3 * main)

    @pl.when(order == 1)
    def _():
        high, low = split_lanes(located(QSTEP), 2)
        weights = jnp.concatenate([ut_ref[0:QSTEP], ut_ref[main : main + QSTEP]], 0)
        v = two_part_dot(high, low, weights)
        put(0, v[:, :LANES])
        clear(QSTEP, main)
        put(main, v[:, LANES:])
        clear(main + QSTEP, 3 * main)

    @pl.when(order == 0)
    def _():
        clear(0, 3 * main)


def slot_orders(order_ref, units):
    row, col = lax.axis_index("row"), lax.axis_index("col")
    nrow = lax.axis_size("row")
    band = order_ref.shape[1]
    reach = (band - 1) // 2
    if units is None:
        offsets = [jnp.where(jnp.logical_and(row + o >= reach, row + o - reach < nrow), o, -1) for o in range(band)]
    else:
        place, parity = row * lax.axis_size("col") + col, 0
        for _ in range((nrow * lax.axis_size("col")).bit_length() - 1):
            parity = parity + lax.rem(place, 2)
            place = lax.div(place, 2)
        parity = lax.rem(parity, 2)
        offsets = [
            (row ^ (a if a == b else jnp.where(parity == 0, a, b))) - row + reach for a, b in zip(*units)
        ]
    return [
        jnp.where(
            jnp.logical_and(o >= 0, o < band), order_ref[col, jnp.clip(o, 0, band - 1)], 0
        )
        for o in offsets
    ]


def far_kernel_values(wave, source, tgeom):
    dx = tgeom[0:1] - source[0]
    dy = tgeom[1:2] - source[1]
    dz = tgeom[2:3] - source[2]
    d2 = dx * dx + dy * dy + dz * dz + SOFT * SOFT
    inv = lax.rsqrt(d2)
    radius = d2 * inv
    cosine = (tgeom[3:4] * dx + tgeom[4:5] * dy + tgeom[5:6] * dz) * inv
    scale = source[3] * (INV_FOUR_PI * inv)
    phase = wave * radius
    t = phase * INV_TURN
    n = jnp.round(t)
    sin, cos = sincos_turns(((phase - n * TURN_HIGH) - n * TURN_LOW) * INV_TURN)
    green_re = scale * cos
    green_im = scale * sin
    factor_re = 1.0 - cosine
    factor_im = cosine * (inv * (-1.0 / wave))
    kern_re = (green_re * factor_re - green_im * factor_im).astype(BF16)
    kern_im = (green_re * factor_im + green_im * factor_re).astype(BF16)
    return kern_re, kern_im


def far_rows(data, exc, wave, tgeom):
    shape = (LANES, 4 * LANES)
    at, wanted = iota(shape, 0) - geom_lane(16), lax.div(iota(shape, 1), LANES)
    pick = jnp.logical_and(
        jnp.logical_and(at >= 0, at < 4 * PARTS), lax.rem(at + 4 * LANES, 4) == wanted
    )
    geom = data[:, EXC_AT + exc :]
    spread = dot(geom, jnp.where(pick, 1.0, 0.0).astype(BF16))
    return far_kernel_values(wave, [spread[:, i * LANES : (i + 1) * LANES] for i in range(4)], tgeom)


def own_targets(tgeom_ref, rows):
    at = pl.multiple_of(lax.axis_index("col") * rows, LANES)
    return tgeom_ref[:, pl.ds(at, rows)]


def near_kernel(
    exc, first, wave_ref, found_ref, data_ref, own_ref, target_ref, ut_ref, tgeom_ref,
    v_ref, kern_re_ref, kern_im_ref, *copy_ref,
):
    if copy_ref:
        copy_ref[0][...] = own_ref[...]
    wave = wave_ref[0]
    tgeom = own_targets(tgeom_ref, kern_re_ref.shape[1])
    data = data_ref[...]
    if kern_re_ref.shape[0] > data.shape[0]:
        data = jnp.concatenate([own_ref[...], data], 0)
    kern_re_ref[...], kern_im_ref[...] = far_rows(data, exc, wave, tgeom)
    slots = v_ref.shape[0]
    skipped = data_ref.shape[0] // 16 - slots
    columns = node_columns(data_ref, exc)
    for slot in range(slots):
        near_slot(
            found_ref[first + slot], columns, skipped + slot, target_ref, ut_ref, wave * INV_TURN, v_ref.at[slot]
        )


def first_near_kernel(
    exc, first, wave_ref, found_ref, data_ref, own_ref, target_ref, tests_ref, tgeom_ref, *refs
):
    *refs, ut_ref = refs
    store_tests(tests_ref, ut_ref)
    near_kernel(exc, first, wave_ref, found_ref, data_ref, own_ref, target_ref, ut_ref, tgeom_ref, *refs)


def last_kernel(
    exc, partner, wave_ref, own_early, own_late, other_first, other_early, other_late, tgeom_ref,
    early_re_ref, early_im_ref, *refs
):
    own = jnp.concatenate([own_early[...], own_late[...]], 0)
    other = jnp.concatenate([other_first[...], other_early[...], other_late[...]], 0)
    out_ref, zre, zim = refs[-3:]
    *made, early_v, late_v, late_re, late_im = refs[:-3]
    v_refs = [*made[::3], early_v, late_v]
    kern_re_refs, kern_im_refs = [*made[1::3], late_re], [*made[2::3], late_im]
    rows = out_ref.shape[0]
    cpd = 16
    main = LANES
    slots = len(partner)
    sign = jnp.where(lax.broadcasted_iota(jnp.int32, (1, LANES), 1) < QSTEP, 1.0, -1.0).astype(BF16)

    def weight_rows(data):
        w = [data[:, i * main : (i + 1) * main] for i in range(3)]
        swapped = jnp.concatenate([w[2][:, QSTEP:], w[2][:, :QSTEP]], 1)
        return jnp.concatenate([w[0], -w[1], w[2] * sign], 1), jnp.concatenate([w[1], w[0], swapped], 1)

    own_re, own_im = weight_rows(own)
    other_re, other_im = weight_rows(other)
    slot = 0
    for v_ref in v_refs:
        for i in range(v_ref.shape[0]):
            here = slice(slot * cpd, (slot + 1) * cpd)
            there = slice(partner[slot] * cpd, (partner[slot] + 1) * cpd)
            left = jnp.concatenate([own_re[here], other_re[there], own_im[here], other_im[there]], 0)
            product = dot(left, v_ref[i])
            a = (product[:, :LANES] + product[:, LANES:]) * INV_FOUR_PI
            there = slice((slots + partner[slot]) * cpd, (slots + partner[slot] + 1) * cpd)
            zre[here] = a[0:cpd]
            zre[there] = a[cpd : 2 * cpd]
            zim[here] = a[2 * cpd : 3 * cpd]
            zim[there] = a[3 * cpd :]
            slot += 1

    late_kern = far_rows(other_late, exc, wave_ref[0], own_targets(tgeom_ref, rows))
    other_kern = [
        jnp.concatenate([early[...], x], 0)
        for x, early in zip(late_kern, (early_re_ref, early_im_ref))
    ]
    kern_re, kern_im = [
        jnp.concatenate([ref[...] for ref in refs] + [last], 0).astype(F32)
        for refs, last in zip((kern_re_refs, kern_im_refs), other_kern)
    ]
    excite = jnp.concatenate(
        [own[:, EXC_AT : EXC_AT + exc], other[:, EXC_AT : EXC_AT + exc]], 0
    ).T
    re = two_parts(kern_re + zre[...])
    im = two_parts(kern_im + zim[...])
    product = dot(excite, jnp.concatenate([*re, *im], 1))
    by_re = product[:, :rows] + product[:, rows : 2 * rows]
    by_im = product[:, 2 * rows : 3 * rows] + product[:, 3 * rows :]
    h = exc // 2
    result = jnp.concatenate([by_re[:h] - by_im[h:], by_re[h:] + by_im[:h]], 0)
    out_ref[...] = result.T


def in_vmem(x):
    return pltpu.with_memory_space_constraint(x, pltpu.VMEM)


def in_smem(x):
    return pltpu.with_memory_space_constraint(x, pltpu.SMEM)


def in_hbm(x):
    return pltpu.with_memory_space_constraint(x, pltpu.HBM)


SMEM_SPEC = pl.BlockSpec(memory_space=pltpu.SMEM)
VMEM_SPEC = pl.BlockSpec(memory_space=pltpu.VMEM)


def packed(units, slots, src_geom, excite, src_nodes, src_weights, tgt_nodes, tgt_weights, near_order):
    excite = excite.T
    src_weights = src_weights.transpose(0, 2, 1)
    cpd, exc = excite.shape
    rows_here = tgt_weights.shape[2] // lax.axis_size("col")
    inputs = (near_order, src_geom, excite, src_nodes, src_weights, tgt_nodes)
    return pl.pallas_call(
        functools.partial(pack_kernel, units),
        out_shape=[
            pltpu.VMEM((cpd, EXC_AT + exc + NODE_WIDTH), BF16),
            pltpu.VMEM((3, 8, LANES), F32),
            pltpu.VMEM((2, QN, rows_here), BF16),
            pltpu.SMEM((slots,), jnp.int32),
        ],
        in_specs=[pl.BlockSpec(memory_space=pl.ANY)] * 7,
        out_specs=[VMEM_SPEC] * 3 + [SMEM_SPEC],
        scratch_shapes=[pltpu.SMEM(near_order.shape, jnp.int32)]
        + [pltpu.VMEM(x.shape, x.dtype) for x in inputs[1:]]
        + [pltpu.SemaphoreType.DMA((7,))],
        compiler_params=SMALL,
    )(*[in_hbm(x) for x in inputs], in_hbm(tgt_weights))


def near_blocks(exc, first, slots, wavenumber, found, fresh, own, target, ut, tgt_geom, hand_on, both=False):
    rows_here = tgt_geom.shape[1] // lax.axis_size("col")
    kern = pltpu.VMEM((fresh.shape[0] + both * own.shape[0], rows_here), BF16)
    cost = pl.CostEstimate(flops=1, bytes_accessed=1, transcendentals=0)
    outs = [pltpu.VMEM((slots, 2 * QN, 2 * LANES), BF16), kern, kern] + [pltpu.VMEM(own.shape, BF16)] * hand_on
    if first == 0:
        outs.append(pltpu.VMEM((2 * QN, 2 * LANES), BF16))
    return pl.pallas_call(
        functools.partial(near_kernel if first else first_near_kernel, exc, first),
        out_shape=outs,
        in_specs=[SMEM_SPEC] * 2 + [VMEM_SPEC] * 5,
        out_specs=[VMEM_SPEC] * len(outs),
        compiler_params=SMALL,
        cost_estimate=cost,
    )(wavenumber, in_smem(found), in_vmem(fresh), in_vmem(own), in_vmem(target), in_vmem(ut), in_vmem(tgt_geom))


def exchanged(
    wavenumber, tgt_geom, src_geom, excite, tgt_nodes, src_nodes, tgt_weights, src_weights, near_order
):
    cpd = src_geom.shape[1]
    exc = excite.shape[0]
    cores = lax.axis_size("col")
    count = cores * lax.axis_size("row")
    rows_here = tgt_geom.shape[1] // cores
    even, odd = exchange_steps(count)
    units = [[p >> 1 for p in relative_places(s)] for s in (even, odd)]
    own, target, ut, found = packed(
        units, len(units[0]), src_geom, excite, src_nodes, src_weights, tgt_nodes, tgt_weights, near_order
    )

    def moved(value, a, b):
        pairs = [(i, i ^ (b if bin(i).count("1") % 2 else a)) for i in range(count)]
        return lax.ppermute(value, ("row", "col"), pairs)

    fresh = own
    near = []
    done = 0
    steps = list(zip(even, odd))
    for step, (a, b) in enumerate(steps):
        arriving = moved(own, a, b)
        slots = fresh.shape[0] // cpd
        made = near_blocks(exc, done, slots, wavenumber, found, fresh, own, target, ut, tgt_geom, True)
        near.extend(made[:3])
        if not done:
            ut = made[4]
        if step == len(steps) - 2:
            other_first = moved(made[3], 1, 1)
        done += slots
        fresh = arriving
        if step < len(steps) - 1:
            own = jnp.concatenate([made[3], arriving], 0)
    half = own.shape[0] // 2
    other_early = moved(own[half:], 1, 1)
    quarter = half // cpd
    early = near_blocks(
        exc, done, quarter, wavenumber, found, other_early, other_first, target, ut, tgt_geom, False, True
    )
    fresh, early, made = lax.optimization_barrier((fresh, early, made))
    other_late = moved(fresh, 1, 1)
    late = near_blocks(
        exc, done + quarter, quarter, wavenumber, found, fresh, fresh, target, ut, tgt_geom, False
    )
    near.append(early[0])
    near.extend(late)
    partner = [units[1].index(u) for u in units[0]]
    return pl.pallas_call(
        functools.partial(last_kernel, exc, partner),
        out_shape=jax.ShapeDtypeStruct((rows_here, exc), F32),
        in_specs=[SMEM_SPEC] + [VMEM_SPEC] * (8 + len(near)),
        out_specs=VMEM_SPEC,
        scratch_shapes=[pltpu.VMEM((count * cpd, rows_here), F32)] * 2,
        compiler_params=SMALL,
    )(
        wavenumber,
        *[in_vmem(x) for x in (made[3], fresh, other_first, other_early, other_late, tgt_geom, *early[1:], *near)],
    )


def gathered(
    wavenumber, tgt_geom, src_geom, excite, tgt_nodes, src_nodes, tgt_weights, src_weights, near_order
):
    cpd = src_geom.shape[1]
    exc = excite.shape[0]
    half = exc // 2
    cores = lax.axis_size("col")
    nrow = lax.axis_size("row")
    row = lax.axis_index("row")
    rows_here = tgt_geom.shape[1] // cores
    band = near_order.shape[1]
    own, target, ut, found = packed(
        None, band, src_geom, excite, src_nodes, src_weights, tgt_nodes, tgt_weights, near_order
    )
    everything = lax.all_gather(own, ("row", "col"), axis=0, tiled=True)
    sources = lax.all_gather(src_geom, ("row", "col"), axis=1, tiled=True)
    blocks = [
        lax.dynamic_slice_in_dim(
            everything, jnp.clip(row + o - (band - 1) // 2, 0, nrow - 1) * cores * cpd, cores * cpd, 0
        )
        for o in range(band)
    ]
    fresh = jnp.concatenate([block[:cpd] for block in blocks], 0)
    near = near_blocks(exc, 0, band, wavenumber, found, fresh, own, target, ut, tgt_geom, False)[0]
    high = lax.Precision.HIGHEST
    total = jnp.zeros((rows_here, exc), F32)
    dims = (((0,), (0,)), ((), ()))
    m, r = LANES, QN - LANES
    for o, block in enumerate(blocks):
        w, x = block[:, :EXC_AT].astype(F32), block[:, EXC_AT : EXC_AT + exc].astype(F32)
        v = near[o, :, :LANES].astype(F32) + near[o, :, LANES:].astype(F32)
        w_re = jnp.concatenate([w[:, :m], w[:, 2 * m : 2 * m + r]], 1)
        w_im = jnp.concatenate([w[:, m : 2 * m], w[:, 2 * m + r :]], 1)
        v_re = jnp.concatenate([v[:m], v[2 * m : 2 * m + r]], 0)
        v_im = jnp.concatenate([v[m : 2 * m], v[2 * m + r :]], 0)
        a_re = jnp.dot(w_re, v_re, precision=high) - jnp.dot(w_im, v_im, precision=high)
        a_im = jnp.dot(w_re, v_im, precision=high) + jnp.dot(w_im, v_re, precision=high)
        re = lax.dot_general(a_re, x, dims, precision=high)
        im = lax.dot_general(a_im, x, dims, precision=high)
        total = total + INV_FOUR_PI * jnp.concatenate(
            [re[:, :half] - im[:, half:], re[:, half:] + im[:, :half]], 1
        )
    targets = lax.dynamic_slice_in_dim(tgt_geom, lax.axis_index("col") * rows_here, rows_here, 1)
    width = math.gcd(everything.shape[0], 512)

    def far(index, accum):
        places = lax.dynamic_slice_in_dim(sources, index * width, width, 1)
        x = lax.dynamic_slice_in_dim(everything, index * width, width, 0)[:, EXC_AT : EXC_AT + exc]
        kern_re, kern_im = far_kernel_values(
            wavenumber[0], [places[i][:, None] for i in range(4)], targets
        )
        re = lax.dot_general(kern_re.astype(BF16), x, dims, preferred_element_type=F32)
        im = lax.dot_general(kern_im.astype(BF16), x, dims, preferred_element_type=F32)
        return accum + jnp.concatenate([re[:, :half] - im[:, half:], re[:, half:] + im[:, :half]], 1)

    return lax.fori_loop(0, everything.shape[0] // width, far, total)


def on_device(*arguments):
    count = lax.axis_size("row") * lax.axis_size("col")
    short = lax.axis_size("col") == 2 and lax.axis_size("row") <= 16 and count & (count - 1) == 0
    return (exchanged if short and count >= 8 else gathered)(*arguments)


def solution(mesh):
    return jax.shard_map(
        on_device,
        mesh=mesh,
        in_specs=(
            P("groups"),
            P(None, ("groups", "row")),
            P(None, ("groups", "row", "col")),
            P(None, ("groups", "row", "col")),
            P(None, ("groups", "row")),
            P(None, ("groups", "row")),
            P(None, None, ("groups", "row")),
            P(None, None, ("groups", "row", "col")),
            P(("groups", "row"), None),
        ),
        out_specs=P(("groups", "row", "col"), None),
        check_vma=False,
    )
```

```python
import functools
import math

import jax
import jax.numpy as jnp
from jax import lax
from jax.experimental import pallas as pl
from jax.experimental.pallas import tpu as pltpu
from jax.sharding import PartitionSpec as P

QSTEP = 64
QN = 192
LANES = 128
PARTS = 3
SOFT = 0.05
INV_FOUR_PI = 1.0 / (4.0 * math.pi)
INV_TURN = 1.0 / (2.0 * math.pi)
TURN_HIGH = 6.28125
TURN_LOW = 2.0 * math.pi - TURN_HIGH
SIN_HALF = (3.14159264, -5.16771009, 2.55007766, -0.59829216, 0.07765941)
COS_HALF = (1.0, -4.93480214, 4.05870916, -1.33521206, 0.23493756, -0.02439672)
COS_FULL = (
    0.99999999, -19.73920453, 64.93911898, -85.45016555, 60.16783171, -25.96831321, 6.52961029
)
BF16 = jnp.bfloat16
F32 = jnp.float32
NN = (((1,), (0,)), ((), ()))
NT = (((1,), (1,)), ((), ()))
EXC_AT = 2 * QN
NODE_WIDTH = LANES
SMALL = pltpu.CompilerParams(vmem_limit_bytes=24 * 2**20)


def dot(left, right, dims=NN):
    return lax.dot_general(left, right, dims, preferred_element_type=F32)


def polynomial(z, coefficients):
    total = coefficients[-1]
    for c in coefficients[-2::-1]:
        total = total * z + c
    return total


def sincos_turns(f):
    z = f * f
    s = f * polynomial(z, SIN_HALF)
    c = polynomial(z, COS_HALF)
    twice = s + s
    return twice * c, 1.0 - twice * s


def three_parts(x):
    first = x.astype(BF16)
    rest = x - first.astype(F32)
    second = rest.astype(BF16)
    third = (rest - second.astype(F32)).astype(BF16)
    return first, second, third


def two_parts(x):
    first = x.astype(BF16)
    return first, (x - first.astype(F32)).astype(BF16)


def exchange_steps(count):
    bits = [1 << b for b in range(count.bit_length() - 2, 0, -1)]
    swapped = bits[:-2] + bits[-2:][::-1] if len(bits) >= 2 else bits
    return [b | 1 for b in bits], [b | 1 for b in swapped]


def relative_places(steps):
    places = [0]
    for step in steps:
        places = places + [p ^ step for p in places]
    return places


def iota(shape, axis):
    return lax.broadcasted_iota(jnp.int32, shape, axis)


def geom_lane(cpd):
    return 3 * PARTS * (QN // cpd)


def place_matrices(cpd):
    groups = QN // cpd
    shape = (LANES, 2 * 16)
    begin, row = iota(shape, 0), iota(shape, 1)
    node = jnp.logical_and(begin >= row * groups, begin < (row + 1) * groups)
    node = jnp.logical_and(node, row < 3 * PARTS)
    source = jnp.logical_and(begin - geom_lane(cpd) == row - 16, row >= 16)
    row_of = jnp.where(jnp.logical_or(node, source), 1.0, 0.0).astype(BF16)
    shape = (LANES, QN)
    lane, group = iota(shape, 0), lax.div(iota(shape, 1), cpd)
    wanted = jnp.where(lane < geom_lane(cpd), lax.rem(lane, groups), 0)
    kept = jnp.where(group == wanted, 1.0, 0.0)
    shape = (cpd, QN)
    column_of = jnp.where(lax.rem(iota(shape, 1), cpd) == iota(shape, 0), 1.0, 0.0).astype(BF16)
    return row_of, kept, column_of


def pack_kernel(
    units, order_hbm, geom_hbm, excite_hbm, nodes_hbm, weights_hbm, tnodes_hbm, tweights_hbm,
    out_ref, target_ref, tests_ref, found_ref,
    order_ref, geom_ref, excite_ref, nodes_ref, weights_ref, tnodes_ref, arrived,
):
    col = lax.axis_index("col")
    rows = tests_ref.shape[2]
    at = pl.ds(pl.multiple_of(col * rows, LANES), rows)
    moves = [
        (weights_hbm, weights_ref),
        (nodes_hbm, nodes_ref),
        (geom_hbm, geom_ref),
        (excite_hbm, excite_ref),
        (tnodes_hbm, tnodes_ref),
        (order_hbm, order_ref),
        (tweights_hbm.at[:, :, at], tests_ref),
    ]
    copies = [pltpu.make_async_copy(*move, arrived.at[i]) for i, move in enumerate(moves)]
    for copy in copies:
        copy.start()
    cpd, exc = excite_ref.shape
    row_of, kept, column_of = place_matrices(cpd)
    for copy in copies[:-1]:
        copy.wait()
    main = LANES
    rest = QN - main
    re, im = weights_ref[0], weights_ref[1]
    out_ref[:, 0:main] = re[:, :main]
    out_ref[:, main : 2 * main] = im[:, :main]
    out_ref[:, 2 * main : 2 * main + 2 * rest] = jnp.concatenate([re[:, main:], im[:, main:]], 1)
    out_ref[:, EXC_AT : EXC_AT + exc] = excite_ref[...]
    nodes = [p.astype(F32) for p in three_parts(nodes_ref[...])]
    geom = jnp.concatenate([p.astype(F32) for p in three_parts(geom_ref[...])], 0)
    values = jnp.concatenate(
        nodes
        + [
            jnp.zeros((16 - 3 * PARTS, QN), F32),
            jnp.concatenate([geom, jnp.zeros((geom.shape[0], QN - cpd), F32)], 1),
            jnp.zeros((16 - geom.shape[0], QN), F32),
        ],
        0,
    ).astype(BF16)
    spread = (dot(row_of, values) * kept).astype(BF16)
    out_ref[:, EXC_AT + exc :] = dot(column_of, spread, NT).astype(BF16)
    nodes = tnodes_ref[:, :QN]
    for b in range(1, tnodes_ref.shape[1] // QN):
        nodes = jnp.where(col == b, tnodes_ref[:, b * QN : (b + 1) * QN], nodes)
    end = nodes[:, LANES:]
    start = nodes[:, :QSTEP]
    target_ref[0, 0:3] = nodes[:, :LANES]
    target_ref[1, 0:3] = jnp.concatenate([end, end], 1)
    target_ref[2, 0:3] = jnp.concatenate([start, start], 1)
    for slot, order in enumerate(slot_orders(order_ref, units)):
        found_ref[slot] = order
    copies[-1].wait()


def store_tests(tests_ref, ut_ref):
    re, im = tests_ref[0], tests_ref[1]
    main = LANES
    ut_ref[0:main, :] = jnp.concatenate([re[:main], im[:main]], 1)
    ut_ref[main : 2 * main, :] = jnp.concatenate([-im[:main], re[:main]], 1)
    ut_ref[2 * main : 2 * main + QSTEP, :] = jnp.concatenate([re[main:], im[main:]], 1)
    ut_ref[2 * main + QSTEP :, :] = jnp.concatenate([-im[main:], re[main:]], 1)


def node_columns(data_ref, exc):
    block = data_ref[:, EXC_AT + exc :].astype(F32)
    step = geom_lane(16) // PARTS
    return (block[:, :step] + block[:, step : 2 * step]) + block[:, 2 * step : 3 * step]


def two_part_dot(high, low, right):
    count = high.shape[0]
    both = dot(jnp.concatenate([high, low], 0), right)
    return both[:count] + both[count:]


def near_slot(order, columns, slot, target_ref, ut_ref, turns, out_ref):
    lane = lax.broadcasted_iota(jnp.int32, (1, LANES), 1)
    quarter = jnp.where(lane < QSTEP, 0.0, 0.25)
    main = LANES

    def located(count):
        return [
            jnp.concatenate(
                [
                    jnp.broadcast_to(columns[16 * slot : 16 * slot + 16, lane : lane + 1], (16, LANES))
                    for lane in range(axis * (QN // 16), axis * (QN // 16) + count // 16)
                ],
                0,
            )
            for axis in range(3)
        ]

    def distance2(source, tile):
        total = SOFT * SOFT
        for axis in range(3):
            d = source[axis] - target_ref[tile, axis : axis + 1, :]
            total = total + d * d
        return total

    def both(source):
        d2 = distance2(source, 0)
        inv = lax.rsqrt(d2)
        t = (d2 * inv) * turns
        sin, cos = sincos_turns(t - jnp.round(t))
        return two_parts(inv * cos), two_parts(inv * sin)

    def split_lanes(source, tile):
        d2 = distance2(source, tile)
        inv = lax.rsqrt(d2)
        t = (d2 * inv) * turns
        f = (t - jnp.round(t - quarter)) - quarter
        return two_parts(inv * polynomial(f * f, COS_FULL))

    def put(at, value):
        high, low = two_parts(value)
        count = value.shape[0]
        out_ref[at : at + count, :LANES] = high
        out_ref[at : at + count, LANES:] = low

    def clear(begin, end):
        out_ref[begin:end, :] = jnp.zeros((end - begin, 2 * LANES), BF16)

    @pl.when(order == 3)
    def _():
        source = located(QN)
        (re_high, re_low), (im_high, im_low) = both(source)
        rest_high, rest_low = split_lanes(source, 1)
        high = jnp.concatenate([re_high, im_high, rest_high], 1)
        low = jnp.concatenate([re_low, im_low, rest_low], 1)
        v = two_part_dot(high, low, ut_ref[...])
        put(0, v[:main, :LANES])
        put(main, v[:main, LANES:])
        put(2 * main, v[main:, :LANES])
        put(2 * main + QSTEP, v[main:, LANES:])

    @pl.when(order == 2)
    def _():
        (re_high, re_low), (im_high, im_low) = both(located(main))
        high = jnp.concatenate([re_high, im_high], 1)
        low = jnp.concatenate([re_low, im_low], 1)
        v = two_part_dot(high, low, ut_ref[: 2 * main])
        put(0, v[:, :LANES])
        put(main, v[:, LANES:])
        clear(2 * main, 3 * main)

    @pl.when(order == 1)
    def _():
        high, low = split_lanes(located(QSTEP), 2)
        weights = jnp.concatenate([ut_ref[0:QSTEP], ut_ref[main : main + QSTEP]], 0)
        v = two_part_dot(high, low, weights)
        put(0, v[:, :LANES])
        clear(QSTEP, main)
        put(main, v[:, LANES:])
        clear(main + QSTEP, 3 * main)

    @pl.when(order == 0)
    def _():
        clear(0, 3 * main)


def slot_orders(order_ref, units):
    row, col = lax.axis_index("row"), lax.axis_index("col")
    nrow = lax.axis_size("row")
    band = order_ref.shape[1]
    reach = (band - 1) // 2
    if units is None:
        offsets = [jnp.where(jnp.logical_and(row + o >= reach, row + o - reach < nrow), o, -1) for o in range(band)]
    else:
        place, parity = row * lax.axis_size("col") + col, 0
        for _ in range((nrow * lax.axis_size("col")).bit_length() - 1):
            parity = parity + lax.rem(place, 2)
            place = lax.div(place, 2)
        parity = lax.rem(parity, 2)
        offsets = [
            (row ^ (a if a == b else jnp.where(parity == 0, a, b))) - row + reach for a, b in zip(*units)
        ]
    return [
        jnp.where(
            jnp.logical_and(o >= 0, o < band), order_ref[col, jnp.clip(o, 0, band - 1)], 0
        )
        for o in offsets
    ]


def far_kernel_values(wave, source, tgeom):
    dx = tgeom[0:1] - source[0]
    dy = tgeom[1:2] - source[1]
    dz = tgeom[2:3] - source[2]
    d2 = dx * dx + dy * dy + dz * dz + SOFT * SOFT
    inv = lax.rsqrt(d2)
    radius = d2 * inv
    cosine = (tgeom[3:4] * dx + tgeom[4:5] * dy + tgeom[5:6] * dz) * inv
    scale = source[3] * (INV_FOUR_PI * inv)
    phase = wave * radius
    t = phase * INV_TURN
    n = jnp.round(t)
    sin, cos = sincos_turns(((phase - n * TURN_HIGH) - n * TURN_LOW) * INV_TURN)
    green_re = scale * cos
    green_im = scale * sin
    factor_re = 1.0 - cosine
    factor_im = cosine * (inv * (-1.0 / wave))
    kern_re = (green_re * factor_re - green_im * factor_im).astype(BF16)
    kern_im = (green_re * factor_im + green_im * factor_re).astype(BF16)
    return kern_re, kern_im


def far_rows(data, exc, wave, tgeom):
    shape = (LANES, 4 * LANES)
    at, wanted = iota(shape, 0) - geom_lane(16), lax.div(iota(shape, 1), LANES)
    pick = jnp.logical_and(
        jnp.logical_and(at >= 0, at < 4 * PARTS), lax.rem(at + 4 * LANES, 4) == wanted
    )
    geom = data[:, EXC_AT + exc :]
    spread = dot(geom, jnp.where(pick, 1.0, 0.0).astype(BF16))
    return far_kernel_values(wave, [spread[:, i * LANES : (i + 1) * LANES] for i in range(4)], tgeom)


def own_targets(tgeom_ref, rows):
    at = pl.multiple_of(lax.axis_index("col") * rows, LANES)
    return tgeom_ref[:, pl.ds(at, rows)]


def near_kernel(
    exc, first, wave_ref, found_ref, data_ref, own_ref, target_ref, ut_ref, tgeom_ref,
    v_ref, kern_re_ref, kern_im_ref, *copy_ref,
):
    if copy_ref:
        copy_ref[0][...] = own_ref[...]
    wave = wave_ref[0]
    tgeom = own_targets(tgeom_ref, kern_re_ref.shape[1])
    data = data_ref[...]
    if kern_re_ref.shape[0] > data.shape[0]:
        data = jnp.concatenate([own_ref[...], data], 0)
    kern_re_ref[...], kern_im_ref[...] = far_rows(data, exc, wave, tgeom)
    slots = v_ref.shape[0]
    skipped = data_ref.shape[0] // 16 - slots
    columns = node_columns(data_ref, exc)
    for slot in range(slots):
        near_slot(
            found_ref[first + slot], columns, skipped + slot, target_ref, ut_ref, wave * INV_TURN, v_ref.at[slot]
        )


def first_near_kernel(
    exc, first, wave_ref, found_ref, data_ref, own_ref, target_ref, tests_ref, tgeom_ref, *refs
):
    *refs, ut_ref = refs
    store_tests(tests_ref, ut_ref)
    near_kernel(exc, first, wave_ref, found_ref, data_ref, own_ref, target_ref, ut_ref, tgeom_ref, *refs)


def last_kernel(
    exc, partner, wave_ref, own_early, own_late, other_first, other_early, other_late, tgeom_ref,
    early_re_ref, early_im_ref, *refs
):
    own = jnp.concatenate([own_early[...], own_late[...]], 0)
    other = jnp.concatenate([other_first[...], other_early[...], other_late[...]], 0)
    out_ref, zre, zim = refs[-3:]
    *made, early_v, late_v, late_re, late_im = refs[:-3]
    v_refs = [*made[::3], early_v, late_v]
    kern_re_refs, kern_im_refs = [*made[1::3], late_re], [*made[2::3], late_im]
    rows = out_ref.shape[0]
    cpd = 16
    main = LANES
    slots = len(partner)
    sign = jnp.where(lax.broadcasted_iota(jnp.int32, (1, LANES), 1) < QSTEP, 1.0, -1.0).astype(BF16)

    def weight_rows(data):
        w = [data[:, i * main : (i + 1) * main] for i in range(3)]
        swapped = jnp.concatenate([w[2][:, QSTEP:], w[2][:, :QSTEP]], 1)
        return jnp.concatenate([w[0], -w[1], w[2] * sign], 1), jnp.concatenate([w[1], w[0], swapped], 1)

    own_re, own_im = weight_rows(own)
    other_re, other_im = weight_rows(other)
    slot = 0
    for v_ref in v_refs:
        for i in range(v_ref.shape[0]):
            here = slice(slot * cpd, (slot + 1) * cpd)
            there = slice(partner[slot] * cpd, (partner[slot] + 1) * cpd)
            left = jnp.concatenate([own_re[here], other_re[there], own_im[here], other_im[there]], 0)
            product = dot(left, v_ref[i])
            a = (product[:, :LANES] + product[:, LANES:]) * INV_FOUR_PI
            there = slice((slots + partner[slot]) * cpd, (slots + partner[slot] + 1) * cpd)
            zre[here] = a[0:cpd]
            zre[there] = a[cpd : 2 * cpd]
            zim[here] = a[2 * cpd : 3 * cpd]
            zim[there] = a[3 * cpd :]
            slot += 1

    late_kern = far_rows(other_late, exc, wave_ref[0], own_targets(tgeom_ref, rows))
    first = other_first.shape[0]
    kern_re, kern_im = [
        jnp.concatenate(
            [*[ref[...] for ref in refs[:-2]], refs[-2][first:], refs[-1][...], refs[-2][:first], early[...], x], 0
        ).astype(F32)
        for refs, early, x in zip((kern_re_refs, kern_im_refs), (early_re_ref, early_im_ref), late_kern)
    ]
    excite = jnp.concatenate(
        [own[:, EXC_AT : EXC_AT + exc], other[:, EXC_AT : EXC_AT + exc]], 0
    ).T
    re = two_parts(kern_re + zre[...])
    im = two_parts(kern_im + zim[...])
    product = dot(excite, jnp.concatenate([*re, *im], 1))
    by_re = product[:, :rows] + product[:, rows : 2 * rows]
    by_im = product[:, 2 * rows : 3 * rows] + product[:, 3 * rows :]
    h = exc // 2
    result = jnp.concatenate([by_re[:h] - by_im[h:], by_re[h:] + by_im[:h]], 0)
    out_ref[...] = result.T


def in_vmem(x):
    return pltpu.with_memory_space_constraint(x, pltpu.VMEM)


def in_smem(x):
    return pltpu.with_memory_space_constraint(x, pltpu.SMEM)


def in_hbm(x):
    return pltpu.with_memory_space_constraint(x, pltpu.HBM)


SMEM_SPEC = pl.BlockSpec(memory_space=pltpu.SMEM)
VMEM_SPEC = pl.BlockSpec(memory_space=pltpu.VMEM)


def packed(units, slots, src_geom, excite, src_nodes, src_weights, tgt_nodes, tgt_weights, near_order):
    excite = excite.T
    src_weights = src_weights.transpose(0, 2, 1)
    cpd, exc = excite.shape
    rows_here = tgt_weights.shape[2] // lax.axis_size("col")
    inputs = (near_order, src_geom, excite, src_nodes, src_weights, tgt_nodes)
    return pl.pallas_call(
        functools.partial(pack_kernel, units),
        out_shape=[
            pltpu.VMEM((cpd, EXC_AT + exc + NODE_WIDTH), BF16),
            pltpu.VMEM((3, 8, LANES), F32),
            pltpu.VMEM((2, QN, rows_here), BF16),
            pltpu.SMEM((slots,), jnp.int32),
        ],
        in_specs=[pl.BlockSpec(memory_space=pl.ANY)] * 7,
        out_specs=[VMEM_SPEC] * 3 + [SMEM_SPEC],
        scratch_shapes=[pltpu.SMEM(near_order.shape, jnp.int32)]
        + [pltpu.VMEM(x.shape, x.dtype) for x in inputs[1:]]
        + [pltpu.SemaphoreType.DMA((7,))],
        compiler_params=SMALL,
    )(*[in_hbm(x) for x in inputs], in_hbm(tgt_weights))


def near_blocks(exc, first, slots, wavenumber, found, fresh, own, target, ut, tgt_geom, hand_on, both=False):
    rows_here = tgt_geom.shape[1] // lax.axis_size("col")
    kern = pltpu.VMEM((fresh.shape[0] + both * own.shape[0], rows_here), BF16)
    cost = pl.CostEstimate(flops=1, bytes_accessed=1, transcendentals=0)
    outs = [pltpu.VMEM((slots, 2 * QN, 2 * LANES), BF16), kern, kern] + [pltpu.VMEM(own.shape, BF16)] * hand_on
    if first == 0:
        outs.append(pltpu.VMEM((2 * QN, 2 * LANES), BF16))
    return pl.pallas_call(
        functools.partial(near_kernel if first else first_near_kernel, exc, first),
        out_shape=outs,
        in_specs=[SMEM_SPEC] * 2 + [VMEM_SPEC] * 5,
        out_specs=[VMEM_SPEC] * len(outs),
        compiler_params=SMALL,
        cost_estimate=cost,
    )(wavenumber, in_smem(found), in_vmem(fresh), in_vmem(own), in_vmem(target), in_vmem(ut), in_vmem(tgt_geom))


def exchanged(
    wavenumber, tgt_geom, src_geom, excite, tgt_nodes, src_nodes, tgt_weights, src_weights, near_order
):
    cpd = src_geom.shape[1]
    exc = excite.shape[0]
    cores = lax.axis_size("col")
    count = cores * lax.axis_size("row")
    rows_here = tgt_geom.shape[1] // cores
    even, odd = exchange_steps(count)
    units = [[p >> 1 for p in relative_places(s)] for s in (even, odd)]
    own, target, ut, found = packed(
        units, len(units[0]), src_geom, excite, src_nodes, src_weights, tgt_nodes, tgt_weights, near_order
    )

    def moved(value, a, b):
        pairs = [(i, i ^ (b if bin(i).count("1") % 2 else a)) for i in range(count)]
        return lax.ppermute(value, ("row", "col"), pairs)

    fresh = own
    near = []
    done = 0
    steps = list(zip(even, odd))
    for step, (a, b) in enumerate(steps):
        arriving = moved(own, a, b)
        slots = fresh.shape[0] // cpd
        last = step == len(steps) - 1
        made = near_blocks(
            exc, done, slots, wavenumber, found, fresh, other_first if last else own, target, ut, tgt_geom,
            not last, last,
        )
        near.extend(made[:3])
        if not done:
            ut = made[4]
        if step == len(steps) - 2:
            other_first = moved(made[3], 1, 1)
        done += slots
        fresh = arriving
        if not last:
            own = jnp.concatenate([made[3], arriving], 0)
        if step == len(steps) - 2:
            own, other_first = lax.optimization_barrier((own, other_first))
    half = own.shape[0] // 2
    other_early = moved(own[half:], 1, 1)
    quarter = half // cpd
    early = near_blocks(
        exc, done, quarter, wavenumber, found, other_early, other_early, target, ut, tgt_geom, False
    )
    fresh, early, made = lax.optimization_barrier((fresh, early, made))
    other_late = moved(fresh, 1, 1)
    late = near_blocks(
        exc, done + quarter, quarter, wavenumber, found, fresh, fresh, target, ut, tgt_geom, False
    )
    near.append(early[0])
    near.extend(late)
    partner = [units[1].index(u) for u in units[0]]
    return pl.pallas_call(
        functools.partial(last_kernel, exc, partner),
        out_shape=jax.ShapeDtypeStruct((rows_here, exc), F32),
        in_specs=[SMEM_SPEC] + [VMEM_SPEC] * (8 + len(near)),
        out_specs=VMEM_SPEC,
        scratch_shapes=[pltpu.VMEM((count * cpd, rows_here), F32)] * 2,
        compiler_params=SMALL,
    )(
        wavenumber,
        *[in_vmem(x) for x in (own, fresh, other_first, other_early, other_late, tgt_geom, *early[1:], *near)],
    )


def gathered(
    wavenumber, tgt_geom, src_geom, excite, tgt_nodes, src_nodes, tgt_weights, src_weights, near_order
):
    cpd = src_geom.shape[1]
    exc = excite.shape[0]
    half = exc // 2
    cores = lax.axis_size("col")
    nrow = lax.axis_size("row")
    row = lax.axis_index("row")
    rows_here = tgt_geom.shape[1] // cores
    band = near_order.shape[1]
    own, target, ut, found = packed(
        None, band, src_geom, excite, src_nodes, src_weights, tgt_nodes, tgt_weights, near_order
    )
    everything = lax.all_gather(own, ("row", "col"), axis=0, tiled=True)
    sources = lax.all_gather(src_geom, ("row", "col"), axis=1, tiled=True)
    blocks = [
        lax.dynamic_slice_in_dim(
            everything, jnp.clip(row + o - (band - 1) // 2, 0, nrow - 1) * cores * cpd, cores * cpd, 0
        )
        for o in range(band)
    ]
    fresh = jnp.concatenate([block[:cpd] for block in blocks], 0)
    near = near_blocks(exc, 0, band, wavenumber, found, fresh, own, target, ut, tgt_geom, False)[0]
    high = lax.Precision.HIGHEST
    total = jnp.zeros((rows_here, exc), F32)
    dims = (((0,), (0,)), ((), ()))
    m, r = LANES, QN - LANES
    for o, block in enumerate(blocks):
        w, x = block[:, :EXC_AT].astype(F32), block[:, EXC_AT : EXC_AT + exc].astype(F32)
        v = near[o, :, :LANES].astype(F32) + near[o, :, LANES:].astype(F32)
        w_re = jnp.concatenate([w[:, :m], w[:, 2 * m : 2 * m + r]], 1)
        w_im = jnp.concatenate([w[:, m : 2 * m], w[:, 2 * m + r :]], 1)
        v_re = jnp.concatenate([v[:m], v[2 * m : 2 * m + r]], 0)
        v_im = jnp.concatenate([v[m : 2 * m], v[2 * m + r :]], 0)
        a_re = jnp.dot(w_re, v_re, precision=high) - jnp.dot(w_im, v_im, precision=high)
        a_im = jnp.dot(w_re, v_im, precision=high) + jnp.dot(w_im, v_re, precision=high)
        re = lax.dot_general(a_re, x, dims, precision=high)
        im = lax.dot_general(a_im, x, dims, precision=high)
        total = total + INV_FOUR_PI * jnp.concatenate(
            [re[:, :half] - im[:, half:], re[:, half:] + im[:, :half]], 1
        )
    targets = lax.dynamic_slice_in_dim(tgt_geom, lax.axis_index("col") * rows_here, rows_here, 1)
    width = math.gcd(everything.shape[0], 512)

    def far(index, accum):
        places = lax.dynamic_slice_in_dim(sources, index * width, width, 1)
        x = lax.dynamic_slice_in_dim(everything, index * width, width, 0)[:, EXC_AT : EXC_AT + exc]
        kern_re, kern_im = far_kernel_values(
            wavenumber[0], [places[i][:, None] for i in range(4)], targets
        )
        re = lax.dot_general(kern_re.astype(BF16), x, dims, preferred_element_type=F32)
        im = lax.dot_general(kern_im.astype(BF16), x, dims, preferred_element_type=F32)
        return accum + jnp.concatenate([re[:, :half] - im[:, half:], re[:, half:] + im[:, :half]], 1)

    return lax.fori_loop(0, everything.shape[0] // width, far, total)


def on_device(*arguments):
    count = lax.axis_size("row") * lax.axis_size("col")
    short = lax.axis_size("col") == 2 and lax.axis_size("row") <= 16 and count & (count - 1) == 0
    return (exchanged if short and count >= 8 else gathered)(*arguments)


def solution(mesh):
    return jax.shard_map(
        on_device,
        mesh=mesh,
        in_specs=(
            P("groups"),
            P(None, ("groups", "row")),
            P(None, ("groups", "row", "col")),
            P(None, ("groups", "row", "col")),
            P(None, ("groups", "row")),
            P(None, ("groups", "row")),
            P(None, None, ("groups", "row")),
            P(None, None, ("groups", "row", "col")),
            P(("groups", "row"), None),
        ),
        out_specs=P(("groups", "row", "col"), None),
        check_vma=False,
    )
```

```python
import functools
import math

import jax
import jax.numpy as jnp
from jax import lax
from jax.experimental import pallas as pl
from jax.experimental.pallas import tpu as pltpu
from jax.sharding import PartitionSpec as P

QSTEP = 64
QN = 192
LANES = 128
PARTS = 3
SOFT = 0.05
INV_FOUR_PI = 1.0 / (4.0 * math.pi)
INV_TURN = 1.0 / (2.0 * math.pi)
TURN_HIGH = 6.28125
TURN_LOW = 2.0 * math.pi - TURN_HIGH
SIN_HALF = (3.14159264, -5.16771009, 2.55007766, -0.59829216, 0.07765941)
COS_HALF = (1.0, -4.93480214, 4.05870916, -1.33521206, 0.23493756, -0.02439672)
COS_FULL = (
    0.99999999, -19.73920453, 64.93911898, -85.45016555, 60.16783171, -25.96831321, 6.52961029
)
BF16 = jnp.bfloat16
F32 = jnp.float32
NN = (((1,), (0,)), ((), ()))
NT = (((1,), (1,)), ((), ()))
EXC_AT = 2 * QN
NODE_WIDTH = LANES
SMALL = pltpu.CompilerParams(vmem_limit_bytes=24 * 2**20)


def dot(left, right, dims=NN):
    return lax.dot_general(left, right, dims, preferred_element_type=F32)


def polynomial(z, coefficients):
    total = coefficients[-1]
    for c in coefficients[-2::-1]:
        total = total * z + c
    return total


def sincos_turns(f):
    z = f * f
    s = f * polynomial(z, SIN_HALF)
    c = polynomial(z, COS_HALF)
    twice = s + s
    return twice * c, 1.0 - twice * s


def three_parts(x):
    first = x.astype(BF16)
    rest = x - first.astype(F32)
    second = rest.astype(BF16)
    third = (rest - second.astype(F32)).astype(BF16)
    return first, second, third


def two_parts(x):
    first = x.astype(BF16)
    return first, (x - first.astype(F32)).astype(BF16)


def exchange_steps(count):
    bits = [1 << b for b in range(count.bit_length() - 2, 0, -1)]
    swapped = bits[:-2] + bits[-2:][::-1] if len(bits) >= 2 else bits
    return [b | 1 for b in bits], [b | 1 for b in swapped]


def relative_places(steps):
    places = [0]
    for step in steps:
        places = places + [p ^ step for p in places]
    return places


def iota(shape, axis):
    return lax.broadcasted_iota(jnp.int32, shape, axis)


def geom_lane(cpd):
    return 3 * PARTS * (QN // cpd)


def place_matrices(cpd):
    groups = QN // cpd
    shape = (LANES, 2 * 16)
    begin, row = iota(shape, 0), iota(shape, 1)
    node = jnp.logical_and(begin >= row * groups, begin < (row + 1) * groups)
    node = jnp.logical_and(node, row < 3 * PARTS)
    source = jnp.logical_and(begin - geom_lane(cpd) == row - 16, row >= 16)
    row_of = jnp.where(jnp.logical_or(node, source), 1.0, 0.0).astype(BF16)
    shape = (LANES, QN)
    lane, group = iota(shape, 0), lax.div(iota(shape, 1), cpd)
    wanted = jnp.where(lane < geom_lane(cpd), lax.rem(lane, groups), 0)
    kept = jnp.where(group == wanted, 1.0, 0.0)
    shape = (cpd, QN)
    column_of = jnp.where(lax.rem(iota(shape, 1), cpd) == iota(shape, 0), 1.0, 0.0).astype(BF16)
    return row_of, kept, column_of


def pack_kernel(
    units, order_hbm, geom_hbm, excite_hbm, nodes_hbm, weights_hbm, tnodes_hbm, tweights_hbm,
    out_ref, target_ref, tests_ref, found_ref,
    order_ref, geom_ref, excite_ref, nodes_ref, weights_ref, tnodes_ref, arrived,
):
    col = lax.axis_index("col")
    rows = tests_ref.shape[2]
    at = pl.ds(pl.multiple_of(col * rows, LANES), rows)
    moves = [
        (weights_hbm, weights_ref),
        (nodes_hbm, nodes_ref),
        (geom_hbm, geom_ref),
        (excite_hbm, excite_ref),
        (tnodes_hbm, tnodes_ref),
        (order_hbm, order_ref),
        (tweights_hbm.at[:, :, at], tests_ref),
    ]
    copies = [pltpu.make_async_copy(*move, arrived.at[i]) for i, move in enumerate(moves)]
    for copy in copies:
        copy.start()
    cpd, exc = excite_ref.shape
    row_of, kept, column_of = place_matrices(cpd)
    for copy in copies[:-1]:
        copy.wait()
    main = LANES
    rest = QN - main
    re, im = weights_ref[0], weights_ref[1]
    out_ref[:, 0:main] = re[:, :main]
    out_ref[:, main : 2 * main] = im[:, :main]
    out_ref[:, 2 * main : 2 * main + 2 * rest] = jnp.concatenate([re[:, main:], im[:, main:]], 1)
    out_ref[:, EXC_AT : EXC_AT + exc] = excite_ref[...]
    nodes = [p.astype(F32) for p in three_parts(nodes_ref[...])]
    geom = jnp.concatenate([p.astype(F32) for p in three_parts(geom_ref[...])], 0)
    values = jnp.concatenate(
        nodes
        + [
            jnp.zeros((16 - 3 * PARTS, QN), F32),
            jnp.concatenate([geom, jnp.zeros((geom.shape[0], QN - cpd), F32)], 1),
            jnp.zeros((16 - geom.shape[0], QN), F32),
        ],
        0,
    ).astype(BF16)
    spread = (dot(row_of, values) * kept).astype(BF16)
    out_ref[:, EXC_AT + exc :] = dot(column_of, spread, NT).astype(BF16)
    nodes = tnodes_ref[:, :QN]
    for b in range(1, tnodes_ref.shape[1] // QN):
        nodes = jnp.where(col == b, tnodes_ref[:, b * QN : (b + 1) * QN], nodes)
    end = nodes[:, LANES:]
    start = nodes[:, :QSTEP]
    target_ref[0, 0:3] = nodes[:, :LANES]
    target_ref[1, 0:3] = jnp.concatenate([end, end], 1)
    target_ref[2, 0:3] = jnp.concatenate([start, start], 1)
    for slot, order in enumerate(slot_orders(order_ref, units)):
        found_ref[slot] = order
    copies[-1].wait()


def store_tests(tests_ref, ut_ref):
    re, im = tests_ref[0], tests_ref[1]
    main = LANES
    ut_ref[0:main, :] = jnp.concatenate([re[:main], im[:main]], 1)
    ut_ref[main : 2 * main, :] = jnp.concatenate([-im[:main], re[:main]], 1)
    ut_ref[2 * main : 2 * main + QSTEP, :] = jnp.concatenate([re[main:], im[main:]], 1)
    ut_ref[2 * main + QSTEP :, :] = jnp.concatenate([-im[main:], re[main:]], 1)


def node_columns(data_ref, exc):
    block = data_ref[:, EXC_AT + exc :].astype(F32)
    step = geom_lane(16) // PARTS
    return (block[:, :step] + block[:, step : 2 * step]) + block[:, 2 * step : 3 * step]


def two_part_dot(high, low, right):
    count = high.shape[0]
    both = dot(jnp.concatenate([high, low], 0), right)
    return both[:count] + both[count:]


def near_slot(order, columns, slot, target_ref, ut_ref, turns, out_ref):
    lane = lax.broadcasted_iota(jnp.int32, (1, LANES), 1)
    quarter = jnp.where(lane < QSTEP, 0.0, 0.25)
    main = LANES

    def located(count):
        return [
            jnp.concatenate(
                [
                    jnp.broadcast_to(columns[16 * slot : 16 * slot + 16, lane : lane + 1], (16, LANES))
                    for lane in range(axis * (QN // 16), axis * (QN // 16) + count // 16)
                ],
                0,
            )
            for axis in range(3)
        ]

    def distance2(source, tile):
        total = SOFT * SOFT
        for axis in range(3):
            d = source[axis] - target_ref[tile, axis : axis + 1, :]
            total = total + d * d
        return total

    def both(source):
        d2 = distance2(source, 0)
        inv = lax.rsqrt(d2)
        t = (d2 * inv) * turns
        sin, cos = sincos_turns(t - jnp.round(t))
        return two_parts(inv * cos), two_parts(inv * sin)

    def split_lanes(source, tile):
        d2 = distance2(source, tile)
        inv = lax.rsqrt(d2)
        t = (d2 * inv) * turns
        f = (t - jnp.round(t - quarter)) - quarter
        return two_parts(inv * polynomial(f * f, COS_FULL))

    def put(at, value):
        high, low = two_parts(value)
        count = value.shape[0]
        out_ref[at : at + count, :LANES] = high
        out_ref[at : at + count, LANES:] = low

    def clear(begin, end):
        out_ref[begin:end, :] = jnp.zeros((end - begin, 2 * LANES), BF16)

    @pl.when(order == 3)
    def _():
        source = located(QN)
        (re_high, re_low), (im_high, im_low) = both(source)
        rest_high, rest_low = split_lanes(source, 1)
        high = jnp.concatenate([re_high, im_high, rest_high], 1)
        low = jnp.concatenate([re_low, im_low, rest_low], 1)
        v = two_part_dot(high, low, ut_ref[...])
        put(0, v[:main, :LANES])
        put(main, v[:main, LANES:])
        put(2 * main, v[main:, :LANES])
        put(2 * main + QSTEP, v[main:, LANES:])

    @pl.when(order == 2)
    def _():
        (re_high, re_low), (im_high, im_low) = both(located(main))
        high = jnp.concatenate([re_high, im_high], 1)
        low = jnp.concatenate([re_low, im_low], 1)
        v = two_part_dot(high, low, ut_ref[: 2 * main])
        put(0, v[:, :LANES])
        put(main, v[:, LANES:])
        clear(2 * main, 3 * main)

    @pl.when(order == 1)
    def _():
        high, low = split_lanes(located(QSTEP), 2)
        weights = jnp.concatenate([ut_ref[0:QSTEP], ut_ref[main : main + QSTEP]], 0)
        v = two_part_dot(high, low, weights)
        put(0, v[:, :LANES])
        clear(QSTEP, main)
        put(main, v[:, LANES:])
        clear(main + QSTEP, 3 * main)

    @pl.when(order == 0)
    def _():
        clear(0, 3 * main)


def slot_orders(order_ref, units):
    row, col = lax.axis_index("row"), lax.axis_index("col")
    nrow = lax.axis_size("row")
    band = order_ref.shape[1]
    reach = (band - 1) // 2
    if units is None:
        offsets = [jnp.where(jnp.logical_and(row + o >= reach, row + o - reach < nrow), o, -1) for o in range(band)]
    else:
        place, parity = row * lax.axis_size("col") + col, 0
        for _ in range((nrow * lax.axis_size("col")).bit_length() - 1):
            parity = parity + lax.rem(place, 2)
            place = lax.div(place, 2)
        parity = lax.rem(parity, 2)
        offsets = [
            (row ^ (a if a == b else jnp.where(parity == 0, a, b))) - row + reach for a, b in zip(*units)
        ]
    return [
        jnp.where(
            jnp.logical_and(o >= 0, o < band), order_ref[col, jnp.clip(o, 0, band - 1)], 0
        )
        for o in offsets
    ]


def far_kernel_values(wave, source, tgeom):
    dx = tgeom[0:1] - source[0]
    dy = tgeom[1:2] - source[1]
    dz = tgeom[2:3] - source[2]
    d2 = dx * dx + dy * dy + dz * dz + SOFT * SOFT
    inv = lax.rsqrt(d2)
    radius = d2 * inv
    cosine = (tgeom[3:4] * dx + tgeom[4:5] * dy + tgeom[5:6] * dz) * inv
    scale = source[3] * (INV_FOUR_PI * inv)
    phase = wave * radius
    t = phase * INV_TURN
    n = jnp.round(t)
    sin, cos = sincos_turns(((phase - n * TURN_HIGH) - n * TURN_LOW) * INV_TURN)
    green_re = scale * cos
    green_im = scale * sin
    factor_re = 1.0 - cosine
    factor_im = cosine * (inv * (-1.0 / wave))
    kern_re = (green_re * factor_re - green_im * factor_im).astype(BF16)
    kern_im = (green_re * factor_im + green_im * factor_re).astype(BF16)
    return kern_re, kern_im


def far_rows(data, exc, wave, tgeom):
    shape = (LANES, 4 * LANES)
    at, wanted = iota(shape, 0) - geom_lane(16), lax.div(iota(shape, 1), LANES)
    pick = jnp.logical_and(
        jnp.logical_and(at >= 0, at < 4 * PARTS), lax.rem(at + 4 * LANES, 4) == wanted
    )
    geom = data[:, EXC_AT + exc :]
    spread = dot(geom, jnp.where(pick, 1.0, 0.0).astype(BF16))
    return far_kernel_values(wave, [spread[:, i * LANES : (i + 1) * LANES] for i in range(4)], tgeom)


def own_targets(tgeom_ref, rows):
    at = pl.multiple_of(lax.axis_index("col") * rows, LANES)
    return tgeom_ref[:, pl.ds(at, rows)]


def near_kernel(
    exc, first, wave_ref, found_ref, data_ref, own_ref, target_ref, ut_ref, tgeom_ref,
    v_ref, kern_re_ref, kern_im_ref, *copy_ref,
):
    if copy_ref:
        copy_ref[0][...] = own_ref[...]
    wave = wave_ref[0]
    tgeom = own_targets(tgeom_ref, kern_re_ref.shape[1])
    data = data_ref[...]
    if kern_re_ref.shape[0] > data.shape[0]:
        data = jnp.concatenate([own_ref[...], data], 0)
    kern_re_ref[...], kern_im_ref[...] = far_rows(data, exc, wave, tgeom)
    slots = v_ref.shape[0]
    skipped = data_ref.shape[0] // 16 - slots
    columns = node_columns(data_ref, exc)
    for slot in range(slots):
        near_slot(
            found_ref[first + slot], columns, skipped + slot, target_ref, ut_ref, wave * INV_TURN, v_ref.at[slot]
        )


def first_near_kernel(
    exc, first, wave_ref, found_ref, data_ref, own_ref, target_ref, tests_ref, tgeom_ref, *refs
):
    *refs, ut_ref = refs
    store_tests(tests_ref, ut_ref)
    near_kernel(exc, first, wave_ref, found_ref, data_ref, own_ref, target_ref, ut_ref, tgeom_ref, *refs)


def weight_rows(data):
    sign = jnp.where(iota((1, LANES), 1) < QSTEP, 1.0, -1.0).astype(BF16)
    w = [data[:, i * LANES : (i + 1) * LANES] for i in range(3)]
    swapped = jnp.concatenate([w[2][:, QSTEP:], w[2][:, :QSTEP]], 1)
    return jnp.concatenate([w[0], -w[1], w[2] * sign], 1), jnp.concatenate([w[1], w[0], swapped], 1)


def near_rows(left, v):
    product = dot(left, v)
    return (product[:, :LANES] + product[:, LANES:]) * INV_FOUR_PI


def known_kernel(own_ref, fresh_ref, other_first, other_early, *refs):
    *v_refs, out_ref = refs
    cpd = 16
    pairs = [(own_ref, other_first), (fresh_ref, other_early)]
    v = [ref[i] for ref in v_refs for i in range(ref.shape[0])]
    rows = []
    for own_half, other_half in pairs:
        other_re, other_im = weight_rows(other_half[...])
        own_re, own_im = weight_rows(own_half[: other_half.shape[0]])
        for k in range(other_half.shape[0] // cpd):
            here = slice(k * cpd, (k + 1) * cpd)
            rows.append(jnp.concatenate([own_re[here], other_re[here], own_im[here], other_im[here]], 0))
    for k, left in enumerate(rows):
        out_ref[k] = near_rows(left, v[k])


def last_kernel(
    exc, partner, wave_ref, own_early, own_late, other_first, other_early, other_late, tgeom_ref,
    known_ref, early_re_ref, early_im_ref, *refs
):
    own = jnp.concatenate([own_early[...], own_late[...]], 0)
    other = jnp.concatenate([other_first[...], other_early[...], other_late[...]], 0)
    out_ref, zre, zim = refs[-3:]
    *made, early_v, late_v, late_re, late_im = refs[:-3]
    v_refs = [*made[::3], early_v, late_v]
    kern_re_refs, kern_im_refs = [*made[1::3], late_re], [*made[2::3], late_im]
    rows = out_ref.shape[0]
    cpd = 16
    main = LANES
    slots = len(partner)
    quarter = slots // 4
    known = [*range(quarter), *range(2 * quarter, 3 * quarter)]
    own_re, own_im = weight_rows(own)
    other_re, other_im = weight_rows(other)
    slot = 0
    for v_ref in v_refs:
        for i in range(v_ref.shape[0]):
            here = slice(slot * cpd, (slot + 1) * cpd)
            there = slice(partner[slot] * cpd, (partner[slot] + 1) * cpd)
            if slot in known:
                a = known_ref[known.index(slot)]
            else:
                left = jnp.concatenate([own_re[here], other_re[there], own_im[here], other_im[there]], 0)
                a = near_rows(left, v_ref[i])
            there = slice((slots + partner[slot]) * cpd, (slots + partner[slot] + 1) * cpd)
            zre[here] = a[0:cpd]
            zre[there] = a[cpd : 2 * cpd]
            zim[here] = a[2 * cpd : 3 * cpd]
            zim[there] = a[3 * cpd :]
            slot += 1

    late_kern = far_rows(other_late, exc, wave_ref[0], own_targets(tgeom_ref, rows))
    first = other_first.shape[0]
    kern_re, kern_im = [
        jnp.concatenate(
            [*[ref[...] for ref in refs[:-2]], refs[-2][first:], refs[-1][...], refs[-2][:first], early[...], x], 0
        ).astype(F32)
        for refs, early, x in zip((kern_re_refs, kern_im_refs), (early_re_ref, early_im_ref), late_kern)
    ]
    excite = jnp.concatenate(
        [own[:, EXC_AT : EXC_AT + exc], other[:, EXC_AT : EXC_AT + exc]], 0
    ).T
    re = two_parts(kern_re + zre[...])
    im = two_parts(kern_im + zim[...])
    product = dot(excite, jnp.concatenate([*re, *im], 1))
    by_re = product[:, :rows] + product[:, rows : 2 * rows]
    by_im = product[:, 2 * rows : 3 * rows] + product[:, 3 * rows :]
    h = exc // 2
    result = jnp.concatenate([by_re[:h] - by_im[h:], by_re[h:] + by_im[:h]], 0)
    out_ref[...] = result.T


def in_vmem(x):
    return pltpu.with_memory_space_constraint(x, pltpu.VMEM)


def in_smem(x):
    return pltpu.with_memory_space_constraint(x, pltpu.SMEM)


def in_hbm(x):
    return pltpu.with_memory_space_constraint(x, pltpu.HBM)


SMEM_SPEC = pl.BlockSpec(memory_space=pltpu.SMEM)
VMEM_SPEC = pl.BlockSpec(memory_space=pltpu.VMEM)


def packed(units, slots, src_geom, excite, src_nodes, src_weights, tgt_nodes, tgt_weights, near_order):
    excite = excite.T
    src_weights = src_weights.transpose(0, 2, 1)
    cpd, exc = excite.shape
    rows_here = tgt_weights.shape[2] // lax.axis_size("col")
    inputs = (near_order, src_geom, excite, src_nodes, src_weights, tgt_nodes)
    return pl.pallas_call(
        functools.partial(pack_kernel, units),
        out_shape=[
            pltpu.VMEM((cpd, EXC_AT + exc + NODE_WIDTH), BF16),
            pltpu.VMEM((3, 8, LANES), F32),
            pltpu.VMEM((2, QN, rows_here), BF16),
            pltpu.SMEM((slots,), jnp.int32),
        ],
        in_specs=[pl.BlockSpec(memory_space=pl.ANY)] * 7,
        out_specs=[VMEM_SPEC] * 3 + [SMEM_SPEC],
        scratch_shapes=[pltpu.SMEM(near_order.shape, jnp.int32)]
        + [pltpu.VMEM(x.shape, x.dtype) for x in inputs[1:]]
        + [pltpu.SemaphoreType.DMA((7,))],
        compiler_params=SMALL,
    )(*[in_hbm(x) for x in inputs], in_hbm(tgt_weights))


def near_blocks(exc, first, slots, wavenumber, found, fresh, own, target, ut, tgt_geom, hand_on, both=False):
    rows_here = tgt_geom.shape[1] // lax.axis_size("col")
    kern = pltpu.VMEM((fresh.shape[0] + both * own.shape[0], rows_here), BF16)
    cost = pl.CostEstimate(flops=1, bytes_accessed=1, transcendentals=0)
    outs = [pltpu.VMEM((slots, 2 * QN, 2 * LANES), BF16), kern, kern] + [pltpu.VMEM(own.shape, BF16)] * hand_on
    if first == 0:
        outs.append(pltpu.VMEM((2 * QN, 2 * LANES), BF16))
    return pl.pallas_call(
        functools.partial(near_kernel if first else first_near_kernel, exc, first),
        out_shape=outs,
        in_specs=[SMEM_SPEC] * 2 + [VMEM_SPEC] * 5,
        out_specs=[VMEM_SPEC] * len(outs),
        compiler_params=SMALL,
        cost_estimate=cost,
    )(wavenumber, in_smem(found), in_vmem(fresh), in_vmem(own), in_vmem(target), in_vmem(ut), in_vmem(tgt_geom))


def exchanged(
    wavenumber, tgt_geom, src_geom, excite, tgt_nodes, src_nodes, tgt_weights, src_weights, near_order
):
    cpd = src_geom.shape[1]
    exc = excite.shape[0]
    cores = lax.axis_size("col")
    count = cores * lax.axis_size("row")
    rows_here = tgt_geom.shape[1] // cores
    even, odd = exchange_steps(count)
    units = [[p >> 1 for p in relative_places(s)] for s in (even, odd)]
    own, target, ut, found = packed(
        units, len(units[0]), src_geom, excite, src_nodes, src_weights, tgt_nodes, tgt_weights, near_order
    )

    def moved(value, a, b):
        pairs = [(i, i ^ (b if bin(i).count("1") % 2 else a)) for i in range(count)]
        return lax.ppermute(value, ("row", "col"), pairs)

    fresh = own
    near = []
    done = 0
    steps = list(zip(even, odd))
    for step, (a, b) in enumerate(steps):
        arriving = moved(own, a, b)
        slots = fresh.shape[0] // cpd
        last = step == len(steps) - 1
        made = near_blocks(
            exc, done, slots, wavenumber, found, fresh, other_first if last else own, target, ut, tgt_geom,
            not last, last,
        )
        near.extend(made[:3])
        if not done:
            ut = made[4]
        if step == len(steps) - 2:
            other_first = moved(made[3], 1, 1)
        done += slots
        fresh = arriving
        if not last:
            own = jnp.concatenate([made[3], arriving], 0)
        if step == len(steps) - 2:
            own, other_first = lax.optimization_barrier((own, other_first))
    half = own.shape[0] // 2
    other_early = moved(own[half:], 1, 1)
    quarter = half // cpd
    early = near_blocks(
        exc, done, quarter, wavenumber, found, other_early, other_early, target, ut, tgt_geom, False
    )
    fresh, early, made = lax.optimization_barrier((fresh, early, made))
    other_late = moved(fresh, 1, 1)
    late = near_blocks(
        exc, done + quarter, quarter, wavenumber, found, fresh, fresh, target, ut, tgt_geom, False
    )
    near.append(early[0])
    near.extend(late)
    firsts = [v for v in near[: 3 * (len(steps) - 1) : 3]]
    known = pl.pallas_call(
        known_kernel,
        out_shape=pltpu.VMEM((2 * quarter, 4 * cpd, rows_here), F32),
        in_specs=[VMEM_SPEC] * (5 + len(firsts)),
        out_specs=VMEM_SPEC,
        compiler_params=SMALL,
        cost_estimate=pl.CostEstimate(flops=1, bytes_accessed=1, transcendentals=0),
    )(*[in_vmem(x) for x in (own, fresh, other_first, other_early, *firsts, early[0])])
    partner = [units[1].index(u) for u in units[0]]
    return pl.pallas_call(
        functools.partial(last_kernel, exc, partner),
        out_shape=jax.ShapeDtypeStruct((rows_here, exc), F32),
        in_specs=[SMEM_SPEC] + [VMEM_SPEC] * (9 + len(near)),
        out_specs=VMEM_SPEC,
        scratch_shapes=[pltpu.VMEM((count * cpd, rows_here), F32)] * 2,
        compiler_params=SMALL,
    )(
        wavenumber,
        *[in_vmem(x) for x in (own, fresh, other_first, other_early, other_late, tgt_geom, known, *early[1:], *near)],
    )


def gathered(
    wavenumber, tgt_geom, src_geom, excite, tgt_nodes, src_nodes, tgt_weights, src_weights, near_order
):
    cpd = src_geom.shape[1]
    exc = excite.shape[0]
    half = exc // 2
    cores = lax.axis_size("col")
    nrow = lax.axis_size("row")
    row = lax.axis_index("row")
    rows_here = tgt_geom.shape[1] // cores
    band = near_order.shape[1]
    own, target, ut, found = packed(
        None, band, src_geom, excite, src_nodes, src_weights, tgt_nodes, tgt_weights, near_order
    )
    everything = lax.all_gather(own, ("row", "col"), axis=0, tiled=True)
    sources = lax.all_gather(src_geom, ("row", "col"), axis=1, tiled=True)
    blocks = [
        lax.dynamic_slice_in_dim(
            everything, jnp.clip(row + o - (band - 1) // 2, 0, nrow - 1) * cores * cpd, cores * cpd, 0
        )
        for o in range(band)
    ]
    fresh = jnp.concatenate([block[:cpd] for block in blocks], 0)
    near = near_blocks(exc, 0, band, wavenumber, found, fresh, own, target, ut, tgt_geom, False)[0]
    high = lax.Precision.HIGHEST
    total = jnp.zeros((rows_here, exc), F32)
    dims = (((0,), (0,)), ((), ()))
    m, r = LANES, QN - LANES
    for o, block in enumerate(blocks):
        w, x = block[:, :EXC_AT].astype(F32), block[:, EXC_AT : EXC_AT + exc].astype(F32)
        v = near[o, :, :LANES].astype(F32) + near[o, :, LANES:].astype(F32)
        w_re = jnp.concatenate([w[:, :m], w[:, 2 * m : 2 * m + r]], 1)
        w_im = jnp.concatenate([w[:, m : 2 * m], w[:, 2 * m + r :]], 1)
        v_re = jnp.concatenate([v[:m], v[2 * m : 2 * m + r]], 0)
        v_im = jnp.concatenate([v[m : 2 * m], v[2 * m + r :]], 0)
        a_re = jnp.dot(w_re, v_re, precision=high) - jnp.dot(w_im, v_im, precision=high)
        a_im = jnp.dot(w_re, v_im, precision=high) + jnp.dot(w_im, v_re, precision=high)
        re = lax.dot_general(a_re, x, dims, precision=high)
        im = lax.dot_general(a_im, x, dims, precision=high)
        total = total + INV_FOUR_PI * jnp.concatenate(
            [re[:, :half] - im[:, half:], re[:, half:] + im[:, :half]], 1
        )
    targets = lax.dynamic_slice_in_dim(tgt_geom, lax.axis_index("col") * rows_here, rows_here, 1)
    width = math.gcd(everything.shape[0], 512)

    def far(index, accum):
        places = lax.dynamic_slice_in_dim(sources, index * width, width, 1)
        x = lax.dynamic_slice_in_dim(everything, index * width, width, 0)[:, EXC_AT : EXC_AT + exc]
        kern_re, kern_im = far_kernel_values(
            wavenumber[0], [places[i][:, None] for i in range(4)], targets
        )
        re = lax.dot_general(kern_re.astype(BF16), x, dims, preferred_element_type=F32)
        im = lax.dot_general(kern_im.astype(BF16), x, dims, preferred_element_type=F32)
        return accum + jnp.concatenate([re[:, :half] - im[:, half:], re[:, half:] + im[:, :half]], 1)

    return lax.fori_loop(0, everything.shape[0] // width, far, total)


def on_device(*arguments):
    count = lax.axis_size("row") * lax.axis_size("col")
    short = lax.axis_size("col") == 2 and lax.axis_size("row") <= 16 and count & (count - 1) == 0
    return (exchanged if short and count >= 8 else gathered)(*arguments)


def solution(mesh):
    return jax.shard_map(
        on_device,
        mesh=mesh,
        in_specs=(
            P("groups"),
            P(None, ("groups", "row")),
            P(None, ("groups", "row", "col")),
            P(None, ("groups", "row", "col")),
            P(None, ("groups", "row")),
            P(None, ("groups", "row")),
            P(None, None, ("groups", "row")),
            P(None, None, ("groups", "row", "col")),
            P(("groups", "row"), None),
        ),
        out_specs=P(("groups", "row", "col"), None),
        check_vma=False,
    )
```

```python
import functools
import math

import jax
import jax.numpy as jnp
from jax import lax
from jax.experimental import pallas as pl
from jax.experimental.pallas import tpu as pltpu
from jax.sharding import PartitionSpec as P

QSTEP = 64
QN = 192
LANES = 128
PARTS = 3
SOFT = 0.05
INV_FOUR_PI = 1.0 / (4.0 * math.pi)
INV_TURN = 1.0 / (2.0 * math.pi)
TURN_HIGH = 6.28125
TURN_LOW = 2.0 * math.pi - TURN_HIGH
SIN_HALF = (3.14159264, -5.16771009, 2.55007766, -0.59829216, 0.07765941)
COS_HALF = (1.0, -4.93480214, 4.05870916, -1.33521206, 0.23493756, -0.02439672)
COS_FULL = (
    0.99999999, -19.73920453, 64.93911898, -85.45016555, 60.16783171, -25.96831321, 6.52961029
)
BF16 = jnp.bfloat16
F32 = jnp.float32
NN = (((1,), (0,)), ((), ()))
NT = (((1,), (1,)), ((), ()))
EXC_AT = 2 * QN
NODE_WIDTH = LANES
SMALL = pltpu.CompilerParams(vmem_limit_bytes=24 * 2**20)


def dot(left, right, dims=NN):
    return lax.dot_general(left, right, dims, preferred_element_type=F32)


def polynomial(z, coefficients):
    total = coefficients[-1]
    for c in coefficients[-2::-1]:
        total = total * z + c
    return total


def sincos_turns(f):
    z = f * f
    s = f * polynomial(z, SIN_HALF)
    c = polynomial(z, COS_HALF)
    twice = s + s
    return twice * c, 1.0 - twice * s


def three_parts(x):
    first = x.astype(BF16)
    rest = x - first.astype(F32)
    second = rest.astype(BF16)
    third = (rest - second.astype(F32)).astype(BF16)
    return first, second, third


def two_parts(x):
    first = x.astype(BF16)
    return first, (x - first.astype(F32)).astype(BF16)


def exchange_steps(count):
    bits = [1 << b for b in range(count.bit_length() - 2, 0, -1)]
    swapped = bits[:-2] + bits[-2:][::-1] if len(bits) >= 2 else bits
    return [b | 1 for b in bits], [b | 1 for b in swapped]


def relative_places(steps):
    places = [0]
    for step in steps:
        places = places + [p ^ step for p in places]
    return places


def iota(shape, axis):
    return lax.broadcasted_iota(jnp.int32, shape, axis)


def geom_lane(cpd):
    return 3 * PARTS * (QN // cpd)


def place_matrices(cpd):
    groups = QN // cpd
    shape = (LANES, 2 * 16)
    begin, row = iota(shape, 0), iota(shape, 1)
    node = jnp.logical_and(begin >= row * groups, begin < (row + 1) * groups)
    node = jnp.logical_and(node, row < 3 * PARTS)
    source = jnp.logical_and(begin - geom_lane(cpd) == row - 16, row >= 16)
    row_of = jnp.where(jnp.logical_or(node, source), 1.0, 0.0).astype(BF16)
    shape = (LANES, QN)
    lane, group = iota(shape, 0), lax.div(iota(shape, 1), cpd)
    wanted = jnp.where(lane < geom_lane(cpd), lax.rem(lane, groups), 0)
    kept = jnp.where(group == wanted, 1.0, 0.0)
    shape = (cpd, QN)
    column_of = jnp.where(lax.rem(iota(shape, 1), cpd) == iota(shape, 0), 1.0, 0.0).astype(BF16)
    return row_of, kept, column_of


def pack_kernel(
    units, order_hbm, geom_hbm, excite_hbm, nodes_hbm, weights_hbm, tnodes_hbm, tweights_hbm,
    out_ref, target_ref, tests_ref, found_ref,
    order_ref, geom_ref, excite_ref, nodes_ref, weights_ref, tnodes_ref, arrived,
):
    col = lax.axis_index("col")
    rows = tests_ref.shape[2]
    at = pl.ds(pl.multiple_of(col * rows, LANES), rows)
    moves = [
        (weights_hbm, weights_ref),
        (nodes_hbm, nodes_ref),
        (geom_hbm, geom_ref),
        (excite_hbm, excite_ref),
        (tnodes_hbm, tnodes_ref),
        (order_hbm, order_ref),
        (tweights_hbm.at[:, :, at], tests_ref),
    ]
    copies = [pltpu.make_async_copy(*move, arrived.at[i]) for i, move in enumerate(moves)]
    for copy in copies:
        copy.start()
    cpd, exc = excite_ref.shape
    row_of, kept, column_of = place_matrices(cpd)
    for copy in copies[:-1]:
        copy.wait()
    main = LANES
    rest = QN - main
    re, im = weights_ref[0], weights_ref[1]
    out_ref[:, 0:main] = re[:, :main]
    out_ref[:, main : 2 * main] = im[:, :main]
    out_ref[:, 2 * main : 2 * main + 2 * rest] = jnp.concatenate([re[:, main:], im[:, main:]], 1)
    out_ref[:, EXC_AT : EXC_AT + exc] = excite_ref[...]
    nodes = [p.astype(F32) for p in three_parts(nodes_ref[...])]
    geom = jnp.concatenate([p.astype(F32) for p in three_parts(geom_ref[...])], 0)
    values = jnp.concatenate(
        nodes
        + [
            jnp.zeros((16 - 3 * PARTS, QN), F32),
            jnp.concatenate([geom, jnp.zeros((geom.shape[0], QN - cpd), F32)], 1),
            jnp.zeros((16 - geom.shape[0], QN), F32),
        ],
        0,
    ).astype(BF16)
    spread = (dot(row_of, values) * kept).astype(BF16)
    out_ref[:, EXC_AT + exc :] = dot(column_of, spread, NT).astype(BF16)
    nodes = tnodes_ref[:, :QN]
    for b in range(1, tnodes_ref.shape[1] // QN):
        nodes = jnp.where(col == b, tnodes_ref[:, b * QN : (b + 1) * QN], nodes)
    end = nodes[:, LANES:]
    start = nodes[:, :QSTEP]
    target_ref[0, 0:3] = nodes[:, :LANES]
    target_ref[1, 0:3] = jnp.concatenate([end, end], 1)
    target_ref[2, 0:3] = jnp.concatenate([start, start], 1)
    for slot, order in enumerate(slot_orders(order_ref, units)):
        found_ref[slot] = order
    copies[-1].wait()


def store_tests(tests_ref, ut_ref):
    re, im = tests_ref[0], tests_ref[1]
    main = LANES
    ut_ref[0:main, :] = jnp.concatenate([re[:main], im[:main]], 1)
    ut_ref[main : 2 * main, :] = jnp.concatenate([-im[:main], re[:main]], 1)
    ut_ref[2 * main : 2 * main + QSTEP, :] = jnp.concatenate([re[main:], im[main:]], 1)
    ut_ref[2 * main + QSTEP :, :] = jnp.concatenate([-im[main:], re[main:]], 1)


def node_columns(data_ref, exc):
    block = data_ref[:, EXC_AT + exc :].astype(F32)
    step = geom_lane(16) // PARTS
    return (block[:, :step] + block[:, step : 2 * step]) + block[:, 2 * step : 3 * step]


def two_part_dot(high, low, right):
    count = high.shape[0]
    both = dot(jnp.concatenate([high, low], 0), right)
    return both[:count] + both[count:]


def near_slot(order, columns, slot, target_ref, ut_ref, turns, out_ref):
    lane = lax.broadcasted_iota(jnp.int32, (1, LANES), 1)
    quarter = jnp.where(lane < QSTEP, 0.0, 0.25)
    main = LANES

    def located(count):
        return [
            jnp.concatenate(
                [
                    jnp.broadcast_to(columns[16 * slot : 16 * slot + 16, lane : lane + 1], (16, LANES))
                    for lane in range(axis * (QN // 16), axis * (QN // 16) + count // 16)
                ],
                0,
            )
            for axis in range(3)
        ]

    def distance2(source, tile):
        total = SOFT * SOFT
        for axis in range(3):
            d = source[axis] - target_ref[tile, axis : axis + 1, :]
            total = total + d * d
        return total

    def both(source):
        d2 = distance2(source, 0)
        inv = lax.rsqrt(d2)
        t = (d2 * inv) * turns
        sin, cos = sincos_turns(t - jnp.round(t))
        return two_parts(inv * cos), two_parts(inv * sin)

    def split_lanes(source, tile):
        d2 = distance2(source, tile)
        inv = lax.rsqrt(d2)
        t = (d2 * inv) * turns
        f = (t - jnp.round(t - quarter)) - quarter
        return two_parts(inv * polynomial(f * f, COS_FULL))

    def put(at, value):
        high, low = two_parts(value)
        count = value.shape[0]
        out_ref[at : at + count, :LANES] = high
        out_ref[at : at + count, LANES:] = low

    def clear(begin, end):
        out_ref[begin:end, :] = jnp.zeros((end - begin, 2 * LANES), BF16)

    @pl.when(order == 3)
    def _():
        source = located(QN)
        (re_high, re_low), (im_high, im_low) = both(source)
        rest_high, rest_low = split_lanes(source, 1)
        high = jnp.concatenate([re_high, im_high, rest_high], 1)
        low = jnp.concatenate([re_low, im_low, rest_low], 1)
        v = two_part_dot(high, low, ut_ref[...])
        put(0, v[:main, :LANES])
        put(main, v[:main, LANES:])
        put(2 * main, v[main:, :LANES])
        put(2 * main + QSTEP, v[main:, LANES:])

    @pl.when(order == 2)
    def _():
        (re_high, re_low), (im_high, im_low) = both(located(main))
        high = jnp.concatenate([re_high, im_high], 1)
        low = jnp.concatenate([re_low, im_low], 1)
        v = two_part_dot(high, low, ut_ref[: 2 * main])
        put(0, v[:, :LANES])
        put(main, v[:, LANES:])
        clear(2 * main, 3 * main)

    @pl.when(order == 1)
    def _():
        high, low = split_lanes(located(QSTEP), 2)
        weights = jnp.concatenate([ut_ref[0:QSTEP], ut_ref[main : main + QSTEP]], 0)
        v = two_part_dot(high, low, weights)
        put(0, v[:, :LANES])
        clear(QSTEP, main)
        put(main, v[:, LANES:])
        clear(main + QSTEP, 3 * main)

    @pl.when(order == 0)
    def _():
        clear(0, 3 * main)


def slot_orders(order_ref, units):
    row, col = lax.axis_index("row"), lax.axis_index("col")
    nrow = lax.axis_size("row")
    band = order_ref.shape[1]
    reach = (band - 1) // 2
    if units is None:
        offsets = [jnp.where(jnp.logical_and(row + o >= reach, row + o - reach < nrow), o, -1) for o in range(band)]
    else:
        place, parity = row * lax.axis_size("col") + col, 0
        for _ in range((nrow * lax.axis_size("col")).bit_length() - 1):
            parity = parity + lax.rem(place, 2)
            place = lax.div(place, 2)
        parity = lax.rem(parity, 2)
        offsets = [
            (row ^ (a if a == b else jnp.where(parity == 0, a, b))) - row + reach for a, b in zip(*units)
        ]
    return [
        jnp.where(
            jnp.logical_and(o >= 0, o < band), order_ref[col, jnp.clip(o, 0, band - 1)], 0
        )
        for o in offsets
    ]


def far_kernel_values(wave, source, tgeom):
    dx = tgeom[0:1] - source[0]
    dy = tgeom[1:2] - source[1]
    dz = tgeom[2:3] - source[2]
    d2 = dx * dx + dy * dy + dz * dz + SOFT * SOFT
    inv = lax.rsqrt(d2)
    radius = d2 * inv
    cosine = (tgeom[3:4] * dx + tgeom[4:5] * dy + tgeom[5:6] * dz) * inv
    scale = source[3] * (INV_FOUR_PI * inv)
    phase = wave * radius
    t = phase * INV_TURN
    n = jnp.round(t)
    sin, cos = sincos_turns(((phase - n * TURN_HIGH) - n * TURN_LOW) * INV_TURN)
    green_re = scale * cos
    green_im = scale * sin
    factor_re = 1.0 - cosine
    factor_im = cosine * (inv * (-1.0 / wave))
    kern_re = (green_re * factor_re - green_im * factor_im).astype(BF16)
    kern_im = (green_re * factor_im + green_im * factor_re).astype(BF16)
    return kern_re, kern_im


def far_rows(data, exc, wave, tgeom):
    shape = (LANES, 4 * LANES)
    at, wanted = iota(shape, 0) - geom_lane(16), lax.div(iota(shape, 1), LANES)
    pick = jnp.logical_and(
        jnp.logical_and(at >= 0, at < 4 * PARTS), lax.rem(at + 4 * LANES, 4) == wanted
    )
    geom = data[:, EXC_AT + exc :]
    spread = dot(geom, jnp.where(pick, 1.0, 0.0).astype(BF16))
    return far_kernel_values(wave, [spread[:, i * LANES : (i + 1) * LANES] for i in range(4)], tgeom)


def own_targets(tgeom_ref, rows):
    at = pl.multiple_of(lax.axis_index("col") * rows, LANES)
    return tgeom_ref[:, pl.ds(at, rows)]


def near_kernel(
    exc, first, wave_ref, found_ref, data_ref, own_ref, target_ref, ut_ref, tgeom_ref,
    v_ref, kern_re_ref, kern_im_ref, *copy_ref,
):
    if copy_ref:
        copy_ref[0][...] = own_ref[...]
    wave = wave_ref[0]
    tgeom = own_targets(tgeom_ref, kern_re_ref.shape[1])
    data = data_ref[...]
    if kern_re_ref.shape[0] > data.shape[0]:
        data = jnp.concatenate([own_ref[...], data], 0)
    kern_re_ref[...], kern_im_ref[...] = far_rows(data, exc, wave, tgeom)
    slots = v_ref.shape[0]
    skipped = data_ref.shape[0] // 16 - slots
    columns = node_columns(data_ref, exc)
    for slot in range(slots):
        near_slot(
            found_ref[first + slot], columns, skipped + slot, target_ref, ut_ref, wave * INV_TURN, v_ref.at[slot]
        )


def first_near_kernel(
    exc, first, wave_ref, found_ref, data_ref, own_ref, target_ref, tests_ref, tgeom_ref, *refs
):
    *refs, ut_ref = refs
    store_tests(tests_ref, ut_ref)
    near_kernel(exc, first, wave_ref, found_ref, data_ref, own_ref, target_ref, ut_ref, tgeom_ref, *refs)


def weight_rows(data):
    sign = jnp.where(iota((1, LANES), 1) < QSTEP, 1.0, -1.0).astype(BF16)
    w = [data[:, i * LANES : (i + 1) * LANES] for i in range(3)]
    swapped = jnp.concatenate([w[2][:, QSTEP:], w[2][:, :QSTEP]], 1)
    return jnp.concatenate([w[0], -w[1], w[2] * sign], 1), jnp.concatenate([w[1], w[0], swapped], 1)


def near_rows(left, v):
    product = dot(left, v)
    return (product[:, :LANES] + product[:, LANES:]) * INV_FOUR_PI


def known_kernel(own_ref, other_ref, *refs):
    *v_refs, out_ref = refs
    cpd = 16
    own_re, own_im = weight_rows(own_ref[: other_ref.shape[0]])
    other_re, other_im = weight_rows(other_ref[...])
    for k, v in enumerate([ref.at[i] for ref in v_refs for i in range(ref.shape[0])]):
        here = slice(k * cpd, (k + 1) * cpd)
        left = jnp.concatenate([own_re[here], other_re[here], own_im[here], other_im[here]], 0)
        out_ref[k] = near_rows(left, v[...])


def last_kernel(
    exc, partner, wave_ref, own_early, own_late, other_first, other_early, other_late, tgeom_ref,
    known_early, known_late, early_re_ref, early_im_ref, *refs
):
    own = jnp.concatenate([own_early[...], own_late[...]], 0)
    other = jnp.concatenate([other_first[...], other_early[...], other_late[...]], 0)
    out_ref, zre, zim = refs[-3:]
    *made, early_v, late_v, late_re, late_im = refs[:-3]
    v_refs = [*made[::3], early_v, late_v]
    kern_re_refs, kern_im_refs = [*made[1::3], late_re], [*made[2::3], late_im]
    rows = out_ref.shape[0]
    cpd = 16
    main = LANES
    slots = len(partner)
    quarter = slots // 4
    own_re, own_im = weight_rows(own)
    other_re, other_im = weight_rows(other)
    slot = 0
    for v_ref in v_refs:
        for i in range(v_ref.shape[0]):
            here = slice(slot * cpd, (slot + 1) * cpd)
            there = slice(partner[slot] * cpd, (partner[slot] + 1) * cpd)
            if slot // quarter in (0, 2):
                a = (known_late if slot // quarter else known_early)[slot % quarter]
            else:
                left = jnp.concatenate([own_re[here], other_re[there], own_im[here], other_im[there]], 0)
                a = near_rows(left, v_ref[i])
            there = slice((slots + partner[slot]) * cpd, (slots + partner[slot] + 1) * cpd)
            zre[here] = a[0:cpd]
            zre[there] = a[cpd : 2 * cpd]
            zim[here] = a[2 * cpd : 3 * cpd]
            zim[there] = a[3 * cpd :]
            slot += 1

    late_kern = far_rows(other_late, exc, wave_ref[0], own_targets(tgeom_ref, rows))
    first = other_first.shape[0]
    kern_re, kern_im = [
        jnp.concatenate(
            [*[ref[...] for ref in refs[:-2]], refs[-2][first:], refs[-1][...], refs[-2][:first], early[...], x], 0
        ).astype(F32)
        for refs, early, x in zip((kern_re_refs, kern_im_refs), (early_re_ref, early_im_ref), late_kern)
    ]
    excite = jnp.concatenate(
        [own[:, EXC_AT : EXC_AT + exc], other[:, EXC_AT : EXC_AT + exc]], 0
    ).T
    re = two_parts(kern_re + zre[...])
    im = two_parts(kern_im + zim[...])
    product = dot(excite, jnp.concatenate([*re, *im], 1))
    by_re = product[:, :rows] + product[:, rows : 2 * rows]
    by_im = product[:, 2 * rows : 3 * rows] + product[:, 3 * rows :]
    h = exc // 2
    result = jnp.concatenate([by_re[:h] - by_im[h:], by_re[h:] + by_im[:h]], 0)
    out_ref[...] = result.T


def in_vmem(x):
    return pltpu.with_memory_space_constraint(x, pltpu.VMEM)


def in_smem(x):
    return pltpu.with_memory_space_constraint(x, pltpu.SMEM)


def in_hbm(x):
    return pltpu.with_memory_space_constraint(x, pltpu.HBM)


SMEM_SPEC = pl.BlockSpec(memory_space=pltpu.SMEM)
VMEM_SPEC = pl.BlockSpec(memory_space=pltpu.VMEM)


def packed(units, slots, src_geom, excite, src_nodes, src_weights, tgt_nodes, tgt_weights, near_order):
    excite = excite.T
    src_weights = src_weights.transpose(0, 2, 1)
    cpd, exc = excite.shape
    rows_here = tgt_weights.shape[2] // lax.axis_size("col")
    inputs = (near_order, src_geom, excite, src_nodes, src_weights, tgt_nodes)
    return pl.pallas_call(
        functools.partial(pack_kernel, units),
        out_shape=[
            pltpu.VMEM((cpd, EXC_AT + exc + NODE_WIDTH), BF16),
            pltpu.VMEM((3, 8, LANES), F32),
            pltpu.VMEM((2, QN, rows_here), BF16),
            pltpu.SMEM((slots,), jnp.int32),
        ],
        in_specs=[pl.BlockSpec(memory_space=pl.ANY)] * 7,
        out_specs=[VMEM_SPEC] * 3 + [SMEM_SPEC],
        scratch_shapes=[pltpu.SMEM(near_order.shape, jnp.int32)]
        + [pltpu.VMEM(x.shape, x.dtype) for x in inputs[1:]]
        + [pltpu.SemaphoreType.DMA((7,))],
        compiler_params=SMALL,
    )(*[in_hbm(x) for x in inputs], in_hbm(tgt_weights))


def near_blocks(exc, first, slots, wavenumber, found, fresh, own, target, ut, tgt_geom, hand_on, both=False):
    rows_here = tgt_geom.shape[1] // lax.axis_size("col")
    kern = pltpu.VMEM((fresh.shape[0] + both * own.shape[0], rows_here), BF16)
    cost = pl.CostEstimate(flops=1, bytes_accessed=1, transcendentals=0)
    outs = [pltpu.VMEM((slots, 2 * QN, 2 * LANES), BF16), kern, kern] + [pltpu.VMEM(own.shape, BF16)] * hand_on
    if first == 0:
        outs.append(pltpu.VMEM((2 * QN, 2 * LANES), BF16))
    return pl.pallas_call(
        functools.partial(near_kernel if first else first_near_kernel, exc, first),
        out_shape=outs,
        in_specs=[SMEM_SPEC] * 2 + [VMEM_SPEC] * 5,
        out_specs=[VMEM_SPEC] * len(outs),
        compiler_params=SMALL,
        cost_estimate=cost,
    )(wavenumber, in_smem(found), in_vmem(fresh), in_vmem(own), in_vmem(target), in_vmem(ut), in_vmem(tgt_geom))


def exchanged(
    wavenumber, tgt_geom, src_geom, excite, tgt_nodes, src_nodes, tgt_weights, src_weights, near_order
):
    cpd = src_geom.shape[1]
    exc = excite.shape[0]
    cores = lax.axis_size("col")
    count = cores * lax.axis_size("row")
    rows_here = tgt_geom.shape[1] // cores
    even, odd = exchange_steps(count)
    units = [[p >> 1 for p in relative_places(s)] for s in (even, odd)]
    own, target, ut, found = packed(
        units, len(units[0]), src_geom, excite, src_nodes, src_weights, tgt_nodes, tgt_weights, near_order
    )

    def moved(value, a, b):
        pairs = [(i, i ^ (b if bin(i).count("1") % 2 else a)) for i in range(count)]
        return lax.ppermute(value, ("row", "col"), pairs)

    fresh = own
    near = []
    done = 0
    steps = list(zip(even, odd))
    for step, (a, b) in enumerate(steps):
        arriving = moved(own, a, b)
        slots = fresh.shape[0] // cpd
        last = step == len(steps) - 1
        made = near_blocks(
            exc, done, slots, wavenumber, found, fresh, other_first if last else own, target, ut, tgt_geom,
            not last, last,
        )
        near.extend(made[:3])
        if not done:
            ut = made[4]
        if step == len(steps) - 2:
            other_first = moved(own, 1, 1)
        done += slots
        fresh = arriving
        if not last:
            own = jnp.concatenate([made[3], arriving], 0)
        if step == len(steps) - 2:
            own, other_first = lax.optimization_barrier((own, other_first))
    half = own.shape[0] // 2
    other_early = moved(own[half:], 1, 1)
    quarter = half // cpd
    early = near_blocks(
        exc, done, quarter, wavenumber, found, other_early, other_early, target, ut, tgt_geom, False
    )

    def known_rows(mine, others, *v):
        return pl.pallas_call(
            known_kernel,
            out_shape=pltpu.VMEM((quarter, 4 * cpd, rows_here), F32),
            in_specs=[VMEM_SPEC] * (2 + len(v)),
            out_specs=VMEM_SPEC,
            compiler_params=SMALL,
            cost_estimate=pl.CostEstimate(flops=1, bytes_accessed=1, transcendentals=0),
        )(*[in_vmem(x) for x in (mine, others, *v)])

    known_early = known_rows(own, other_first, *near[: 3 * (len(steps) - 1) : 3])
    fresh, early, made, known_early = lax.optimization_barrier((fresh, early, made, known_early))
    other_late = moved(fresh, 1, 1)
    late = near_blocks(
        exc, done + quarter, quarter, wavenumber, found, fresh, fresh, target, ut, tgt_geom, False
    )
    near.append(early[0])
    near.extend(late)
    known_late = known_rows(fresh, other_early, early[0])
    partner = [units[1].index(u) for u in units[0]]
    return pl.pallas_call(
        functools.partial(last_kernel, exc, partner),
        out_shape=jax.ShapeDtypeStruct((rows_here, exc), F32),
        in_specs=[SMEM_SPEC] + [VMEM_SPEC] * (10 + len(near)),
        out_specs=VMEM_SPEC,
        scratch_shapes=[pltpu.VMEM((count * cpd, rows_here), F32)] * 2,
        compiler_params=SMALL,
    )(
        wavenumber,
        *[in_vmem(x) for x in (own, fresh, other_first, other_early, other_late, tgt_geom, known_early, known_late, *early[1:], *near)],
    )


def gathered(
    wavenumber, tgt_geom, src_geom, excite, tgt_nodes, src_nodes, tgt_weights, src_weights, near_order
):
    cpd = src_geom.shape[1]
    exc = excite.shape[0]
    half = exc // 2
    cores = lax.axis_size("col")
    nrow = lax.axis_size("row")
    row = lax.axis_index("row")
    rows_here = tgt_geom.shape[1] // cores
    band = near_order.shape[1]
    own, target, ut, found = packed(
        None, band, src_geom, excite, src_nodes, src_weights, tgt_nodes, tgt_weights, near_order
    )
    everything = lax.all_gather(own, ("row", "col"), axis=0, tiled=True)
    sources = lax.all_gather(src_geom, ("row", "col"), axis=1, tiled=True)
    blocks = [
        lax.dynamic_slice_in_dim(
            everything, jnp.clip(row + o - (band - 1) // 2, 0, nrow - 1) * cores * cpd, cores * cpd, 0
        )
        for o in range(band)
    ]
    fresh = jnp.concatenate([block[:cpd] for block in blocks], 0)
    near = near_blocks(exc, 0, band, wavenumber, found, fresh, own, target, ut, tgt_geom, False)[0]
    high = lax.Precision.HIGHEST
    total = jnp.zeros((rows_here, exc), F32)
    dims = (((0,), (0,)), ((), ()))
    m, r = LANES, QN - LANES
    for o, block in enumerate(blocks):
        w, x = block[:, :EXC_AT].astype(F32), block[:, EXC_AT : EXC_AT + exc].astype(F32)
        v = near[o, :, :LANES].astype(F32) + near[o, :, LANES:].astype(F32)
        w_re = jnp.concatenate([w[:, :m], w[:, 2 * m : 2 * m + r]], 1)
        w_im = jnp.concatenate([w[:, m : 2 * m], w[:, 2 * m + r :]], 1)
        v_re = jnp.concatenate([v[:m], v[2 * m : 2 * m + r]], 0)
        v_im = jnp.concatenate([v[m : 2 * m], v[2 * m + r :]], 0)
        a_re = jnp.dot(w_re, v_re, precision=high) - jnp.dot(w_im, v_im, precision=high)
        a_im = jnp.dot(w_re, v_im, precision=high) + jnp.dot(w_im, v_re, precision=high)
        re = lax.dot_general(a_re, x, dims, precision=high)
        im = lax.dot_general(a_im, x, dims, precision=high)
        total = total + INV_FOUR_PI * jnp.concatenate(
            [re[:, :half] - im[:, half:], re[:, half:] + im[:, :half]], 1
        )
    targets = lax.dynamic_slice_in_dim(tgt_geom, lax.axis_index("col") * rows_here, rows_here, 1)
    width = math.gcd(everything.shape[0], 512)

    def far(index, accum):
        places = lax.dynamic_slice_in_dim(sources, index * width, width, 1)
        x = lax.dynamic_slice_in_dim(everything, index * width, width, 0)[:, EXC_AT : EXC_AT + exc]
        kern_re, kern_im = far_kernel_values(
            wavenumber[0], [places[i][:, None] for i in range(4)], targets
        )
        re = lax.dot_general(kern_re.astype(BF16), x, dims, preferred_element_type=F32)
        im = lax.dot_general(kern_im.astype(BF16), x, dims, preferred_element_type=F32)
        return accum + jnp.concatenate([re[:, :half] - im[:, half:], re[:, half:] + im[:, :half]], 1)

    return lax.fori_loop(0, everything.shape[0] // width, far, total)


def on_device(*arguments):
    count = lax.axis_size("row") * lax.axis_size("col")
    short = lax.axis_size("col") == 2 and lax.axis_size("row") <= 16 and count & (count - 1) == 0
    return (exchanged if short and count >= 8 else gathered)(*arguments)


def solution(mesh):
    return jax.shard_map(
        on_device,
        mesh=mesh,
        in_specs=(
            P("groups"),
            P(None, ("groups", "row")),
            P(None, ("groups", "row", "col")),
            P(None, ("groups", "row", "col")),
            P(None, ("groups", "row")),
            P(None, ("groups", "row")),
            P(None, None, ("groups", "row")),
            P(None, None, ("groups", "row", "col")),
            P(("groups", "row"), None),
        ),
        out_specs=P(("groups", "row", "col"), None),
        check_vma=False,
    )
```

```python
import functools
import math

import jax
import jax.numpy as jnp
from jax import lax
from jax.experimental import pallas as pl
from jax.experimental.pallas import tpu as pltpu
from jax.sharding import PartitionSpec as P

QSTEP = 64
QN = 192
LANES = 128
PARTS = 3
SOFT = 0.05
INV_FOUR_PI = 1.0 / (4.0 * math.pi)
INV_TURN = 1.0 / (2.0 * math.pi)
TURN_HIGH = 6.28125
TURN_LOW = 2.0 * math.pi - TURN_HIGH
SIN_HALF = (3.14159264, -5.16771009, 2.55007766, -0.59829216, 0.07765941)
COS_HALF = (1.0, -4.93480214, 4.05870916, -1.33521206, 0.23493756, -0.02439672)
COS_FULL = (
    0.99999999, -19.73920453, 64.93911898, -85.45016555, 60.16783171, -25.96831321, 6.52961029
)
BF16 = jnp.bfloat16
F32 = jnp.float32
NN = (((1,), (0,)), ((), ()))
NT = (((1,), (1,)), ((), ()))
EXC_AT = 2 * QN
NODE_WIDTH = LANES
SMALL = pltpu.CompilerParams(vmem_limit_bytes=24 * 2**20)


def dot(left, right, dims=NN):
    return lax.dot_general(left, right, dims, preferred_element_type=F32)


def polynomial(z, coefficients):
    total = coefficients[-1]
    for c in coefficients[-2::-1]:
        total = total * z + c
    return total


def sincos_turns(f):
    z = f * f
    s = f * polynomial(z, SIN_HALF)
    c = polynomial(z, COS_HALF)
    twice = s + s
    return twice * c, 1.0 - twice * s


def three_parts(x):
    first = x.astype(BF16)
    rest = x - first.astype(F32)
    second = rest.astype(BF16)
    third = (rest - second.astype(F32)).astype(BF16)
    return first, second, third


def two_parts(x):
    first = x.astype(BF16)
    return first, (x - first.astype(F32)).astype(BF16)


def exchange_steps(count):
    bits = [1 << b for b in range(count.bit_length() - 2, 0, -1)]
    swapped = bits[:-2] + bits[-2:][::-1] if len(bits) >= 2 else bits
    return [b | 1 for b in bits], [b | 1 for b in swapped]


def relative_places(steps):
    places = [0]
    for step in steps:
        places = places + [p ^ step for p in places]
    return places


def iota(shape, axis):
    return lax.broadcasted_iota(jnp.int32, shape, axis)


def geom_lane(cpd):
    return 3 * PARTS * (QN // cpd)


def place_matrices(cpd):
    groups = QN // cpd
    shape = (LANES, 2 * 16)
    begin, row = iota(shape, 0), iota(shape, 1)
    node = jnp.logical_and(begin >= row * groups, begin < (row + 1) * groups)
    node = jnp.logical_and(node, row < 3 * PARTS)
    source = jnp.logical_and(begin - geom_lane(cpd) == row - 16, row >= 16)
    row_of = jnp.where(jnp.logical_or(node, source), 1.0, 0.0).astype(BF16)
    shape = (LANES, QN)
    lane, group = iota(shape, 0), lax.div(iota(shape, 1), cpd)
    wanted = jnp.where(lane < geom_lane(cpd), lax.rem(lane, groups), 0)
    kept = jnp.where(group == wanted, 1.0, 0.0)
    shape = (cpd, QN)
    column_of = jnp.where(lax.rem(iota(shape, 1), cpd) == iota(shape, 0), 1.0, 0.0).astype(BF16)
    return row_of, kept, column_of


def pack_kernel(
    units, order_hbm, geom_hbm, excite_hbm, nodes_hbm, weights_hbm, tnodes_hbm, tweights_hbm,
    out_ref, target_ref, tests_ref, found_ref,
    order_ref, geom_ref, excite_ref, nodes_ref, weights_ref, tnodes_ref, arrived,
):
    col = lax.axis_index("col")
    rows = tests_ref.shape[2]
    at = pl.ds(pl.multiple_of(col * rows, LANES), rows)
    moves = [
        (weights_hbm, weights_ref),
        (nodes_hbm, nodes_ref),
        (geom_hbm, geom_ref),
        (excite_hbm, excite_ref),
        (tnodes_hbm, tnodes_ref),
        (order_hbm, order_ref),
        (tweights_hbm.at[:, :, at], tests_ref),
    ]
    copies = [pltpu.make_async_copy(*move, arrived.at[i]) for i, move in enumerate(moves)]
    for copy in copies:
        copy.start()
    cpd, exc = excite_ref.shape
    row_of, kept, column_of = place_matrices(cpd)
    for copy in copies[:-1]:
        copy.wait()
    main = LANES
    rest = QN - main
    re, im = weights_ref[0], weights_ref[1]
    out_ref[:, 0:main] = re[:, :main]
    out_ref[:, main : 2 * main] = im[:, :main]
    out_ref[:, 2 * main : 2 * main + 2 * rest] = jnp.concatenate([re[:, main:], im[:, main:]], 1)
    out_ref[:, EXC_AT : EXC_AT + exc] = excite_ref[...]
    nodes = [p.astype(F32) for p in three_parts(nodes_ref[...])]
    geom = jnp.concatenate([p.astype(F32) for p in three_parts(geom_ref[...])], 0)
    values = jnp.concatenate(
        nodes
        + [
            jnp.zeros((16 - 3 * PARTS, QN), F32),
            jnp.concatenate([geom, jnp.zeros((geom.shape[0], QN - cpd), F32)], 1),
            jnp.zeros((16 - geom.shape[0], QN), F32),
        ],
        0,
    ).astype(BF16)
    spread = (dot(row_of, values) * kept).astype(BF16)
    out_ref[:, EXC_AT + exc :] = dot(column_of, spread, NT).astype(BF16)
    nodes = tnodes_ref[:, :QN]
    for b in range(1, tnodes_ref.shape[1] // QN):
        nodes = jnp.where(col == b, tnodes_ref[:, b * QN : (b + 1) * QN], nodes)
    end = nodes[:, LANES:]
    start = nodes[:, :QSTEP]
    target_ref[0, 0:3] = nodes[:, :LANES]
    target_ref[1, 0:3] = jnp.concatenate([end, end], 1)
    target_ref[2, 0:3] = jnp.concatenate([start, start], 1)
    for slot, order in enumerate(slot_orders(order_ref, units)):
        found_ref[slot] = order
    copies[-1].wait()


def store_tests(tests_ref, ut_ref):
    re, im = tests_ref[0], tests_ref[1]
    main = LANES
    ut_ref[0:main, :] = jnp.concatenate([re[:main], im[:main]], 1)
    ut_ref[main : 2 * main, :] = jnp.concatenate([-im[:main], re[:main]], 1)
    ut_ref[2 * main : 2 * main + QSTEP, :] = jnp.concatenate([re[main:], im[main:]], 1)
    ut_ref[2 * main + QSTEP :, :] = jnp.concatenate([-im[main:], re[main:]], 1)


def node_columns(data_ref, exc):
    block = data_ref[:, EXC_AT + exc :].astype(F32)
    step = geom_lane(16) // PARTS
    return (block[:, :step] + block[:, step : 2 * step]) + block[:, 2 * step : 3 * step]


def two_part_dot(high, low, right):
    count = high.shape[0]
    both = dot(jnp.concatenate([high, low], 0), right)
    return both[:count] + both[count:]


def near_slot(order, columns, slot, target_ref, ut_ref, turns, out_ref):
    lane = lax.broadcasted_iota(jnp.int32, (1, LANES), 1)
    quarter = jnp.where(lane < QSTEP, 0.0, 0.25)
    main = LANES

    def located(count):
        return [
            jnp.concatenate(
                [
                    jnp.broadcast_to(columns[16 * slot : 16 * slot + 16, lane : lane + 1], (16, LANES))
                    for lane in range(axis * (QN // 16), axis * (QN // 16) + count // 16)
                ],
                0,
            )
            for axis in range(3)
        ]

    def distance2(source, tile):
        total = SOFT * SOFT
        for axis in range(3):
            d = source[axis] - target_ref[tile, axis : axis + 1, :]
            total = total + d * d
        return total

    def both(source):
        d2 = distance2(source, 0)
        inv = lax.rsqrt(d2)
        t = (d2 * inv) * turns
        sin, cos = sincos_turns(t - jnp.round(t))
        return two_parts(inv * cos), two_parts(inv * sin)

    def split_lanes(source, tile):
        d2 = distance2(source, tile)
        inv = lax.rsqrt(d2)
        t = (d2 * inv) * turns
        f = (t - jnp.round(t - quarter)) - quarter
        return two_parts(inv * polynomial(f * f, COS_FULL))

    def put(at, value):
        high, low = two_parts(value)
        count = value.shape[0]
        out_ref[at : at + count, :LANES] = high
        out_ref[at : at + count, LANES:] = low

    def clear(begin, end):
        out_ref[begin:end, :] = jnp.zeros((end - begin, 2 * LANES), BF16)

    @pl.when(order == 3)
    def _():
        source = located(QN)
        (re_high, re_low), (im_high, im_low) = both(source)
        rest_high, rest_low = split_lanes(source, 1)
        high = jnp.concatenate([re_high, im_high, rest_high], 1)
        low = jnp.concatenate([re_low, im_low, rest_low], 1)
        v = two_part_dot(high, low, ut_ref[...])
        put(0, v[:main, :LANES])
        put(main, v[:main, LANES:])
        put(2 * main, v[main:, :LANES])
        put(2 * main + QSTEP, v[main:, LANES:])

    @pl.when(order == 2)
    def _():
        (re_high, re_low), (im_high, im_low) = both(located(main))
        high = jnp.concatenate([re_high, im_high], 1)
        low = jnp.concatenate([re_low, im_low], 1)
        v = two_part_dot(high, low, ut_ref[: 2 * main])
        put(0, v[:, :LANES])
        put(main, v[:, LANES:])
        clear(2 * main, 3 * main)

    @pl.when(order == 1)
    def _():
        high, low = split_lanes(located(QSTEP), 2)
        weights = jnp.concatenate([ut_ref[0:QSTEP], ut_ref[main : main + QSTEP]], 0)
        v = two_part_dot(high, low, weights)
        put(0, v[:, :LANES])
        clear(QSTEP, main)
        put(main, v[:, LANES:])
        clear(main + QSTEP, 3 * main)

    @pl.when(order == 0)
    def _():
        clear(0, 3 * main)


def slot_orders(order_ref, units):
    row, col = lax.axis_index("row"), lax.axis_index("col")
    nrow = lax.axis_size("row")
    band = order_ref.shape[1]
    reach = (band - 1) // 2
    if units is None:
        offsets = [jnp.where(jnp.logical_and(row + o >= reach, row + o - reach < nrow), o, -1) for o in range(band)]
    else:
        place, parity = row * lax.axis_size("col") + col, 0
        for _ in range((nrow * lax.axis_size("col")).bit_length() - 1):
            parity = parity + lax.rem(place, 2)
            place = lax.div(place, 2)
        parity = lax.rem(parity, 2)
        offsets = [
            (row ^ (a if a == b else jnp.where(parity == 0, a, b))) - row + reach for a, b in zip(*units)
        ]
    return [
        jnp.where(
            jnp.logical_and(o >= 0, o < band), order_ref[col, jnp.clip(o, 0, band - 1)], 0
        )
        for o in offsets
    ]


def far_kernel_values(wave, source, tgeom):
    dx = tgeom[0:1] - source[0]
    dy = tgeom[1:2] - source[1]
    dz = tgeom[2:3] - source[2]
    d2 = dx * dx + dy * dy + dz * dz + SOFT * SOFT
    inv = lax.rsqrt(d2)
    radius = d2 * inv
    cosine = (tgeom[3:4] * dx + tgeom[4:5] * dy + tgeom[5:6] * dz) * inv
    scale = source[3] * (INV_FOUR_PI * inv)
    phase = wave * radius
    t = phase * INV_TURN
    n = jnp.round(t)
    sin, cos = sincos_turns(((phase - n * TURN_HIGH) - n * TURN_LOW) * INV_TURN)
    green_re = scale * cos
    green_im = scale * sin
    factor_re = 1.0 - cosine
    factor_im = cosine * (inv * (-1.0 / wave))
    kern_re = (green_re * factor_re - green_im * factor_im).astype(BF16)
    kern_im = (green_re * factor_im + green_im * factor_re).astype(BF16)
    return kern_re, kern_im


def far_rows(data, exc, wave, tgeom):
    at = geom_lane(16)
    geom = data[:, EXC_AT + exc :].astype(F32)
    parts = [geom[:, at + 4 * i : at + 4 * i + 4] for i in range(PARTS)]
    total = (parts[0] + parts[1]) + parts[2]
    return far_kernel_values(wave, [total[:, i : i + 1] for i in range(4)], tgeom)


def own_targets(tgeom_ref, rows):
    at = pl.multiple_of(lax.axis_index("col") * rows, LANES)
    return tgeom_ref[:, pl.ds(at, rows)]


def near_kernel(
    exc, first, wave_ref, found_ref, data_ref, own_ref, target_ref, ut_ref, tgeom_ref,
    v_ref, kern_re_ref, kern_im_ref, *copy_ref,
):
    if copy_ref:
        copy_ref[0][...] = own_ref[...]
    wave = wave_ref[0]
    tgeom = own_targets(tgeom_ref, kern_re_ref.shape[1])
    data = data_ref[...]
    if kern_re_ref.shape[0] > data.shape[0]:
        data = jnp.concatenate([own_ref[...], data], 0)
    kern_re_ref[...], kern_im_ref[...] = far_rows(data, exc, wave, tgeom)
    slots = v_ref.shape[0]
    skipped = data_ref.shape[0] // 16 - slots
    columns = node_columns(data_ref, exc)
    for slot in range(slots):
        near_slot(
            found_ref[first + slot], columns, skipped + slot, target_ref, ut_ref, wave * INV_TURN, v_ref.at[slot]
        )


def first_near_kernel(
    exc, first, wave_ref, found_ref, data_ref, own_ref, target_ref, tests_ref, tgeom_ref, *refs
):
    *refs, ut_ref = refs
    store_tests(tests_ref, ut_ref)
    near_kernel(exc, first, wave_ref, found_ref, data_ref, own_ref, target_ref, ut_ref, tgeom_ref, *refs)


def weight_rows(data):
    sign = jnp.where(iota((1, LANES), 1) < QSTEP, 1.0, -1.0).astype(BF16)
    w = [data[:, i * LANES : (i + 1) * LANES] for i in range(3)]
    swapped = jnp.concatenate([w[2][:, QSTEP:], w[2][:, :QSTEP]], 1)
    return jnp.concatenate([w[0], -w[1], w[2] * sign], 1), jnp.concatenate([w[1], w[0], swapped], 1)


def near_rows(left, v):
    product = dot(left, v)
    return (product[:, :LANES] + product[:, LANES:]) * INV_FOUR_PI


def known_kernel(own_ref, other_ref, *refs):
    *v_refs, out_ref = refs
    cpd = 16
    own_re, own_im = weight_rows(own_ref[: other_ref.shape[0]])
    other_re, other_im = weight_rows(other_ref[...])
    for k, v in enumerate([ref.at[i] for ref in v_refs for i in range(ref.shape[0])]):
        here = slice(k * cpd, (k + 1) * cpd)
        left = jnp.concatenate([own_re[here], other_re[here], own_im[here], other_im[here]], 0)
        out_ref[k] = near_rows(left, v[...])


def last_kernel(
    exc, partner, wave_ref, own_early, own_late, other_first, other_early, other_late, tgeom_ref,
    known_early, known_late, early_re_ref, early_im_ref, *refs
):
    own = jnp.concatenate([own_early[...], own_late[...]], 0)
    other = jnp.concatenate([other_first[...], other_early[...], other_late[...]], 0)
    out_ref, zre, zim = refs[-3:]
    *made, early_v, late_v, late_re, late_im = refs[:-3]
    v_refs = [*made[::3], early_v, late_v]
    kern_re_refs, kern_im_refs = [*made[1::3], late_re], [*made[2::3], late_im]
    rows = out_ref.shape[0]
    cpd = 16
    main = LANES
    slots = len(partner)
    quarter = slots // 4
    own_re, own_im = weight_rows(own)
    other_re, other_im = weight_rows(other)
    slot = 0
    for v_ref in v_refs:
        for i in range(v_ref.shape[0]):
            here = slice(slot * cpd, (slot + 1) * cpd)
            there = slice(partner[slot] * cpd, (partner[slot] + 1) * cpd)
            if slot // quarter in (0, 2):
                a = (known_late if slot // quarter else known_early)[slot % quarter]
            else:
                left = jnp.concatenate([own_re[here], other_re[there], own_im[here], other_im[there]], 0)
                a = near_rows(left, v_ref[i])
            there = slice((slots + partner[slot]) * cpd, (slots + partner[slot] + 1) * cpd)
            zre[here] = a[0:cpd]
            zre[there] = a[cpd : 2 * cpd]
            zim[here] = a[2 * cpd : 3 * cpd]
            zim[there] = a[3 * cpd :]
            slot += 1

    late_kern = far_rows(other_late, exc, wave_ref[0], own_targets(tgeom_ref, rows))
    first = other_first.shape[0]
    kern_re, kern_im = [
        jnp.concatenate(
            [*[ref[...] for ref in refs[:-2]], refs[-2][first:], refs[-1][...], refs[-2][:first], early[...], x], 0
        ).astype(F32)
        for refs, early, x in zip((kern_re_refs, kern_im_refs), (early_re_ref, early_im_ref), late_kern)
    ]
    excite = jnp.concatenate(
        [own[:, EXC_AT : EXC_AT + exc], other[:, EXC_AT : EXC_AT + exc]], 0
    ).T
    re = two_parts(kern_re + zre[...])
    im = two_parts(kern_im + zim[...])
    product = dot(excite, jnp.concatenate([*re, *im], 1))
    by_re = product[:, :rows] + product[:, rows : 2 * rows]
    by_im = product[:, 2 * rows : 3 * rows] + product[:, 3 * rows :]
    h = exc // 2
    result = jnp.concatenate([by_re[:h] - by_im[h:], by_re[h:] + by_im[:h]], 0)
    out_ref[...] = result.T


def in_vmem(x):
    return pltpu.with_memory_space_constraint(x, pltpu.VMEM)


def in_smem(x):
    return pltpu.with_memory_space_constraint(x, pltpu.SMEM)


def in_hbm(x):
    return pltpu.with_memory_space_constraint(x, pltpu.HBM)


SMEM_SPEC = pl.BlockSpec(memory_space=pltpu.SMEM)
VMEM_SPEC = pl.BlockSpec(memory_space=pltpu.VMEM)


def packed(units, slots, src_geom, excite, src_nodes, src_weights, tgt_nodes, tgt_weights, near_order):
    excite = excite.T
    src_weights = src_weights.transpose(0, 2, 1)
    cpd, exc = excite.shape
    rows_here = tgt_weights.shape[2] // lax.axis_size("col")
    inputs = (near_order, src_geom, excite, src_nodes, src_weights, tgt_nodes)
    return pl.pallas_call(
        functools.partial(pack_kernel, units),
        out_shape=[
            pltpu.VMEM((cpd, EXC_AT + exc + NODE_WIDTH), BF16),
            pltpu.VMEM((3, 8, LANES), F32),
            pltpu.VMEM((2, QN, rows_here), BF16),
            pltpu.SMEM((slots,), jnp.int32),
        ],
        in_specs=[pl.BlockSpec(memory_space=pl.ANY)] * 7,
        out_specs=[VMEM_SPEC] * 3 + [SMEM_SPEC],
        scratch_shapes=[pltpu.SMEM(near_order.shape, jnp.int32)]
        + [pltpu.VMEM(x.shape, x.dtype) for x in inputs[1:]]
        + [pltpu.SemaphoreType.DMA((7,))],
        compiler_params=SMALL,
    )(*[in_hbm(x) for x in inputs], in_hbm(tgt_weights))


def near_blocks(exc, first, slots, wavenumber, found, fresh, own, target, ut, tgt_geom, hand_on, both=False):
    rows_here = tgt_geom.shape[1] // lax.axis_size("col")
    kern = pltpu.VMEM((fresh.shape[0] + both * own.shape[0], rows_here), BF16)
    cost = pl.CostEstimate(flops=1, bytes_accessed=1, transcendentals=0)
    outs = [pltpu.VMEM((slots, 2 * QN, 2 * LANES), BF16), kern, kern] + [pltpu.VMEM(own.shape, BF16)] * hand_on
    if first == 0:
        outs.append(pltpu.VMEM((2 * QN, 2 * LANES), BF16))
    return pl.pallas_call(
        functools.partial(near_kernel if first else first_near_kernel, exc, first),
        out_shape=outs,
        in_specs=[SMEM_SPEC] * 2 + [VMEM_SPEC] * 5,
        out_specs=[VMEM_SPEC] * len(outs),
        compiler_params=SMALL,
        cost_estimate=cost,
    )(wavenumber, in_smem(found), in_vmem(fresh), in_vmem(own), in_vmem(target), in_vmem(ut), in_vmem(tgt_geom))


def exchanged(
    wavenumber, tgt_geom, src_geom, excite, tgt_nodes, src_nodes, tgt_weights, src_weights, near_order
):
    cpd = src_geom.shape[1]
    exc = excite.shape[0]
    cores = lax.axis_size("col")
    count = cores * lax.axis_size("row")
    rows_here = tgt_geom.shape[1] // cores
    even, odd = exchange_steps(count)
    units = [[p >> 1 for p in relative_places(s)] for s in (even, odd)]
    own, target, ut, found = packed(
        units, len(units[0]), src_geom, excite, src_nodes, src_weights, tgt_nodes, tgt_weights, near_order
    )

    def moved(value, a, b):
        pairs = [(i, i ^ (b if bin(i).count("1") % 2 else a)) for i in range(count)]
        return lax.ppermute(value, ("row", "col"), pairs)

    fresh = own
    near = []
    done = 0
    steps = list(zip(even, odd))
    for step, (a, b) in enumerate(steps):
        arriving = moved(own, a, b)
        slots = fresh.shape[0] // cpd
        last = step == len(steps) - 1
        made = near_blocks(
            exc, done, slots, wavenumber, found, fresh, other_first if last else own, target, ut, tgt_geom,
            not last, last,
        )
        near.extend(made[:3])
        if not done:
            ut = made[4]
        if step == len(steps) - 2:
            other_first = moved(own, 1, 1)
        done += slots
        fresh = arriving
        if not last:
            own = jnp.concatenate([made[3], arriving], 0)
        if step == len(steps) - 2:
            own, other_first = lax.optimization_barrier((own, other_first))
    half = own.shape[0] // 2
    other_early = moved(own[half:], 1, 1)
    quarter = half // cpd
    early = near_blocks(
        exc, done, quarter, wavenumber, found, other_early, other_early, target, ut, tgt_geom, False
    )

    def known_rows(mine, others, *v):
        return pl.pallas_call(
            known_kernel,
            out_shape=pltpu.VMEM((quarter, 4 * cpd, rows_here), F32),
            in_specs=[VMEM_SPEC] * (2 + len(v)),
            out_specs=VMEM_SPEC,
            compiler_params=SMALL,
            cost_estimate=pl.CostEstimate(flops=1, bytes_accessed=1, transcendentals=0),
        )(*[in_vmem(x) for x in (mine, others, *v)])

    known_early = known_rows(own, other_first, *near[: 3 * (len(steps) - 1) : 3])
    fresh, early, made, known_early = lax.optimization_barrier((fresh, early, made, known_early))
    other_late = moved(fresh, 1, 1)
    late = near_blocks(
        exc, done + quarter, quarter, wavenumber, found, fresh, fresh, target, ut, tgt_geom, False
    )
    near.append(early[0])
    near.extend(late)
    known_late = known_rows(fresh, other_early, early[0])
    partner = [units[1].index(u) for u in units[0]]
    return pl.pallas_call(
        functools.partial(last_kernel, exc, partner),
        out_shape=jax.ShapeDtypeStruct((rows_here, exc), F32),
        in_specs=[SMEM_SPEC] + [VMEM_SPEC] * (10 + len(near)),
        out_specs=VMEM_SPEC,
        scratch_shapes=[pltpu.VMEM((count * cpd, rows_here), F32)] * 2,
        compiler_params=SMALL,
    )(
        wavenumber,
        *[in_vmem(x) for x in (own, fresh, other_first, other_early, other_late, tgt_geom, known_early, known_late, *early[1:], *near)],
    )


def gathered(
    wavenumber, tgt_geom, src_geom, excite, tgt_nodes, src_nodes, tgt_weights, src_weights, near_order
):
    cpd = src_geom.shape[1]
    exc = excite.shape[0]
    half = exc // 2
    cores = lax.axis_size("col")
    nrow = lax.axis_size("row")
    row = lax.axis_index("row")
    rows_here = tgt_geom.shape[1] // cores
    band = near_order.shape[1]
    own, target, ut, found = packed(
        None, band, src_geom, excite, src_nodes, src_weights, tgt_nodes, tgt_weights, near_order
    )
    everything = lax.all_gather(own, ("row", "col"), axis=0, tiled=True)
    sources = lax.all_gather(src_geom, ("row", "col"), axis=1, tiled=True)
    blocks = [
        lax.dynamic_slice_in_dim(
            everything, jnp.clip(row + o - (band - 1) // 2, 0, nrow - 1) * cores * cpd, cores * cpd, 0
        )
        for o in range(band)
    ]
    fresh = jnp.concatenate([block[:cpd] for block in blocks], 0)
    near = near_blocks(exc, 0, band, wavenumber, found, fresh, own, target, ut, tgt_geom, False)[0]
    high = lax.Precision.HIGHEST
    total = jnp.zeros((rows_here, exc), F32)
    dims = (((0,), (0,)), ((), ()))
    m, r = LANES, QN - LANES
    for o, block in enumerate(blocks):
        w, x = block[:, :EXC_AT].astype(F32), block[:, EXC_AT : EXC_AT + exc].astype(F32)
        v = near[o, :, :LANES].astype(F32) + near[o, :, LANES:].astype(F32)
        w_re = jnp.concatenate([w[:, :m], w[:, 2 * m : 2 * m + r]], 1)
        w_im = jnp.concatenate([w[:, m : 2 * m], w[:, 2 * m + r :]], 1)
        v_re = jnp.concatenate([v[:m], v[2 * m : 2 * m + r]], 0)
        v_im = jnp.concatenate([v[m : 2 * m], v[2 * m + r :]], 0)
        a_re = jnp.dot(w_re, v_re, precision=high) - jnp.dot(w_im, v_im, precision=high)
        a_im = jnp.dot(w_re, v_im, precision=high) + jnp.dot(w_im, v_re, precision=high)
        re = lax.dot_general(a_re, x, dims, precision=high)
        im = lax.dot_general(a_im, x, dims, precision=high)
        total = total + INV_FOUR_PI * jnp.concatenate(
            [re[:, :half] - im[:, half:], re[:, half:] + im[:, :half]], 1
        )
    targets = lax.dynamic_slice_in_dim(tgt_geom, lax.axis_index("col") * rows_here, rows_here, 1)
    width = math.gcd(everything.shape[0], 512)

    def far(index, accum):
        places = lax.dynamic_slice_in_dim(sources, index * width, width, 1)
        x = lax.dynamic_slice_in_dim(everything, index * width, width, 0)[:, EXC_AT : EXC_AT + exc]
        kern_re, kern_im = far_kernel_values(
            wavenumber[0], [places[i][:, None] for i in range(4)], targets
        )
        re = lax.dot_general(kern_re.astype(BF16), x, dims, preferred_element_type=F32)
        im = lax.dot_general(kern_im.astype(BF16), x, dims, preferred_element_type=F32)
        return accum + jnp.concatenate([re[:, :half] - im[:, half:], re[:, half:] + im[:, :half]], 1)

    return lax.fori_loop(0, everything.shape[0] // width, far, total)


def on_device(*arguments):
    count = lax.axis_size("row") * lax.axis_size("col")
    short = lax.axis_size("col") == 2 and lax.axis_size("row") <= 16 and count & (count - 1) == 0
    return (exchanged if short and count >= 8 else gathered)(*arguments)


def solution(mesh):
    return jax.shard_map(
        on_device,
        mesh=mesh,
        in_specs=(
            P("groups"),
            P(None, ("groups", "row")),
            P(None, ("groups", "row", "col")),
            P(None, ("groups", "row", "col")),
            P(None, ("groups", "row")),
            P(None, ("groups", "row")),
            P(None, None, ("groups", "row")),
            P(None, None, ("groups", "row", "col")),
            P(("groups", "row"), None),
        ),
        out_specs=P(("groups", "row", "col"), None),
        check_vma=False,
    )
```

```python
import functools
import math

import jax
import jax.numpy as jnp
from jax import lax
from jax.experimental import pallas as pl
from jax.experimental.pallas import tpu as pltpu
from jax.sharding import PartitionSpec as P

QSTEP = 64
QN = 192
LANES = 128
PARTS = 3
SOFT = 0.05
INV_FOUR_PI = 1.0 / (4.0 * math.pi)
INV_TURN = 1.0 / (2.0 * math.pi)
TURN_HIGH = 6.28125
TURN_LOW = 2.0 * math.pi - TURN_HIGH
SIN_HALF = (3.14159264, -5.16771009, 2.55007766, -0.59829216, 0.07765941)
COS_HALF = (1.0, -4.93480214, 4.05870916, -1.33521206, 0.23493756, -0.02439672)
COS_FULL = (
    0.99999999, -19.73920453, 64.93911898, -85.45016555, 60.16783171, -25.96831321, 6.52961029
)
BF16 = jnp.bfloat16
F32 = jnp.float32
NN = (((1,), (0,)), ((), ()))
NT = (((1,), (1,)), ((), ()))
EXC_AT = 2 * QN
NODE_WIDTH = LANES
SMALL = pltpu.CompilerParams(vmem_limit_bytes=24 * 2**20)


def dot(left, right, dims=NN):
    return lax.dot_general(left, right, dims, preferred_element_type=F32)


def polynomial(z, coefficients):
    total = coefficients[-1]
    for c in coefficients[-2::-1]:
        total = total * z + c
    return total


def sincos_turns(f):
    z = f * f
    s = f * polynomial(z, SIN_HALF)
    c = polynomial(z, COS_HALF)
    twice = s + s
    return twice * c, 1.0 - twice * s


def three_parts(x):
    first = x.astype(BF16)
    rest = x - first.astype(F32)
    second = rest.astype(BF16)
    third = (rest - second.astype(F32)).astype(BF16)
    return first, second, third


def two_parts(x):
    first = x.astype(BF16)
    return first, (x - first.astype(F32)).astype(BF16)


def exchange_steps(count):
    bits = [1 << b for b in range(count.bit_length() - 2, 0, -1)]
    swapped = bits[:-2] + bits[-2:][::-1] if len(bits) >= 2 else bits
    return [b | 1 for b in bits], [b | 1 for b in swapped]


def relative_places(steps):
    places = [0]
    for step in steps:
        places = places + [p ^ step for p in places]
    return places


def iota(shape, axis):
    return lax.broadcasted_iota(jnp.int32, shape, axis)


def geom_lane(cpd):
    return 3 * PARTS * (QN // cpd)


def place_matrices(cpd):
    groups = QN // cpd
    shape = (LANES, 2 * 16)
    begin, row = iota(shape, 0), iota(shape, 1)
    node = jnp.logical_and(begin >= row * groups, begin < (row + 1) * groups)
    node = jnp.logical_and(node, row < 3 * PARTS)
    source = jnp.logical_and(begin - geom_lane(cpd) == row - 16, row >= 16)
    row_of = jnp.where(jnp.logical_or(node, source), 1.0, 0.0).astype(BF16)
    shape = (LANES, QN)
    lane, group = iota(shape, 0), lax.div(iota(shape, 1), cpd)
    wanted = jnp.where(lane < geom_lane(cpd), lax.rem(lane, groups), 0)
    kept = jnp.where(group == wanted, 1.0, 0.0)
    shape = (cpd, QN)
    column_of = jnp.where(lax.rem(iota(shape, 1), cpd) == iota(shape, 0), 1.0, 0.0).astype(BF16)
    return row_of, kept, column_of


def pack_kernel(
    units, order_hbm, geom_hbm, excite_hbm, nodes_hbm, weights_hbm, tnodes_hbm, tweights_hbm,
    out_ref, target_ref, tests_ref, found_ref,
    order_ref, geom_ref, excite_ref, nodes_ref, weights_ref, tnodes_ref, arrived,
):
    col = lax.axis_index("col")
    rows = tests_ref.shape[2]
    at = pl.ds(pl.multiple_of(col * rows, LANES), rows)
    moves = [
        (order_hbm, order_ref),
        (nodes_hbm, nodes_ref),
        (geom_hbm, geom_ref),
        (tnodes_hbm, tnodes_ref),
        (excite_hbm, excite_ref),
        (weights_hbm, weights_ref),
        (tweights_hbm.at[:, :, at], tests_ref),
    ]
    copies = [pltpu.make_async_copy(*move, arrived.at[i]) for i, move in enumerate(moves)]
    for copy in copies:
        copy.start()
    cpd, exc = excite_ref.shape
    row_of, kept, column_of = place_matrices(cpd)
    for copy in copies[:-1]:
        copy.wait()
    main = LANES
    rest = QN - main
    re, im = weights_ref[0], weights_ref[1]
    out_ref[:, 0:main] = re[:, :main]
    out_ref[:, main : 2 * main] = im[:, :main]
    out_ref[:, 2 * main : 2 * main + 2 * rest] = jnp.concatenate([re[:, main:], im[:, main:]], 1)
    out_ref[:, EXC_AT : EXC_AT + exc] = excite_ref[...]
    nodes = [p.astype(F32) for p in three_parts(nodes_ref[...])]
    geom = jnp.concatenate([p.astype(F32) for p in three_parts(geom_ref[...])], 0)
    values = jnp.concatenate(
        nodes
        + [
            jnp.zeros((16 - 3 * PARTS, QN), F32),
            jnp.concatenate([geom, jnp.zeros((geom.shape[0], QN - cpd), F32)], 1),
            jnp.zeros((16 - geom.shape[0], QN), F32),
        ],
        0,
    ).astype(BF16)
    spread = (dot(row_of, values) * kept).astype(BF16)
    out_ref[:, EXC_AT + exc :] = dot(column_of, spread, NT).astype(BF16)
    nodes = tnodes_ref[:, :QN]
    for b in range(1, tnodes_ref.shape[1] // QN):
        nodes = jnp.where(col == b, tnodes_ref[:, b * QN : (b + 1) * QN], nodes)
    end = nodes[:, LANES:]
    start = nodes[:, :QSTEP]
    target_ref[0, 0:3] = nodes[:, :LANES]
    target_ref[1, 0:3] = jnp.concatenate([end, end], 1)
    target_ref[2, 0:3] = jnp.concatenate([start, start], 1)
    for slot, order in enumerate(slot_orders(order_ref, units)):
        found_ref[slot] = order
    copies[-1].wait()


def store_tests(tests_ref, ut_ref):
    re, im = tests_ref[0], tests_ref[1]
    main = LANES
    ut_ref[0:main, :] = jnp.concatenate([re[:main], im[:main]], 1)
    ut_ref[main : 2 * main, :] = jnp.concatenate([-im[:main], re[:main]], 1)
    ut_ref[2 * main : 2 * main + QSTEP, :] = jnp.concatenate([re[main:], im[main:]], 1)
    ut_ref[2 * main + QSTEP :, :] = jnp.concatenate([-im[main:], re[main:]], 1)


def node_columns(data_ref, exc):
    block = data_ref[:, EXC_AT + exc :].astype(F32)
    step = geom_lane(16) // PARTS
    return (block[:, :step] + block[:, step : 2 * step]) + block[:, 2 * step : 3 * step]


def two_part_dot(high, low, right):
    count = high.shape[0]
    both = dot(jnp.concatenate([high, low], 0), right)
    return both[:count] + both[count:]


def near_slot(order, columns, slot, target_ref, ut_ref, turns, out_ref):
    lane = lax.broadcasted_iota(jnp.int32, (1, LANES), 1)
    quarter = jnp.where(lane < QSTEP, 0.0, 0.25)
    main = LANES

    def located(count):
        return [
            jnp.concatenate(
                [
                    jnp.broadcast_to(columns[16 * slot : 16 * slot + 16, lane : lane + 1], (16, LANES))
                    for lane in range(axis * (QN // 16), axis * (QN // 16) + count // 16)
                ],
                0,
            )
            for axis in range(3)
        ]

    def distance2(source, tile):
        total = SOFT * SOFT
        for axis in range(3):
            d = source[axis] - target_ref[tile, axis : axis + 1, :]
            total = total + d * d
        return total

    def both(source):
        d2 = distance2(source, 0)
        inv = lax.rsqrt(d2)
        t = (d2 * inv) * turns
        sin, cos = sincos_turns(t - jnp.round(t))
        return two_parts(inv * cos), two_parts(inv * sin)

    def split_lanes(source, tile):
        d2 = distance2(source, tile)
        inv = lax.rsqrt(d2)
        t = (d2 * inv) * turns
        f = (t - jnp.round(t - quarter)) - quarter
        return two_parts(inv * polynomial(f * f, COS_FULL))

    def put(at, value):
        high, low = two_parts(value)
        count = value.shape[0]
        out_ref[at : at + count, :LANES] = high
        out_ref[at : at + count, LANES:] = low

    def clear(begin, end):
        out_ref[begin:end, :] = jnp.zeros((end - begin, 2 * LANES), BF16)

    @pl.when(order == 3)
    def _():
        source = located(QN)
        (re_high, re_low), (im_high, im_low) = both(source)
        rest_high, rest_low = split_lanes(source, 1)
        high = jnp.concatenate([re_high, im_high, rest_high], 1)
        low = jnp.concatenate([re_low, im_low, rest_low], 1)
        v = two_part_dot(high, low, ut_ref[...])
        put(0, v[:main, :LANES])
        put(main, v[:main, LANES:])
        put(2 * main, v[main:, :LANES])
        put(2 * main + QSTEP, v[main:, LANES:])

    @pl.when(order == 2)
    def _():
        (re_high, re_low), (im_high, im_low) = both(located(main))
        high = jnp.concatenate([re_high, im_high], 1)
        low = jnp.concatenate([re_low, im_low], 1)
        v = two_part_dot(high, low, ut_ref[: 2 * main])
        put(0, v[:, :LANES])
        put(main, v[:, LANES:])
        clear(2 * main, 3 * main)

    @pl.when(order == 1)
    def _():
        high, low = split_lanes(located(QSTEP), 2)
        weights = jnp.concatenate([ut_ref[0:QSTEP], ut_ref[main : main + QSTEP]], 0)
        v = two_part_dot(high, low, weights)
        put(0, v[:, :LANES])
        clear(QSTEP, main)
        put(main, v[:, LANES:])
        clear(main + QSTEP, 3 * main)

    @pl.when(order == 0)
    def _():
        clear(0, 3 * main)


def slot_orders(order_ref, units):
    row, col = lax.axis_index("row"), lax.axis_index("col")
    nrow = lax.axis_size("row")
    band = order_ref.shape[1]
    reach = (band - 1) // 2
    if units is None:
        offsets = [jnp.where(jnp.logical_and(row + o >= reach, row + o - reach < nrow), o, -1) for o in range(band)]
    else:
        place, parity = row * lax.axis_size("col") + col, 0
        for _ in range((nrow * lax.axis_size("col")).bit_length() - 1):
            parity = parity + lax.rem(place, 2)
            place = lax.div(place, 2)
        parity = lax.rem(parity, 2)
        offsets = [
            (row ^ (a if a == b else jnp.where(parity == 0, a, b))) - row + reach for a, b in zip(*units)
        ]
    return [
        jnp.where(
            jnp.logical_and(o >= 0, o < band), order_ref[col, jnp.clip(o, 0, band - 1)], 0
        )
        for o in offsets
    ]


def far_kernel_values(wave, source, tgeom):
    dx = tgeom[0:1] - source[0]
    dy = tgeom[1:2] - source[1]
    dz = tgeom[2:3] - source[2]
    d2 = dx * dx + dy * dy + dz * dz + SOFT * SOFT
    inv = lax.rsqrt(d2)
    radius = d2 * inv
    cosine = (tgeom[3:4] * dx + tgeom[4:5] * dy + tgeom[5:6] * dz) * inv
    scale = source[3] * (INV_FOUR_PI * inv)
    phase = wave * radius
    t = phase * INV_TURN
    n = jnp.round(t)
    sin, cos = sincos_turns(((phase - n * TURN_HIGH) - n * TURN_LOW) * INV_TURN)
    green_re = scale * cos
    green_im = scale * sin
    factor_re = 1.0 - cosine
    factor_im = cosine * (inv * (-1.0 / wave))
    kern_re = (green_re * factor_re - green_im * factor_im).astype(BF16)
    kern_im = (green_re * factor_im + green_im * factor_re).astype(BF16)
    return kern_re, kern_im


def far_rows(data, exc, wave, tgeom):
    at = geom_lane(16)
    geom = data[:, EXC_AT + exc :].astype(F32)
    parts = [geom[:, at + 4 * i : at + 4 * i + 4] for i in range(PARTS)]
    total = (parts[0] + parts[1]) + parts[2]
    return far_kernel_values(wave, [total[:, i : i + 1] for i in range(4)], tgeom)


def own_targets(tgeom_ref, rows):
    at = pl.multiple_of(lax.axis_index("col") * rows, LANES)
    return tgeom_ref[:, pl.ds(at, rows)]


def near_kernel(
    exc, first, wave_ref, found_ref, data_ref, own_ref, target_ref, ut_ref, tgeom_ref,
    v_ref, kern_re_ref, kern_im_ref, *copy_ref,
):
    if copy_ref:
        copy_ref[0][...] = own_ref[...]
    wave = wave_ref[0]
    tgeom = own_targets(tgeom_ref, kern_re_ref.shape[1])
    data = data_ref[...]
    if kern_re_ref.shape[0] > data.shape[0]:
        data = jnp.concatenate([own_ref[...], data], 0)
    kern_re_ref[...], kern_im_ref[...] = far_rows(data, exc, wave, tgeom)
    slots = v_ref.shape[0]
    skipped = data_ref.shape[0] // 16 - slots
    columns = node_columns(data_ref, exc)
    for slot in range(slots):
        near_slot(
            found_ref[first + slot], columns, skipped + slot, target_ref, ut_ref, wave * INV_TURN, v_ref.at[slot]
        )


def first_near_kernel(
    exc, first, wave_ref, found_ref, data_ref, own_ref, target_ref, tests_ref, tgeom_ref, *refs
):
    *refs, ut_ref = refs
    store_tests(tests_ref, ut_ref)
    near_kernel(exc, first, wave_ref, found_ref, data_ref, own_ref, target_ref, ut_ref, tgeom_ref, *refs)


def weight_rows(data):
    sign = jnp.where(iota((1, LANES), 1) < QSTEP, 1.0, -1.0).astype(BF16)
    w = [data[:, i * LANES : (i + 1) * LANES] for i in range(3)]
    swapped = jnp.concatenate([w[2][:, QSTEP:], w[2][:, :QSTEP]], 1)
    return jnp.concatenate([w[0], -w[1], w[2] * sign], 1), jnp.concatenate([w[1], w[0], swapped], 1)


def near_rows(left, v):
    product = dot(left, v)
    return (product[:, :LANES] + product[:, LANES:]) * INV_FOUR_PI


def known_kernel(own_ref, other_ref, *refs):
    *v_refs, out_ref = refs
    cpd = 16
    own_re, own_im = weight_rows(own_ref[: other_ref.shape[0]])
    other_re, other_im = weight_rows(other_ref[...])
    for k, v in enumerate([ref.at[i] for ref in v_refs for i in range(ref.shape[0])]):
        here = slice(k * cpd, (k + 1) * cpd)
        left = jnp.concatenate([own_re[here], other_re[here], own_im[here], other_im[here]], 0)
        out_ref[k] = near_rows(left, v[...])


def last_kernel(
    exc, partner, wave_ref, own_early, own_late, other_first, other_early, other_late, tgeom_ref,
    known_early, known_late, early_re_ref, early_im_ref, *refs
):
    own = jnp.concatenate([own_early[...], own_late[...]], 0)
    other = jnp.concatenate([other_first[...], other_early[...], other_late[...]], 0)
    out_ref, zre, zim = refs[-3:]
    *made, early_v, late_v, late_re, late_im = refs[:-3]
    v_refs = [*made[::3], early_v, late_v]
    kern_re_refs, kern_im_refs = [*made[1::3], late_re], [*made[2::3], late_im]
    rows = out_ref.shape[0]
    cpd = 16
    main = LANES
    slots = len(partner)
    quarter = slots // 4
    own_re, own_im = weight_rows(own)
    other_re, other_im = weight_rows(other)
    slot = 0
    for v_ref in v_refs:
        for i in range(v_ref.shape[0]):
            here = slice(slot * cpd, (slot + 1) * cpd)
            there = slice(partner[slot] * cpd, (partner[slot] + 1) * cpd)
            if slot // quarter in (0, 2):
                a = (known_late if slot // quarter else known_early)[slot % quarter]
            else:
                left = jnp.concatenate([own_re[here], other_re[there], own_im[here], other_im[there]], 0)
                a = near_rows(left, v_ref[i])
            there = slice((slots + partner[slot]) * cpd, (slots + partner[slot] + 1) * cpd)
            zre[here] = a[0:cpd]
            zre[there] = a[cpd : 2 * cpd]
            zim[here] = a[2 * cpd : 3 * cpd]
            zim[there] = a[3 * cpd :]
            slot += 1

    late_kern = far_rows(other_late, exc, wave_ref[0], own_targets(tgeom_ref, rows))
    first = other_first.shape[0]
    kern_re, kern_im = [
        jnp.concatenate(
            [*[ref[...] for ref in refs[:-2]], refs[-2][first:], refs[-1][...], refs[-2][:first], early[...], x], 0
        ).astype(F32)
        for refs, early, x in zip((kern_re_refs, kern_im_refs), (early_re_ref, early_im_ref), late_kern)
    ]
    excite = jnp.concatenate(
        [own[:, EXC_AT : EXC_AT + exc], other[:, EXC_AT : EXC_AT + exc]], 0
    ).T
    re = two_parts(kern_re + zre[...])
    im = two_parts(kern_im + zim[...])
    product = dot(excite, jnp.concatenate([*re, *im], 1))
    by_re = product[:, :rows] + product[:, rows : 2 * rows]
    by_im = product[:, 2 * rows : 3 * rows] + product[:, 3 * rows :]
    h = exc // 2
    result = jnp.concatenate([by_re[:h] - by_im[h:], by_re[h:] + by_im[:h]], 0)
    out_ref[...] = result.T


def in_vmem(x):
    return pltpu.with_memory_space_constraint(x, pltpu.VMEM)


def in_smem(x):
    return pltpu.with_memory_space_constraint(x, pltpu.SMEM)


def in_hbm(x):
    return pltpu.with_memory_space_constraint(x, pltpu.HBM)


SMEM_SPEC = pl.BlockSpec(memory_space=pltpu.SMEM)
VMEM_SPEC = pl.BlockSpec(memory_space=pltpu.VMEM)


def packed(units, slots, src_geom, excite, src_nodes, src_weights, tgt_nodes, tgt_weights, near_order):
    excite = excite.T
    src_weights = src_weights.transpose(0, 2, 1)
    cpd, exc = excite.shape
    rows_here = tgt_weights.shape[2] // lax.axis_size("col")
    inputs = (near_order, src_geom, excite, src_nodes, src_weights, tgt_nodes)
    return pl.pallas_call(
        functools.partial(pack_kernel, units),
        out_shape=[
            pltpu.VMEM((cpd, EXC_AT + exc + NODE_WIDTH), BF16),
            pltpu.VMEM((3, 8, LANES), F32),
            pltpu.VMEM((2, QN, rows_here), BF16),
            pltpu.SMEM((slots,), jnp.int32),
        ],
        in_specs=[pl.BlockSpec(memory_space=pl.ANY)] * 7,
        out_specs=[VMEM_SPEC] * 3 + [SMEM_SPEC],
        scratch_shapes=[pltpu.SMEM(near_order.shape, jnp.int32)]
        + [pltpu.VMEM(x.shape, x.dtype) for x in inputs[1:]]
        + [pltpu.SemaphoreType.DMA((7,))],
        compiler_params=SMALL,
    )(*[in_hbm(x) for x in inputs], in_hbm(tgt_weights))


def near_blocks(exc, first, slots, wavenumber, found, fresh, own, target, ut, tgt_geom, hand_on, both=False):
    rows_here = tgt_geom.shape[1] // lax.axis_size("col")
    kern = pltpu.VMEM((fresh.shape[0] + both * own.shape[0], rows_here), BF16)
    cost = pl.CostEstimate(flops=1, bytes_accessed=1, transcendentals=0)
    outs = [pltpu.VMEM((slots, 2 * QN, 2 * LANES), BF16), kern, kern] + [pltpu.VMEM(own.shape, BF16)] * hand_on
    if first == 0:
        outs.append(pltpu.VMEM((2 * QN, 2 * LANES), BF16))
    return pl.pallas_call(
        functools.partial(near_kernel if first else first_near_kernel, exc, first),
        out_shape=outs,
        in_specs=[SMEM_SPEC] * 2 + [VMEM_SPEC] * 5,
        out_specs=[VMEM_SPEC] * len(outs),
        compiler_params=SMALL,
        cost_estimate=cost,
    )(wavenumber, in_smem(found), in_vmem(fresh), in_vmem(own), in_vmem(target), in_vmem(ut), in_vmem(tgt_geom))


def exchanged(
    wavenumber, tgt_geom, src_geom, excite, tgt_nodes, src_nodes, tgt_weights, src_weights, near_order
):
    cpd = src_geom.shape[1]
    exc = excite.shape[0]
    cores = lax.axis_size("col")
    count = cores * lax.axis_size("row")
    rows_here = tgt_geom.shape[1] // cores
    even, odd = exchange_steps(count)
    units = [[p >> 1 for p in relative_places(s)] for s in (even, odd)]
    own, target, ut, found = packed(
        units, len(units[0]), src_geom, excite, src_nodes, src_weights, tgt_nodes, tgt_weights, near_order
    )

    def moved(value, a, b):
        pairs = [(i, i ^ (b if bin(i).count("1") % 2 else a)) for i in range(count)]
        return lax.ppermute(value, ("row", "col"), pairs)

    fresh = own
    near = []
    done = 0
    steps = list(zip(even, odd))
    for step, (a, b) in enumerate(steps):
        arriving = moved(own, a, b)
        slots = fresh.shape[0] // cpd
        last = step == len(steps) - 1
        made = near_blocks(
            exc, done, slots, wavenumber, found, fresh, other_first if last else own, target, ut, tgt_geom,
            not last, last,
        )
        near.extend(made[:3])
        if not done:
            ut = made[4]
        if step == len(steps) - 2:
            other_first = moved(own, 1, 1)
        done += slots
        fresh = arriving
        if not last:
            own = jnp.concatenate([made[3], arriving], 0)
        if step == len(steps) - 2:
            own, other_first = lax.optimization_barrier((own, other_first))
    half = own.shape[0] // 2
    other_early = moved(own[half:], 1, 1)
    quarter = half // cpd
    early = near_blocks(
        exc, done, quarter, wavenumber, found, other_early, other_early, target, ut, tgt_geom, False
    )

    def known_rows(mine, others, *v):
        return pl.pallas_call(
            known_kernel,
            out_shape=pltpu.VMEM((quarter, 4 * cpd, rows_here), F32),
            in_specs=[VMEM_SPEC] * (2 + len(v)),
            out_specs=VMEM_SPEC,
            compiler_params=SMALL,
            cost_estimate=pl.CostEstimate(flops=1, bytes_accessed=1, transcendentals=0),
        )(*[in_vmem(x) for x in (mine, others, *v)])

    known_early = known_rows(own, other_first, *near[: 3 * (len(steps) - 1) : 3])
    fresh, early, made, known_early = lax.optimization_barrier((fresh, early, made, known_early))
    other_late = moved(fresh, 1, 1)
    late = near_blocks(
        exc, done + quarter, quarter, wavenumber, found, fresh, fresh, target, ut, tgt_geom, False
    )
    near.append(early[0])
    near.extend(late)
    known_late = known_rows(fresh, other_early, early[0])
    partner = [units[1].index(u) for u in units[0]]
    return pl.pallas_call(
        functools.partial(last_kernel, exc, partner),
        out_shape=jax.ShapeDtypeStruct((rows_here, exc), F32),
        in_specs=[SMEM_SPEC] + [VMEM_SPEC] * (10 + len(near)),
        out_specs=VMEM_SPEC,
        scratch_shapes=[pltpu.VMEM((count * cpd, rows_here), F32)] * 2,
        compiler_params=SMALL,
    )(
        wavenumber,
        *[in_vmem(x) for x in (own, fresh, other_first, other_early, other_late, tgt_geom, known_early, known_late, *early[1:], *near)],
    )


def gathered(
    wavenumber, tgt_geom, src_geom, excite, tgt_nodes, src_nodes, tgt_weights, src_weights, near_order
):
    cpd = src_geom.shape[1]
    exc = excite.shape[0]
    half = exc // 2
    cores = lax.axis_size("col")
    nrow = lax.axis_size("row")
    row = lax.axis_index("row")
    rows_here = tgt_geom.shape[1] // cores
    band = near_order.shape[1]
    own, target, ut, found = packed(
        None, band, src_geom, excite, src_nodes, src_weights, tgt_nodes, tgt_weights, near_order
    )
    everything = lax.all_gather(own, ("row", "col"), axis=0, tiled=True)
    sources = lax.all_gather(src_geom, ("row", "col"), axis=1, tiled=True)
    blocks = [
        lax.dynamic_slice_in_dim(
            everything, jnp.clip(row + o - (band - 1) // 2, 0, nrow - 1) * cores * cpd, cores * cpd, 0
        )
        for o in range(band)
    ]
    fresh = jnp.concatenate([block[:cpd] for block in blocks], 0)
    near = near_blocks(exc, 0, band, wavenumber, found, fresh, own, target, ut, tgt_geom, False)[0]
    high = lax.Precision.HIGHEST
    total = jnp.zeros((rows_here, exc), F32)
    dims = (((0,), (0,)), ((), ()))
    m, r = LANES, QN - LANES
    for o, block in enumerate(blocks):
        w, x = block[:, :EXC_AT].astype(F32), block[:, EXC_AT : EXC_AT + exc].astype(F32)
        v = near[o, :, :LANES].astype(F32) + near[o, :, LANES:].astype(F32)
        w_re = jnp.concatenate([w[:, :m], w[:, 2 * m : 2 * m + r]], 1)
        w_im = jnp.concatenate([w[:, m : 2 * m], w[:, 2 * m + r :]], 1)
        v_re = jnp.concatenate([v[:m], v[2 * m : 2 * m + r]], 0)
        v_im = jnp.concatenate([v[m : 2 * m], v[2 * m + r :]], 0)
        a_re = jnp.dot(w_re, v_re, precision=high) - jnp.dot(w_im, v_im, precision=high)
        a_im = jnp.dot(w_re, v_im, precision=high) + jnp.dot(w_im, v_re, precision=high)
        re = lax.dot_general(a_re, x, dims, precision=high)
        im = lax.dot_general(a_im, x, dims, precision=high)
        total = total + INV_FOUR_PI * jnp.concatenate(
            [re[:, :half] - im[:, half:], re[:, half:] + im[:, :half]], 1
        )
    targets = lax.dynamic_slice_in_dim(tgt_geom, lax.axis_index("col") * rows_here, rows_here, 1)
    width = math.gcd(everything.shape[0], 512)

    def far(index, accum):
        places = lax.dynamic_slice_in_dim(sources, index * width, width, 1)
        x = lax.dynamic_slice_in_dim(everything, index * width, width, 0)[:, EXC_AT : EXC_AT + exc]
        kern_re, kern_im = far_kernel_values(
            wavenumber[0], [places[i][:, None] for i in range(4)], targets
        )
        re = lax.dot_general(kern_re.astype(BF16), x, dims, preferred_element_type=F32)
        im = lax.dot_general(kern_im.astype(BF16), x, dims, preferred_element_type=F32)
        return accum + jnp.concatenate([re[:, :half] - im[:, half:], re[:, half:] + im[:, :half]], 1)

    return lax.fori_loop(0, everything.shape[0] // width, far, total)


def on_device(*arguments):
    count = lax.axis_size("row") * lax.axis_size("col")
    short = lax.axis_size("col") == 2 and lax.axis_size("row") <= 16 and count & (count - 1) == 0
    return (exchanged if short and count >= 8 else gathered)(*arguments)


def solution(mesh):
    return jax.shard_map(
        on_device,
        mesh=mesh,
        in_specs=(
            P("groups"),
            P(None, ("groups", "row")),
            P(None, ("groups", "row", "col")),
            P(None, ("groups", "row", "col")),
            P(None, ("groups", "row")),
            P(None, ("groups", "row")),
            P(None, None, ("groups", "row")),
            P(None, None, ("groups", "row", "col")),
            P(("groups", "row"), None),
        ),
        out_specs=P(("groups", "row", "col"), None),
        check_vma=False,
    )
```

```python
import functools
import math

import jax
import jax.numpy as jnp
from jax import lax
from jax.experimental import pallas as pl
from jax.experimental.pallas import tpu as pltpu
from jax.sharding import PartitionSpec as P

QSTEP = 64
QN = 192
LANES = 128
PARTS = 3
SOFT = 0.05
INV_FOUR_PI = 1.0 / (4.0 * math.pi)
INV_TURN = 1.0 / (2.0 * math.pi)
TURN_HIGH = 6.28125
TURN_LOW = 2.0 * math.pi - TURN_HIGH
SIN_HALF = (3.14159264, -5.16771009, 2.55007766, -0.59829216, 0.07765941)
COS_HALF = (1.0, -4.93480214, 4.05870916, -1.33521206, 0.23493756, -0.02439672)
COS_FULL = (
    0.99999999, -19.73920453, 64.93911898, -85.45016555, 60.16783171, -25.96831321, 6.52961029
)
BF16 = jnp.bfloat16
F32 = jnp.float32
NN = (((1,), (0,)), ((), ()))
NT = (((1,), (1,)), ((), ()))
EXC_AT = 2 * QN
NODE_WIDTH = LANES
SMALL = pltpu.CompilerParams(vmem_limit_bytes=24 * 2**20)


def dot(left, right, dims=NN):
    return lax.dot_general(left, right, dims, preferred_element_type=F32)


def polynomial(z, coefficients):
    total = coefficients[-1]
    for c in coefficients[-2::-1]:
        total = total * z + c
    return total


def sincos_turns(f):
    z = f * f
    s = f * polynomial(z, SIN_HALF)
    c = polynomial(z, COS_HALF)
    twice = s + s
    return twice * c, 1.0 - twice * s


def three_parts(x):
    first = x.astype(BF16)
    rest = x - first.astype(F32)
    second = rest.astype(BF16)
    third = (rest - second.astype(F32)).astype(BF16)
    return first, second, third


def two_parts(x):
    first = x.astype(BF16)
    return first, (x - first.astype(F32)).astype(BF16)


def exchange_steps(count):
    bits = [1 << b for b in range(count.bit_length() - 2, 0, -1)]
    swapped = bits[:-2] + bits[-2:][::-1] if len(bits) >= 2 else bits
    return [b | 1 for b in bits], [b | 1 for b in swapped]


def relative_places(steps):
    places = [0]
    for step in steps:
        places = places + [p ^ step for p in places]
    return places


def iota(shape, axis):
    return lax.broadcasted_iota(jnp.int32, shape, axis)


def geom_lane(cpd):
    return 3 * PARTS * (QN // cpd)


def place_matrices(cpd):
    groups = QN // cpd
    shape = (LANES, 2 * 16)
    begin, row = iota(shape, 0), iota(shape, 1)
    node = jnp.logical_and(begin >= row * groups, begin < (row + 1) * groups)
    node = jnp.logical_and(node, row < 3 * PARTS)
    source = jnp.logical_and(begin - geom_lane(cpd) == row - 16, row >= 16)
    row_of = jnp.where(jnp.logical_or(node, source), 1.0, 0.0).astype(BF16)
    shape = (LANES, QN)
    lane, group = iota(shape, 0), lax.div(iota(shape, 1), cpd)
    wanted = jnp.where(lane < geom_lane(cpd), lax.rem(lane, groups), 0)
    kept = jnp.where(group == wanted, 1.0, 0.0)
    shape = (cpd, QN)
    column_of = jnp.where(lax.rem(iota(shape, 1), cpd) == iota(shape, 0), 1.0, 0.0).astype(BF16)
    return row_of, kept, column_of


def pack_kernel(
    units, order_hbm, geom_hbm, excite_hbm, nodes_hbm, weights_hbm, tnodes_hbm, tweights_hbm,
    out_ref, target_ref, tests_ref, found_ref,
    order_ref, geom_ref, excite_ref, nodes_ref, weights_ref, tnodes_ref, arrived,
):
    col = lax.axis_index("col")
    rows = tests_ref.shape[2]
    at = pl.ds(pl.multiple_of(col * rows, LANES), rows)
    moves = [
        (order_hbm, order_ref),
        (nodes_hbm, nodes_ref),
        (geom_hbm, geom_ref),
        (tnodes_hbm, tnodes_ref),
        (excite_hbm, excite_ref),
        (weights_hbm, weights_ref),
        (tweights_hbm.at[:, :, at], tests_ref),
    ]
    copies = [pltpu.make_async_copy(*move, arrived.at[i]) for i, move in enumerate(moves)]
    for copy in copies:
        copy.start()
    cpd, exc = excite_ref.shape
    row_of, kept, column_of = place_matrices(cpd)
    for copy in copies[:-1]:
        copy.wait()
    main = LANES
    rest = QN - main
    re, im = weights_ref[0], weights_ref[1]
    out_ref[:, 0:main] = re[:, :main]
    out_ref[:, main : 2 * main] = im[:, :main]
    out_ref[:, 2 * main : 2 * main + 2 * rest] = jnp.concatenate([re[:, main:], im[:, main:]], 1)
    out_ref[:, EXC_AT : EXC_AT + exc] = excite_ref[...]
    nodes = [p.astype(F32) for p in three_parts(nodes_ref[...])]
    geom = jnp.concatenate([p.astype(F32) for p in three_parts(geom_ref[...])], 0)
    values = jnp.concatenate(
        nodes
        + [
            jnp.zeros((16 - 3 * PARTS, QN), F32),
            jnp.concatenate([geom, jnp.zeros((geom.shape[0], QN - cpd), F32)], 1),
            jnp.zeros((16 - geom.shape[0], QN), F32),
        ],
        0,
    ).astype(BF16)
    spread = (dot(row_of, values) * kept).astype(BF16)
    out_ref[:, EXC_AT + exc :] = dot(column_of, spread, NT).astype(BF16)
    nodes = tnodes_ref[:, :QN]
    for b in range(1, tnodes_ref.shape[1] // QN):
        nodes = jnp.where(col == b, tnodes_ref[:, b * QN : (b + 1) * QN], nodes)
    end = nodes[:, LANES:]
    start = nodes[:, :QSTEP]
    target_ref[0, 0:3] = nodes[:, :LANES]
    target_ref[1, 0:3] = jnp.concatenate([end, end], 1)
    target_ref[2, 0:3] = jnp.concatenate([start, start], 1)
    for slot, order in enumerate(slot_orders(order_ref, units)):
        found_ref[slot] = order
    copies[-1].wait()


def store_tests(tests_ref, ut_ref):
    re, im = tests_ref[0], tests_ref[1]
    main = LANES
    ut_ref[0:main, :] = jnp.concatenate([re[:main], im[:main]], 1)
    ut_ref[main : 2 * main, :] = jnp.concatenate([-im[:main], re[:main]], 1)
    ut_ref[2 * main : 2 * main + QSTEP, :] = jnp.concatenate([re[main:], im[main:]], 1)
    ut_ref[2 * main + QSTEP :, :] = jnp.concatenate([-im[main:], re[main:]], 1)


def node_columns(data_ref, exc):
    block = data_ref[:, EXC_AT + exc :].astype(F32)
    step = geom_lane(16) // PARTS
    return (block[:, :step] + block[:, step : 2 * step]) + block[:, 2 * step : 3 * step]


def two_part_dot(high, low, right):
    count = high.shape[0]
    both = dot(jnp.concatenate([high, low], 0), right)
    return both[:count] + both[count:]


def near_slot(order, columns, slot, target_ref, ut_ref, turns, out_ref):
    lane = lax.broadcasted_iota(jnp.int32, (1, LANES), 1)
    quarter = jnp.where(lane < QSTEP, 0.0, 0.25)
    main = LANES

    def located(count):
        return [
            jnp.concatenate(
                [
                    jnp.broadcast_to(columns[16 * slot : 16 * slot + 16, lane : lane + 1], (16, LANES))
                    for lane in range(axis * (QN // 16), axis * (QN // 16) + count // 16)
                ],
                0,
            )
            for axis in range(3)
        ]

    def distance2(source, tile):
        total = SOFT * SOFT
        for axis in range(3):
            d = source[axis] - target_ref[tile, axis : axis + 1, :]
            total = total + d * d
        return total

    def both(source):
        d2 = distance2(source, 0)
        inv = lax.rsqrt(d2)
        t = (d2 * inv) * turns
        sin, cos = sincos_turns(t - jnp.round(t))
        return two_parts(inv * cos), two_parts(inv * sin)

    def split_lanes(source, tile):
        d2 = distance2(source, tile)
        inv = lax.rsqrt(d2)
        t = (d2 * inv) * turns
        f = (t - jnp.round(t - quarter)) - quarter
        return two_parts(inv * polynomial(f * f, COS_FULL))

    def put(at, value):
        high, low = two_parts(value)
        count = value.shape[0]
        out_ref[at : at + count, :LANES] = high
        out_ref[at : at + count, LANES:] = low

    def clear(begin, end):
        out_ref[begin:end, :] = jnp.zeros((end - begin, 2 * LANES), BF16)

    @pl.when(order == 3)
    def _():
        source = located(QN)
        (re_high, re_low), (im_high, im_low) = both(source)
        rest_high, rest_low = split_lanes(source, 1)
        high = jnp.concatenate([re_high, im_high, rest_high], 1)
        low = jnp.concatenate([re_low, im_low, rest_low], 1)
        v = two_part_dot(high, low, ut_ref[...])
        put(0, v[:main, :LANES])
        put(main, v[:main, LANES:])
        put(2 * main, v[main:, :LANES])
        put(2 * main + QSTEP, v[main:, LANES:])

    @pl.when(order == 2)
    def _():
        (re_high, re_low), (im_high, im_low) = both(located(main))
        high = jnp.concatenate([re_high, im_high], 1)
        low = jnp.concatenate([re_low, im_low], 1)
        v = two_part_dot(high, low, ut_ref[: 2 * main])
        put(0, v[:, :LANES])
        put(main, v[:, LANES:])
        clear(2 * main, 3 * main)

    @pl.when(order == 1)
    def _():
        high, low = split_lanes(located(QSTEP), 2)
        weights = jnp.concatenate([ut_ref[0:QSTEP], ut_ref[main : main + QSTEP]], 0)
        v = two_part_dot(high, low, weights)
        put(0, v[:, :LANES])
        clear(QSTEP, main)
        put(main, v[:, LANES:])
        clear(main + QSTEP, 3 * main)

    @pl.when(order == 0)
    def _():
        clear(0, 3 * main)


def slot_orders(order_ref, units):
    row, col = lax.axis_index("row"), lax.axis_index("col")
    nrow = lax.axis_size("row")
    band = order_ref.shape[1]
    reach = (band - 1) // 2
    if units is None:
        offsets = [jnp.where(jnp.logical_and(row + o >= reach, row + o - reach < nrow), o, -1) for o in range(band)]
    else:
        place, parity = row * lax.axis_size("col") + col, 0
        for _ in range((nrow * lax.axis_size("col")).bit_length() - 1):
            parity = parity + lax.rem(place, 2)
            place = lax.div(place, 2)
        parity = lax.rem(parity, 2)
        offsets = [
            (row ^ (a if a == b else jnp.where(parity == 0, a, b))) - row + reach for a, b in zip(*units)
        ]
    return [
        jnp.where(
            jnp.logical_and(o >= 0, o < band), order_ref[col, jnp.clip(o, 0, band - 1)], 0
        )
        for o in offsets
    ]


def far_kernel_values(wave, source, tgeom):
    dx = tgeom[0:1] - source[0]
    dy = tgeom[1:2] - source[1]
    dz = tgeom[2:3] - source[2]
    d2 = dx * dx + dy * dy + dz * dz + SOFT * SOFT
    inv = lax.rsqrt(d2)
    radius = d2 * inv
    cosine = (tgeom[3:4] * dx + tgeom[4:5] * dy + tgeom[5:6] * dz) * inv
    scale = source[3] * (INV_FOUR_PI * inv)
    phase = wave * radius
    t = phase * INV_TURN
    n = jnp.round(t)
    sin, cos = sincos_turns(((phase - n * TURN_HIGH) - n * TURN_LOW) * INV_TURN)
    green_re = scale * cos
    green_im = scale * sin
    factor_re = 1.0 - cosine
    factor_im = cosine * (inv * (-1.0 / wave))
    kern_re = (green_re * factor_re - green_im * factor_im).astype(BF16)
    kern_im = (green_re * factor_im + green_im * factor_re).astype(BF16)
    return kern_re, kern_im


def far_rows(data, exc, wave, tgeom):
    at = geom_lane(16)
    geom = data[:, EXC_AT + exc :].astype(F32)
    parts = [geom[:, at + 4 * i : at + 4 * i + 4] for i in range(PARTS)]
    total = (parts[0] + parts[1]) + parts[2]
    return far_kernel_values(wave, [total[:, i : i + 1] for i in range(4)], tgeom)


def own_targets(tgeom_ref, rows):
    at = pl.multiple_of(lax.axis_index("col") * rows, LANES)
    return tgeom_ref[:, pl.ds(at, rows)]


def near_kernel(
    exc, first, wave_ref, found_ref, data_ref, own_ref, target_ref, ut_ref, tgeom_ref,
    v_ref, kern_re_ref, kern_im_ref, *copy_ref,
):
    if copy_ref:
        copy_ref[0][...] = own_ref[...]
    wave = wave_ref[0]
    tgeom = own_targets(tgeom_ref, kern_re_ref.shape[1])
    data = data_ref[...]
    if kern_re_ref.shape[0] > data.shape[0]:
        data = jnp.concatenate([own_ref[...], data], 0)
    kern_re_ref[...], kern_im_ref[...] = far_rows(data, exc, wave, tgeom)
    slots = v_ref.shape[0]
    skipped = data_ref.shape[0] // 16 - slots
    columns = node_columns(data_ref, exc)
    for slot in range(slots):
        near_slot(
            found_ref[first + slot], columns, skipped + slot, target_ref, ut_ref, wave * INV_TURN, v_ref.at[slot]
        )


def first_near_kernel(
    exc, first, wave_ref, found_ref, data_ref, own_ref, target_ref, tests_ref, tgeom_ref, *refs
):
    *refs, ut_ref = refs
    store_tests(tests_ref, ut_ref)
    near_kernel(exc, first, wave_ref, found_ref, data_ref, own_ref, target_ref, ut_ref, tgeom_ref, *refs)


def weight_rows(data):
    sign = jnp.where(iota((1, LANES), 1) < QSTEP, 1.0, -1.0).astype(BF16)
    w = [data[:, i * LANES : (i + 1) * LANES] for i in range(3)]
    swapped = jnp.concatenate([w[2][:, QSTEP:], w[2][:, :QSTEP]], 1)
    return jnp.concatenate([w[0], -w[1], w[2] * sign], 1), jnp.concatenate([w[1], w[0], swapped], 1)


def near_rows(left, v):
    product = dot(left, v)
    return (product[:, :LANES] + product[:, LANES:]) * INV_FOUR_PI


def known_kernel(own_ref, other_ref, *refs):
    *v_refs, out_ref = refs
    cpd = 16
    own_re, own_im = weight_rows(own_ref[: other_ref.shape[0]])
    other_re, other_im = weight_rows(other_ref[...])
    for k, v in enumerate([ref.at[i] for ref in v_refs for i in range(ref.shape[0])]):
        here = slice(k * cpd, (k + 1) * cpd)
        left = jnp.concatenate([own_re[here], other_re[here], own_im[here], other_im[here]], 0)
        out_ref[k] = near_rows(left, v[...])


def last_kernel(
    exc, partner, wave_ref, own_early, own_late, other_first, other_early, other_late, tgeom_ref,
    known_early, known_late, early_re_ref, early_im_ref, *refs
):
    own = jnp.concatenate([own_early[...], own_late[...]], 0)
    other = jnp.concatenate([other_first[...], other_early[...], other_late[...]], 0)
    out_ref, zre, zim = refs[-3:]
    *made, early_v, late_v, late_re, late_im = refs[:-3]
    v_refs = [*made[::3], early_v, late_v]
    kern_re_refs, kern_im_refs = [*made[1::3], late_re], [*made[2::3], late_im]
    rows = out_ref.shape[0]
    cpd = 16
    main = LANES
    slots = len(partner)
    quarter = slots // 4
    late_kern = far_rows(other_late, exc, wave_ref[0], own_targets(tgeom_ref, rows))
    own_re, own_im = weight_rows(own)
    other_re, other_im = weight_rows(other)
    slot = 0
    for v_ref in v_refs:
        for i in range(v_ref.shape[0]):
            here = slice(slot * cpd, (slot + 1) * cpd)
            there = slice(partner[slot] * cpd, (partner[slot] + 1) * cpd)
            if slot // quarter in (0, 2):
                a = (known_late if slot // quarter else known_early)[slot % quarter]
            else:
                left = jnp.concatenate([own_re[here], other_re[there], own_im[here], other_im[there]], 0)
                a = near_rows(left, v_ref[i])
            there = slice((slots + partner[slot]) * cpd, (slots + partner[slot] + 1) * cpd)
            zre[here] = a[0:cpd]
            zre[there] = a[cpd : 2 * cpd]
            zim[here] = a[2 * cpd : 3 * cpd]
            zim[there] = a[3 * cpd :]
            slot += 1

    first = other_first.shape[0]
    kern_re, kern_im = [
        jnp.concatenate(
            [*[ref[...] for ref in refs[:-2]], refs[-2][first:], refs[-1][...], refs[-2][:first], early[...], x], 0
        ).astype(F32)
        for refs, early, x in zip((kern_re_refs, kern_im_refs), (early_re_ref, early_im_ref), late_kern)
    ]
    excite = jnp.concatenate(
        [own[:, EXC_AT : EXC_AT + exc], other[:, EXC_AT : EXC_AT + exc]], 0
    ).T
    re = two_parts(kern_re + zre[...])
    im = two_parts(kern_im + zim[...])
    product = dot(excite, jnp.concatenate([*re, *im], 1))
    by_re = product[:, :rows] + product[:, rows : 2 * rows]
    by_im = product[:, 2 * rows : 3 * rows] + product[:, 3 * rows :]
    h = exc // 2
    result = jnp.concatenate([by_re[:h] - by_im[h:], by_re[h:] + by_im[:h]], 0)
    out_ref[...] = result.T


def in_vmem(x):
    return pltpu.with_memory_space_constraint(x, pltpu.VMEM)


def in_smem(x):
    return pltpu.with_memory_space_constraint(x, pltpu.SMEM)


def in_hbm(x):
    return pltpu.with_memory_space_constraint(x, pltpu.HBM)


SMEM_SPEC = pl.BlockSpec(memory_space=pltpu.SMEM)
VMEM_SPEC = pl.BlockSpec(memory_space=pltpu.VMEM)


def packed(units, slots, src_geom, excite, src_nodes, src_weights, tgt_nodes, tgt_weights, near_order):
    excite = excite.T
    src_weights = src_weights.transpose(0, 2, 1)
    cpd, exc = excite.shape
    rows_here = tgt_weights.shape[2] // lax.axis_size("col")
    inputs = (near_order, src_geom, excite, src_nodes, src_weights, tgt_nodes)
    return pl.pallas_call(
        functools.partial(pack_kernel, units),
        out_shape=[
            pltpu.VMEM((cpd, EXC_AT + exc + NODE_WIDTH), BF16),
            pltpu.VMEM((3, 8, LANES), F32),
            pltpu.VMEM((2, QN, rows_here), BF16),
            pltpu.SMEM((slots,), jnp.int32),
        ],
        in_specs=[pl.BlockSpec(memory_space=pl.ANY)] * 7,
        out_specs=[VMEM_SPEC] * 3 + [SMEM_SPEC],
        scratch_shapes=[pltpu.SMEM(near_order.shape, jnp.int32)]
        + [pltpu.VMEM(x.shape, x.dtype) for x in inputs[1:]]
        + [pltpu.SemaphoreType.DMA((7,))],
        compiler_params=SMALL,
    )(*[in_hbm(x) for x in inputs], in_hbm(tgt_weights))


def near_blocks(exc, first, slots, wavenumber, found, fresh, own, target, ut, tgt_geom, hand_on, both=False):
    rows_here = tgt_geom.shape[1] // lax.axis_size("col")
    kern = pltpu.VMEM((fresh.shape[0] + both * own.shape[0], rows_here), BF16)
    cost = pl.CostEstimate(flops=1, bytes_accessed=1, transcendentals=0)
    outs = [pltpu.VMEM((slots, 2 * QN, 2 * LANES), BF16), kern, kern] + [pltpu.VMEM(own.shape, BF16)] * hand_on
    if first == 0:
        outs.append(pltpu.VMEM((2 * QN, 2 * LANES), BF16))
    return pl.pallas_call(
        functools.partial(near_kernel if first else first_near_kernel, exc, first),
        out_shape=outs,
        in_specs=[SMEM_SPEC] * 2 + [VMEM_SPEC] * 5,
        out_specs=[VMEM_SPEC] * len(outs),
        compiler_params=SMALL,
        cost_estimate=cost,
    )(wavenumber, in_smem(found), in_vmem(fresh), in_vmem(own), in_vmem(target), in_vmem(ut), in_vmem(tgt_geom))


def exchanged(
    wavenumber, tgt_geom, src_geom, excite, tgt_nodes, src_nodes, tgt_weights, src_weights, near_order
):
    cpd = src_geom.shape[1]
    exc = excite.shape[0]
    cores = lax.axis_size("col")
    count = cores * lax.axis_size("row")
    rows_here = tgt_geom.shape[1] // cores
    even, odd = exchange_steps(count)
    units = [[p >> 1 for p in relative_places(s)] for s in (even, odd)]
    own, target, ut, found = packed(
        units, len(units[0]), src_geom, excite, src_nodes, src_weights, tgt_nodes, tgt_weights, near_order
    )

    def moved(value, a, b):
        pairs = [(i, i ^ (b if bin(i).count("1") % 2 else a)) for i in range(count)]
        return lax.ppermute(value, ("row", "col"), pairs)

    fresh = own
    near = []
    done = 0
    steps = list(zip(even, odd))
    for step, (a, b) in enumerate(steps):
        arriving = moved(own, a, b)
        slots = fresh.shape[0] // cpd
        last = step == len(steps) - 1
        made = near_blocks(
            exc, done, slots, wavenumber, found, fresh, other_first if last else own, target, ut, tgt_geom,
            not last, last,
        )
        near.extend(made[:3])
        if not done:
            ut = made[4]
        if step == len(steps) - 2:
            other_first = moved(own, 1, 1)
        done += slots
        fresh = arriving
        if not last:
            own = jnp.concatenate([made[3], arriving], 0)
        if step == len(steps) - 2:
            own, other_first = lax.optimization_barrier((own, other_first))
    half = own.shape[0] // 2
    other_early = moved(own[half:], 1, 1)
    quarter = half // cpd
    early = near_blocks(
        exc, done, quarter, wavenumber, found, other_early, other_early, target, ut, tgt_geom, False
    )

    def known_rows(mine, others, *v):
        return pl.pallas_call(
            known_kernel,
            out_shape=pltpu.VMEM((quarter, 4 * cpd, rows_here), F32),
            in_specs=[VMEM_SPEC] * (2 + len(v)),
            out_specs=VMEM_SPEC,
            compiler_params=SMALL,
            cost_estimate=pl.CostEstimate(flops=1, bytes_accessed=1, transcendentals=0),
        )(*[in_vmem(x) for x in (mine, others, *v)])

    known_early = known_rows(own, other_first, *near[: 3 * (len(steps) - 1) : 3])
    fresh, early, made, known_early = lax.optimization_barrier((fresh, early, made, known_early))
    other_late = moved(fresh, 1, 1)
    late = near_blocks(
        exc, done + quarter, quarter, wavenumber, found, fresh, fresh, target, ut, tgt_geom, False
    )
    near.append(early[0])
    near.extend(late)
    known_late = known_rows(fresh, other_early, early[0])
    partner = [units[1].index(u) for u in units[0]]
    return pl.pallas_call(
        functools.partial(last_kernel, exc, partner),
        out_shape=jax.ShapeDtypeStruct((rows_here, exc), F32),
        in_specs=[SMEM_SPEC] + [VMEM_SPEC] * (10 + len(near)),
        out_specs=VMEM_SPEC,
        scratch_shapes=[pltpu.VMEM((count * cpd, rows_here), F32)] * 2,
        compiler_params=SMALL,
    )(
        wavenumber,
        *[in_vmem(x) for x in (own, fresh, other_first, other_early, other_late, tgt_geom, known_early, known_late, *early[1:], *near)],
    )


def gathered(
    wavenumber, tgt_geom, src_geom, excite, tgt_nodes, src_nodes, tgt_weights, src_weights, near_order
):
    cpd = src_geom.shape[1]
    exc = excite.shape[0]
    half = exc // 2
    cores = lax.axis_size("col")
    nrow = lax.axis_size("row")
    row = lax.axis_index("row")
    rows_here = tgt_geom.shape[1] // cores
    band = near_order.shape[1]
    own, target, ut, found = packed(
        None, band, src_geom, excite, src_nodes, src_weights, tgt_nodes, tgt_weights, near_order
    )
    everything = lax.all_gather(own, ("row", "col"), axis=0, tiled=True)
    sources = lax.all_gather(src_geom, ("row", "col"), axis=1, tiled=True)
    blocks = [
        lax.dynamic_slice_in_dim(
            everything, jnp.clip(row + o - (band - 1) // 2, 0, nrow - 1) * cores * cpd, cores * cpd, 0
        )
        for o in range(band)
    ]
    fresh = jnp.concatenate([block[:cpd] for block in blocks], 0)
    near = near_blocks(exc, 0, band, wavenumber, found, fresh, own, target, ut, tgt_geom, False)[0]
    high = lax.Precision.HIGHEST
    total = jnp.zeros((rows_here, exc), F32)
    dims = (((0,), (0,)), ((), ()))
    m, r = LANES, QN - LANES
    for o, block in enumerate(blocks):
        w, x = block[:, :EXC_AT].astype(F32), block[:, EXC_AT : EXC_AT + exc].astype(F32)
        v = near[o, :, :LANES].astype(F32) + near[o, :, LANES:].astype(F32)
        w_re = jnp.concatenate([w[:, :m], w[:, 2 * m : 2 * m + r]], 1)
        w_im = jnp.concatenate([w[:, m : 2 * m], w[:, 2 * m + r :]], 1)
        v_re = jnp.concatenate([v[:m], v[2 * m : 2 * m + r]], 0)
        v_im = jnp.concatenate([v[m : 2 * m], v[2 * m + r :]], 0)
        a_re = jnp.dot(w_re, v_re, precision=high) - jnp.dot(w_im, v_im, precision=high)
        a_im = jnp.dot(w_re, v_im, precision=high) + jnp.dot(w_im, v_re, precision=high)
        re = lax.dot_general(a_re, x, dims, precision=high)
        im = lax.dot_general(a_im, x, dims, precision=high)
        total = total + INV_FOUR_PI * jnp.concatenate(
            [re[:, :half] - im[:, half:], re[:, half:] + im[:, :half]], 1
        )
    targets = lax.dynamic_slice_in_dim(tgt_geom, lax.axis_index("col") * rows_here, rows_here, 1)
    width = math.gcd(everything.shape[0], 512)

    def far(index, accum):
        places = lax.dynamic_slice_in_dim(sources, index * width, width, 1)
        x = lax.dynamic_slice_in_dim(everything, index * width, width, 0)[:, EXC_AT : EXC_AT + exc]
        kern_re, kern_im = far_kernel_values(
            wavenumber[0], [places[i][:, None] for i in range(4)], targets
        )
        re = lax.dot_general(kern_re.astype(BF16), x, dims, preferred_element_type=F32)
        im = lax.dot_general(kern_im.astype(BF16), x, dims, preferred_element_type=F32)
        return accum + jnp.concatenate([re[:, :half] - im[:, half:], re[:, half:] + im[:, :half]], 1)

    return lax.fori_loop(0, everything.shape[0] // width, far, total)


def on_device(*arguments):
    count = lax.axis_size("row") * lax.axis_size("col")
    short = lax.axis_size("col") == 2 and lax.axis_size("row") <= 16 and count & (count - 1) == 0
    return (exchanged if short and count >= 8 else gathered)(*arguments)


def solution(mesh):
    return jax.shard_map(
        on_device,
        mesh=mesh,
        in_specs=(
            P("groups"),
            P(None, ("groups", "row")),
            P(None, ("groups", "row", "col")),
            P(None, ("groups", "row", "col")),
            P(None, ("groups", "row")),
            P(None, ("groups", "row")),
            P(None, None, ("groups", "row")),
            P(None, None, ("groups", "row", "col")),
            P(("groups", "row"), None),
        ),
        out_specs=P(("groups", "row", "col"), None),
        check_vma=False,
    )
```
